32 devices in a mesh: seq: 8 (over y, x, core), head: 4 (over z).
Axes of the slice: x: 2, y: 2, z: 4, core: 2. Of those that a mesh axis runs over, the one named last changes fastest.
Arguments:
- query_act: bfloat16 [2048, 1536], P('seq', 'head'), may hold values from -0.59765625 to 0.59765625
- key_act: bfloat16 [2048, 1536], P('seq', 'head'), may hold values from -0.59765625 to 0.59765625
- value_act: bfloat16 [2048, 1536], P('seq', 'head'), may hold values from -0.59765625 to 0.59765625
- grad_output: bfloat16 [2048, 1536], P('seq', 'head'), may hold values from -1.0546875 to 1.0546875
- log_decay: float32 [2048, 12], P('seq', 'head'), may hold values from -1 to 0
- w_query: bfloat16 [6144, 1536], P(None, 'head'), may hold values from -0.109375 to 0.109375
- w_key: bfloat16 [6144, 1536], P(None, 'head'), may hold values from -0.109375 to 0.109375
Outputs:
- grad_input: bfloat16 [6144, 2048], P('head', 'seq')
The draws below stay inside these ranges and needn't reach their ends.
All inputs are finite; a program needn't handle non-finite values.
Results may differ from the reference program's by a relative error of at most 0.015.
Values may be sent and summed in bfloat16 or wider, within the bound.
No kernel may reach another device: no remote copies, remote signals or barrier semaphores. Data moves between devices by JAX's collectives and lax.ppermute only.
A program may use at most 128 MiB of HBM per device.

```python
import math
import jax
import jax.numpy as jnp
from jax import lax

D = 6144
HD = 128
HEADS_DEV = 3
TOK_DEV = 256
ATTENTION_HEADS = 12
SEQUENCE_TOKENS = 2048
N_SEQ = 8
N_HEAD = 4


def draw_log_decay(key, part):
    random_split_keys = jax.random.split(jax.random.fold_in(key, 7), 5)
    fast_share = 0.5
    fast_heads = jax.random.bernoulli(random_split_keys[0], fast_share, (ATTENTION_HEADS,))
    fast_rate = jnp.exp(jax.random.uniform(random_split_keys[1], (ATTENTION_HEADS,), jnp.float32, math.log(1.0 / 50.0), math.log(1.0 / 30.0)))
    slow_rate = jnp.full((ATTENTION_HEADS,), 0.5 / SEQUENCE_TOKENS, jnp.float32)
    baseline_decay_rate = jnp.where(fast_heads, fast_rate, slow_rate)
    random_noise = jnp.exp(jax.random.uniform(random_split_keys[2], (SEQUENCE_TOKENS, ATTENTION_HEADS), jnp.float32, -math.log(2.0), math.log(2.0)))
    spike_row_count = jax.random.randint(random_split_keys[3], (3,), 0, SEQUENCE_TOKENS)
    spike_lengths = -jnp.log(1.0 - jax.random.uniform(random_split_keys[4], (3, ATTENTION_HEADS), jnp.float32, 0.2, 0.4))
    decay_spikes = jnp.zeros((SEQUENCE_TOKENS, ATTENTION_HEADS), jnp.float32).at[spike_row_count].add(spike_lengths)
    return (-(baseline_decay_rate[None, :] * random_noise) - decay_spikes).astype(jnp.float32)


def block_levels(rng, shape, cuts, smallest, largest):
    loudness = 1.0
    for dim, blocks in cuts:
        steps = jax.random.uniform(jax.random.fold_in(jax.random.fold_in(rng, 6), dim), (blocks,), jnp.float32, smallest / len(cuts), largest / len(cuts))
        loudness = loudness * jnp.repeat(jnp.exp(steps), shape[dim] // blocks).reshape((-1,) + (1,) * (len(shape) - 1 - dim))
    return loudness


def noise(key, shape, width, most, cuts=(), kind=jnp.bfloat16):
    array = width * jax.random.normal(key, shape, jnp.float32)
    if cuts:
        array = array * block_levels(key, shape, cuts, -0.22, 0.18)
    return jnp.clip(array, -most, most).astype(kind)


def setup_inputs(seed: int = 0) -> dict:
    arg_keys = jax.random.split(jax.random.key(seed), 8)
    query_act = noise(arg_keys[0], (SEQUENCE_TOKENS, ATTENTION_HEADS * HD), 0.1, 0.59765625, ((0, 8), (1, 4)))
    key_act = noise(arg_keys[1], (SEQUENCE_TOKENS, ATTENTION_HEADS * HD), 0.1, 0.59765625, ((0, 8), (1, 4)))
    value_act = noise(arg_keys[2], (SEQUENCE_TOKENS, ATTENTION_HEADS * HD), 0.1, 0.59765625, ((0, 8), (1, 4)))
    grad_output = noise(arg_keys[3], (SEQUENCE_TOKENS, ATTENTION_HEADS * HD), (8.0 / SEQUENCE_TOKENS ** 0.5), 1.0546875, ((0, 8), (1, 4)))
    log_decay = draw_log_decay(jax.random.fold_in(arg_keys[7], 71), 0)
    w_query = noise(arg_keys[5], (D, ATTENTION_HEADS * HD), (2 * ATTENTION_HEADS * HD) ** -0.5, 0.109375, ((1, 4),))
    w_key = noise(arg_keys[6], (D, ATTENTION_HEADS * HD), (2 * ATTENTION_HEADS * HD) ** -0.5, 0.109375, ((1, 4),))
    return dict(query_act=query_act, key_act=key_act, value_act=value_act, grad_output=grad_output, log_decay=log_decay, w_query=w_query, w_key=w_key)


def to_bf16(values):
    return lax.optimization_barrier(values.astype(jnp.bfloat16))


def block_grads(queries, keys_blk, values_blk, grads_blk, cumlog, state_in, grad_in):
    f32 = jnp.float32
    span = cumlog.shape[0]
    last_log = cumlog[-1]
    log_gap = cumlog[:, None, :] - cumlog[None, :, :]
    positions = jnp.arange(span)
    causal_mask = positions[:, None] >= positions[None, :]
    decay_mat = jnp.where(causal_mask[:, :, None], jnp.exp(jnp.minimum(log_gap, 0.0)), 0.0)
    dot_scores = jnp.einsum("the,she->tsh", grads_blk.astype(f32), values_blk.astype(f32))
    weighted = to_bf16(dot_scores * decay_mat).astype(f32)
    dq_local = jnp.einsum("tsh,shd->thd", weighted, keys_blk.astype(f32))
    dk_local = jnp.einsum("tsh,thd->shd", weighted, queries.astype(f32))
    state_bf = to_bf16(state_in).astype(f32)
    grad_bf = to_bf16(grad_in).astype(f32)
    dq_carry = jnp.einsum("the,hde->thd", grads_blk.astype(f32), state_bf) * jnp.exp(cumlog)[:, :, None]
    dk_carry = jnp.einsum("the,hde->thd", values_blk.astype(f32), grad_bf) * jnp.exp(last_log[None, :] - cumlog)[:, :, None]
    return to_bf16(dq_local + dq_carry), to_bf16(dk_local + dk_carry)


def reference(query_act, key_act, value_act, grad_output, log_decay, w_query, w_key):
    f32 = jnp.float32
    shape_four = (N_SEQ, TOK_DEV, ATTENTION_HEADS, HD)
    queries = query_act.reshape(shape_four)
    keys_all = key_act.reshape(shape_four)
    values_all = value_act.reshape(shape_four)
    grads_all = grad_output.reshape(shape_four)
    cumlog = jnp.cumsum(log_decay.reshape(N_SEQ, TOK_DEV, ATTENTION_HEADS).astype(f32), axis=1)
    last_log = cumlog[:, -1]
    decay_total = jnp.exp(last_log)
    key_weighted = to_bf16(keys_all.astype(f32) * jnp.exp(last_log[:, None, :] - cumlog)[..., None]).astype(f32)
    query_weighted = to_bf16(queries.astype(f32) * jnp.exp(cumlog)[..., None]).astype(f32)
    local_states = jnp.einsum("nthd,nthe->nhde", key_weighted, values_all.astype(f32))
    local_grads = jnp.einsum("nthd,nthe->nhde", query_weighted, grads_all.astype(f32))

    def forward_step(running, inputs):
        total, state = inputs
        return total[:, None, None] * running + state, running

    start_state = jnp.zeros((ATTENTION_HEADS, HD, HD), f32)
    _, states_in = lax.scan(forward_step, start_state, (decay_total, local_states))
    _, grads_in = lax.scan(forward_step, start_state, (decay_total, local_grads), reverse=True)
    grad_query, grad_key = lax.map(lambda packed: block_grads(*packed),
                                   (queries, keys_all, values_all, grads_all, cumlog, states_in, grads_in))
    dq_flat = grad_query.reshape(SEQUENCE_TOKENS, ATTENTION_HEADS * HD)
    dk_flat = grad_key.reshape(SEQUENCE_TOKENS, ATTENTION_HEADS * HD)
    group_width = HEADS_DEV * HD
    dims = (((1,), (1,)), ((), ()))
    summed = jnp.zeros((D, SEQUENCE_TOKENS), f32)
    for group_index in range(N_HEAD):
        lower = group_index * group_width
        upper = lower + group_width
        partial_term = lax.dot_general(w_query[:, lower:upper], dq_flat[:, lower:upper], dims, preferred_element_type=f32)
        partial_term = partial_term + lax.dot_general(w_key[:, lower:upper], dk_flat[:, lower:upper], dims, preferred_element_type=f32)
        summed = summed + to_bf16(partial_term).astype(f32)
    return summed.astype(jnp.bfloat16)
```

```python
import jax
import jax.numpy as jnp
from jax import lax
from jax.sharding import PartitionSpec as P

F32 = jnp.float32
BF16 = jnp.bfloat16


def scan_blocks(state, grad, last_log):
    count, mine = lax.axis_size("seq"), lax.axis_index("seq")
    nheads, width = state.shape[0], state.shape[1]
    shape = state.shape
    rows = nheads * width
    before = jnp.zeros_like(last_log)
    after = jnp.zeros_like(last_log)
    total = last_log
    state_in = jnp.zeros(shape, F32)
    grad_in = jnp.zeros(shape, F32)
    hop = 1
    while hop < count:
        pairs = [(i, i ^ hop) for i in range(count)]
        upper = (mine // hop) % 2 == 1
        if 2 * hop < count:
            high = total.astype(BF16)
            low = (total - high.astype(F32)).astype(BF16)
            tail = jnp.zeros((16, width), BF16).at[0, :nheads].set(high).at[1, :nheads].set(low)
            sent = jnp.concatenate(
                [state.astype(BF16).reshape(rows, width), grad.astype(BF16).reshape(rows, width), tail]
            )
            got = lax.ppermute(sent, "seq", pairs)
            got_state = got[:rows].astype(F32).reshape(shape)
            got_grad = got[rows : 2 * rows].astype(F32).reshape(shape)
            tail = got[2 * rows :].astype(F32)
            got_total = tail[0, :nheads] + tail[1, :nheads]
        else:
            sent = jnp.where(upper, grad, state).astype(BF16).reshape(rows, width)
            got_state = got_grad = lax.ppermute(sent, "seq", pairs).astype(F32).reshape(shape)
            got_total = total
        state_in = jnp.where(upper, state_in + jnp.exp(before)[:, None, None] * got_state, state_in)
        grad_in = jnp.where(upper, grad_in, grad_in + jnp.exp(after)[:, None, None] * got_grad)
        mine_decay = jnp.exp(total)[:, None, None]
        other_decay = jnp.exp(got_total)[:, None, None]
        state, grad = (
            jnp.where(upper, mine_decay * got_state + state, other_decay * state + got_state),
            jnp.where(upper, got_grad + other_decay * grad, grad + mine_decay * got_grad),
        )
        before = jnp.where(upper, before + got_total, before)
        after = jnp.where(upper, after, after + got_total)
        total = total + got_total
        hop *= 2
    return state_in, grad_in


def share_order(count):
    bits = []
    hop = 2
    while hop < count:
        bits.append(hop)
        hop *= 2
    return bits, bits[::-1]


def gather_shares(piece):
    count = lax.axis_size("seq")
    even, odd = share_order(count)
    held = piece
    for hop_even, hop_odd in zip(even, odd):
        pairs = [(i, i ^ (hop_odd if i % 2 else hop_even)) for i in range(count)]
        held = jnp.concatenate([held, lax.ppermute(held, "seq", pairs)])
    return jnp.concatenate([held, lax.ppermute(held, "seq", [(i, i ^ 1) for i in range(count)])])


def share_places(count):
    even, odd = share_order(count)
    tables = []
    for first, second in ((even, odd), (odd, even)):
        def spread(order):
            out = [0]
            for hop in order:
                out = out + [d ^ hop for d in out]
            return out
        order = spread(first) + [d ^ 1 for d in spread(second)]
        place = [0] * count
        for position, delta in enumerate(order):
            place[delta] = position
        tables.append(place)
    return tables


def shards(query_act, key_act, value_act, grad_output, log_decay, w_query, w_key):
    span = query_act.shape[0]
    nheads = log_decay.shape[1]
    width = query_act.shape[1] // nheads
    nseq, nhead = lax.axis_size("seq"), lax.axis_size("head")
    my_seq, my_head = lax.axis_index("seq"), lax.axis_index("head")
    chunk = w_query.shape[0] // nhead
    share = chunk // nseq

    pieces = []
    sources = []
    for k in range(1, nhead):
        if nhead & (nhead - 1) == 0:
            pairs = [(i, i ^ k) for i in range(nhead)]
            target = source = my_head ^ k
        else:
            pairs = [(i, (i + k) % nhead) for i in range(nhead)]
            target, source = (my_head + k) % nhead, (my_head + nhead - k) % nhead
        start = target * chunk + my_seq * share
        sent = jnp.concatenate(
            [lax.dynamic_slice_in_dim(w, start, share, 0) for w in (w_query, w_key)], axis=1
        )
        pieces.append(lax.ppermute(sent, "head", pairs))
        sources.append(source)

    queries = query_act.reshape(span, nheads, width)
    keys_blk = key_act.reshape(span, nheads, width)
    values_blk = value_act.reshape(span, nheads, width)
    grads_blk = grad_output.reshape(span, nheads, width)
    cumlog = jnp.cumsum(log_decay, axis=0)
    last_log = cumlog[-1]
    key_weighted = (keys_blk * jnp.exp(last_log[None, :] - cumlog)[:, :, None]).astype(BF16)
    query_weighted = (queries * jnp.exp(cumlog)[:, :, None]).astype(BF16)
    local_state = jnp.einsum("thd,the->hde", key_weighted, values_blk, preferred_element_type=F32)
    local_grad = jnp.einsum("thd,the->hde", query_weighted, grads_blk, preferred_element_type=F32)
    state_in, grad_in = scan_blocks(local_state, local_grad, last_log)

    positions = jnp.arange(span)
    causal_mask = positions[:, None] >= positions[None, :]
    log_gap = cumlog[:, None, :] - cumlog[None, :, :]
    decay_mat = jnp.where(causal_mask[:, :, None], jnp.exp(jnp.minimum(log_gap, 0.0)), 0.0)
    dot_scores = jnp.einsum("the,she->tsh", grads_blk, values_blk, preferred_element_type=F32)
    weighted = (dot_scores * decay_mat).astype(BF16)
    dq_local = jnp.einsum("tsh,shd->thd", weighted, keys_blk, preferred_element_type=F32)
    dk_local = jnp.einsum("tsh,thd->shd", weighted, queries, preferred_element_type=F32)
    dq_carry = (
        jnp.einsum("the,hde->thd", grads_blk, state_in.astype(BF16), preferred_element_type=F32)
        * jnp.exp(cumlog)[:, :, None]
    )
    dk_carry = (
        jnp.einsum("the,hde->thd", values_blk, grad_in.astype(BF16), preferred_element_type=F32)
        * jnp.exp(last_log[None, :] - cumlog)[:, :, None]
    )
    dq_flat = (dq_local + dq_carry).astype(BF16).reshape(span, nheads * width)
    dk_flat = (dk_local + dk_carry).astype(BF16).reshape(span, nheads * width)
    both = jnp.concatenate([dq_flat, dk_flat], axis=1)

    if nhead == 4:
        p1 = lax.ppermute(both, "head", [(0, 1), (1, 0), (2, 3), (3, 2)])
        p2 = lax.ppermute(both, "head", [(1, 2), (2, 1)])
        p3 = lax.ppermute(p2, "head", [(2, 3), (1, 0)])
        p4 = lax.ppermute(p1, "head", [(1, 2), (2, 1)])
        p5 = lax.ppermute(p4, "head", [(2, 3), (1, 0)])
        inner = (my_head == 1) | (my_head == 2)
        others = [p1, jnp.where(inner, p4, p3), jnp.where(inner, p2, p5)]
    else:
        gathered = lax.all_gather(both, "head")
        others = [gathered[source] for source in sources]

    dims = (((1,), (1,)), ((), ()))
    start = my_head * chunk
    total = lax.dot_general(
        lax.dynamic_slice_in_dim(w_query, start, chunk, 0), dq_flat, dims, preferred_element_type=F32
    ) + lax.dot_general(
        lax.dynamic_slice_in_dim(w_key, start, chunk, 0), dk_flat, dims, preferred_element_type=F32
    )
    remote = 0.0
    for piece, grads in zip(pieces, others):
        remote = remote + lax.dot_general(gather_shares(piece), grads, dims, preferred_element_type=F32)
    even, odd = share_places(nseq)
    deltas = jnp.arange(nseq) ^ my_seq
    place = jnp.where(my_seq % 2 == 1, jnp.array(odd)[deltas], jnp.array(even)[deltas])
    remote = remote.reshape(nseq, share, span)[place].reshape(chunk, span)
    return (total + remote).astype(BF16)


def solution(mesh):
    placed = (
        P("seq", "head"),
        P("seq", "head"),
        P("seq", "head"),
        P("seq", "head"),
        P("seq", "head"),
        P(None, "head"),
        P(None, "head"),
    )
    return jax.shard_map(
        shards, mesh=mesh, in_specs=placed, out_specs=P("head", "seq"), check_vma=False
    )
```

```python
import functools

import jax
import jax.numpy as jnp
from jax import lax
from jax.experimental import pallas as pl
from jax.experimental.pallas import tpu as pltpu
from jax.sharding import PartitionSpec as P

F32 = jnp.float32
BF16 = jnp.bfloat16
VMEM_BYTES = 40 * 1024 * 1024


def contract(a, b, left, right):
    return lax.dot_general(a, b, (((left,), (right,)), ((), ())), preferred_element_type=F32)


def call(kernel, out_shape, flops, nbytes, *args, aliases=None, **spec):
    return pl.pallas_call(
        kernel,
        out_shape=out_shape,
        cost_estimate=pl.CostEstimate(flops=flops, bytes_accessed=nbytes, transcendentals=0),
        compiler_params=pltpu.CompilerParams(vmem_limit_bytes=VMEM_BYTES),
        input_output_aliases=aliases or {},
        **spec,
    )(*args)


def whole(shape):
    return pl.BlockSpec(shape, lambda *_: (0,) * len(shape))


def thirds(x):
    high = x.astype(BF16)
    rest = x - high.astype(F32)
    middle = rest.astype(BF16)
    return high, middle, (rest - middle.astype(F32)).astype(BF16)


def triangle(span):
    rows = lax.broadcasted_iota(jnp.int32, (span, span), 0)
    cols = lax.broadcasted_iota(jnp.int32, (span, span), 1)
    return rows >= cols


def upper_half(hop):
    return ((lax.axis_index("seq") // hop) % 2).astype(F32)


def states_kernel(nheads, width, decay_ref, q_ref, k_ref, v_ref, g_ref, sent_ref, held_ref, logs_ref):
    span = q_ref.shape[0]
    tri = triangle(span).astype(F32).astype(BF16)
    cum = sum(contract(tri, part, 1, 0) for part in thirds(decay_ref[...]))
    rows = nheads * width
    row = lax.broadcasted_iota(jnp.int32, (8, width), 0)
    totals = jnp.zeros((8, width), F32)
    for h in range(nheads):
        cols = slice(h * width, (h + 1) * width)
        cum_h = cum[:, h : h + 1]
        last = cum[span - 1 : span, h : h + 1]
        key_w = (k_ref[:, cols].astype(F32) * jnp.exp(last - cum_h)).astype(BF16)
        query_w = (q_ref[:, cols].astype(F32) * jnp.exp(cum_h)).astype(BF16)
        state = contract(key_w, v_ref[:, cols], 0, 0)
        grad = contract(query_w, g_ref[:, cols], 0, 0)
        held_ref[h * width : (h + 1) * width, :] = state
        held_ref[rows + h * width : rows + (h + 1) * width, :] = grad
        sent_ref[h * width : (h + 1) * width, :] = state.astype(BF16)
        sent_ref[rows + h * width : rows + (h + 1) * width, :] = grad.astype(BF16)
        totals = jnp.where(row == h, jnp.broadcast_to(last, (8, width)), totals)
    high = totals.astype(BF16).astype(F32)
    sent_ref[2 * rows :, :] = jnp.concatenate([high, totals - high]).astype(BF16)
    logs_ref[0:8, :] = totals
    logs_ref[8:24, :] = jnp.zeros((16, width), F32)


def step_kernel(nheads, width, hop, first, final_next, got_ref, held_ref, logs_ref, *refs):
    if first:
        sent_ref, held_out, logs_out, enter_out = refs
    else:
        enter_ref, sent_ref, held_out, logs_out, enter_out = refs
    rows = nheads * width
    up = upper_half(hop)
    low = 1.0 - up
    tail = got_ref[2 * rows :, :].astype(F32)
    got_total = tail[0:8] + tail[8:16]
    total, before, after = logs_ref[0:8, :], logs_ref[8:16, :], logs_ref[16:24, :]
    own_decay, got_decay = jnp.exp(total), jnp.exp(got_total)
    from_before, from_after = up * jnp.exp(before), low * jnp.exp(after)
    total = total + got_total
    logs_out[0:8, :] = total
    logs_out[8:16, :] = before + up * got_total
    logs_out[16:24, :] = after + low * got_total
    if final_next:
        next_up = upper_half(2 * hop) > 0.5
    else:
        high = total.astype(BF16).astype(F32)
        sent_ref[2 * rows :, :] = jnp.concatenate([high, total - high]).astype(BF16)
    for h in range(nheads):
        one = slice(h * width, (h + 1) * width)
        two = slice(rows + h * width, rows + (h + 1) * width)
        got_state, got_grad = got_ref[one, :].astype(F32), got_ref[two, :].astype(F32)
        own, got = own_decay[h : h + 1, :], got_decay[h : h + 1, :]
        state = (up + low * got) * held_ref[one, :] + (up * own + low) * got_state
        grad = (low + up * got) * held_ref[two, :] + (low * own + up) * got_grad
        state_in = from_before[h : h + 1, :] * got_state
        grad_in = from_after[h : h + 1, :] * got_grad
        if not first:
            state_in = enter_ref[one, :] + state_in
            grad_in = enter_ref[two, :] + grad_in
        enter_out[one, :] = state_in
        enter_out[two, :] = grad_in
        held_out[one, :] = state
        held_out[two, :] = grad
        if final_next:
            sent_ref[one, :] = jnp.where(next_up, grad, state).astype(BF16)
        else:
            sent_ref[one, :] = state.astype(BF16)
            sent_ref[two, :] = grad.astype(BF16)


def local_kernel(nheads, width, decay_ref, q_ref, k_ref, v_ref, g_ref, out_ref):
    span = q_ref.shape[0]
    rows = nheads * width
    causal = triangle(span)
    tri = causal.astype(F32).astype(BF16)
    parts = thirds(decay_ref[...])
    cum = sum(contract(tri, part, 1, 0) for part in parts)
    cum_rows = sum(contract(part, tri, 0, 1) for part in parts)
    for h in range(nheads):
        cols = slice(h * width, (h + 1) * width)
        gap = cum[:, h : h + 1] - cum_rows[h : h + 1, :]
        decay = jnp.where(causal, jnp.exp(jnp.minimum(gap, 0.0)), 0.0)
        weighted = (contract(g_ref[:, cols], v_ref[:, cols], 1, 1) * decay).astype(BF16)
        out_ref[h * width : (h + 1) * width, :] = contract(k_ref[:, cols], weighted, 0, 1)
        out_ref[rows + h * width : rows + (h + 1) * width, :] = contract(
            q_ref[:, cols], weighted, 0, 0
        )


def carry_kernel(nheads, width, hop, decay_ref, v_ref, g_ref, got_ref, logs_ref, enter_ref, local_ref, out_ref):
    span = v_ref.shape[0]
    rows = nheads * width
    tri = triangle(span).astype(F32).astype(BF16)
    cum_rows = sum(contract(part, tri, 0, 1) for part in thirds(decay_ref[...]))
    up = upper_half(hop)
    low = 1.0 - up
    from_before = up * jnp.exp(logs_ref[8:16, :])
    from_after = low * jnp.exp(logs_ref[16:24, :])
    for h in range(nheads):
        cols = slice(h * width, (h + 1) * width)
        two = slice(rows + h * width, rows + (h + 1) * width)
        got = got_ref[cols, :].astype(F32)
        state_in = (enter_ref[cols, :] + from_before[h : h + 1, :] * got).astype(BF16)
        grad_in = (enter_ref[two, :] + from_after[h : h + 1, :] * got).astype(BF16)
        cum_h = cum_rows[h : h + 1, :]
        last = cum_h[:, span - 1 : span]
        dq = local_ref[cols, :] + contract(state_in, g_ref[:, cols], 1, 1) * jnp.exp(cum_h)
        dk = local_ref[two, :] + contract(grad_in, v_ref[:, cols], 1, 1) * jnp.exp(last - cum_h)
        out_ref[cols, :] = dq.astype(BF16)
        out_ref[two, :] = dk.astype(BF16)


def scan_blocks(sent, held, logs, nheads, width):
    count = lax.axis_size("seq")
    rows = nheads * width
    hop, enter = 1, None
    while True:
        got = lax.ppermute(sent, "seq", [(i, i ^ hop) for i in range(count)])
        if 2 * hop >= count:
            return got, logs, enter, hop
        final_next = 4 * hop >= count
        out_shape = (
            jax.ShapeDtypeStruct((rows if final_next else 2 * rows + 16, width), BF16),
            jax.ShapeDtypeStruct((2 * rows, width), F32),
            jax.ShapeDtypeStruct((24, width), F32),
            jax.ShapeDtypeStruct((2 * rows, width), F32),
        )
        args = [got, held, logs] + ([] if enter is None else [enter])
        sent, held, logs, enter = call(
            functools.partial(step_kernel, nheads, width, hop, enter is None, final_next),
            out_shape, 10 * rows * width, 16 * rows * width, *args,
        )
        hop *= 2


def share_order(count):
    bits = []
    hop = 2
    while hop < count:
        bits.append(hop)
        hop *= 2
    return bits, bits[::-1]


def gather_shares(piece):
    count = lax.axis_size("seq")
    even, odd = share_order(count)
    held = piece
    for hop_even, hop_odd in zip(even, odd):
        pairs = [(i, i ^ (hop_odd if i % 2 else hop_even)) for i in range(count)]
        held = jnp.concatenate([held, lax.ppermute(held, "seq", pairs)])
    return held, lax.ppermute(held, "seq", [(i, i ^ 1) for i in range(count)])


def share_deltas(count):
    even, odd = share_order(count)

    def spread(order):
        out = [0]
        for hop in order:
            out = out + [d ^ hop for d in out]
        return out

    return tuple(
        spread(first) + [d ^ 1 for d in spread(second)] for first, second in ((even, odd), (odd, even))
    )


def pack_kernel(share, npieces, starts_ref, wq_ref, wk_ref, *refs):
    outs, sems = refs[:npieces], refs[npieces]
    copies = []
    wide = wq_ref.shape[1]
    for i in range(npieces):
        rows = pl.ds(pl.multiple_of(starts_ref[i], 16), share)
        for j, src in enumerate((wq_ref, wk_ref)):
            copies.append(
                pltpu.make_async_copy(
                    src.at[rows, :], outs[i].at[:, pl.ds(j * wide, wide)], sems.at[i, j]
                )
            )
    for copy in copies:
        copy.start()
    for copy in copies:
        copy.wait()


def pack_weights(w_query, w_key, starts, share):
    npieces = len(starts)
    wide = w_query.shape[1]
    if share % 16:
        return [
            jnp.concatenate([lax.dynamic_slice_in_dim(w, s, share, 0) for w in (w_query, w_key)], axis=1)
            for s in starts
        ]
    return call(
        functools.partial(pack_kernel, share, npieces),
        [jax.ShapeDtypeStruct((share, 2 * wide), BF16)] * npieces,
        0, npieces * share * wide * 8,
        jnp.stack(starts).astype(jnp.int32), w_query, w_key,
        in_specs=[pl.BlockSpec(memory_space=pltpu.SMEM)] + [pl.BlockSpec(memory_space=pl.ANY)] * 2,
        out_specs=[pl.BlockSpec(memory_space=pl.ANY)] * npieces,
        scratch_shapes=[pltpu.SemaphoreType.DMA((npieces, 2))],
    )


def own_kernel(table_ref, wq_ref, wk_ref, grads_ref, out_ref):
    wide = wq_ref.shape[1]
    out_ref[...] = contract(wq_ref[...], grads_ref[:wide, :], 1, 0) + contract(
        wk_ref[...], grads_ref[wide:, :], 1, 0
    )


def add_kernel(blocks, nother, last, table_ref, held_ref, got_ref, *refs):
    others, refs = refs[:nother], refs[nother:]
    total_ref, out_ref, grads = refs
    step = pl.program_id(0)
    half = pl.num_programs(0) // 2

    @pl.when(step == 0)
    def _():
        if nother == 1:
            grads[...] = others[0][...]
        else:
            grads[...] = jnp.where(table_ref[2 * blocks] == 1, others[1][...], others[0][...])

    def finish(weights):
        total = total_ref[...] + contract(weights, grads[...], 1, 0)
        if last:
            per = blocks // pl.num_programs(0)
            share = out_ref.shape[0] // blocks
            for i in range(per):
                place = table_ref[blocks + step * per + i]
                out_ref[pl.ds(pl.multiple_of(place * share, 8), share), :] = total[
                    i * share : (i + 1) * share, :
                ].astype(BF16)
        else:
            out_ref[...] = total

    @pl.when(step < half)
    def _():
        finish(held_ref[...])

    @pl.when(step >= half)
    def _():
        finish(got_ref[...])


def own_product(table, w_query, w_key, grads, blocks):
    span = grads.shape[1]
    wide = w_query.shape[1]
    share = w_query.shape[0] // (lax.axis_size("head") * blocks)
    chunk = share * blocks
    grid_spec = pltpu.PrefetchScalarGridSpec(
        num_scalar_prefetch=1,
        grid=(blocks,),
        in_specs=[pl.BlockSpec((share, wide), lambda j, t: (t[j], 0))] * 2 + [whole(grads.shape)],
        out_specs=pl.BlockSpec((share, span), lambda j, t: (j, 0)),
    )
    return call(
        own_kernel, jax.ShapeDtypeStruct((chunk, span), F32),
        4 * chunk * span * wide, chunk * wide * 4 + chunk * span * 4,
        table, w_query, w_key, grads, grid_spec=grid_spec,
    )


def add_product(table, held, got, others, total, blocks, last):
    chunk, span = total.shape
    deep = held.shape[1]
    steps = 4
    rows = chunk // steps
    half = steps // 2
    grid_spec = pltpu.PrefetchScalarGridSpec(
        num_scalar_prefetch=1,
        grid=(steps,),
        in_specs=[
            pl.BlockSpec((rows, deep), lambda j, t: (jnp.minimum(j, half - 1), 0)),
            pl.BlockSpec((rows, deep), lambda j, t: (jnp.maximum(j - half, 0), 0)),
        ]
        + [whole(others[0].shape)] * len(others)
        + [pl.BlockSpec((rows, span), lambda j, t: (j, 0))],
        out_specs=whole(total.shape) if last else pl.BlockSpec((rows, span), lambda j, t: (j, 0)),
        scratch_shapes=[pltpu.VMEM(others[0].shape, BF16)],
    )
    return call(
        functools.partial(add_kernel, blocks, len(others), last),
        jax.ShapeDtypeStruct((chunk, span), BF16 if last else F32),
        2 * chunk * span * deep, chunk * deep * 2 + chunk * span * 6,
        table, held, got, *others, total, grid_spec=grid_spec,
    )


def shards(query_act, key_act, value_act, grad_output, log_decay, w_query, w_key):
    span = query_act.shape[0]
    nheads = log_decay.shape[1]
    width = query_act.shape[1] // nheads
    nseq, nhead = lax.axis_size("seq"), lax.axis_size("head")
    my_seq, my_head = lax.axis_index("seq"), lax.axis_index("head")
    chunk = w_query.shape[0] // nhead
    share = chunk // nseq
    rows = nheads * width

    starts, sources, routes = [], [], []
    for k in range(1, nhead):
        if nhead & (nhead - 1) == 0:
            routes.append([(i, i ^ k) for i in range(nhead)])
            target = source = my_head ^ k
        else:
            routes.append([(i, (i + k) % nhead) for i in range(nhead)])
            target, source = (my_head + k) % nhead, (my_head + nhead - k) % nhead
        starts.append(target * chunk + my_seq * share)
        sources.append(source)
    packed = pack_weights(w_query, w_key, starts, share)
    pieces = [lax.ppermute(p, "head", route) for p, route in zip(packed, routes)]

    sent, held, logs = call(
        functools.partial(states_kernel, nheads, width),
        (
            jax.ShapeDtypeStruct((2 * rows + 16, width), BF16),
            jax.ShapeDtypeStruct((2 * rows, width), F32),
            jax.ShapeDtypeStruct((24, width), F32),
        ),
        4 * span * rows * width, 8 * span * rows,
        log_decay, query_act, key_act, value_act, grad_output,
    )
    got, logs, enter, hop = scan_blocks(sent, held, logs, nheads, width)
    local = call(
        functools.partial(local_kernel, nheads, width),
        jax.ShapeDtypeStruct((2 * rows, span), F32),
        6 * span * span * rows, 16 * span * rows,
        log_decay, query_act, key_act, value_act, grad_output,
    )
    both = call(
        functools.partial(carry_kernel, nheads, width, hop),
        jax.ShapeDtypeStruct((2 * rows, span), BF16),
        4 * span * rows * width, 16 * span * rows,
        log_decay, value_act, grad_output, got, logs, enter, local,
    )

    if nhead == 4:
        p1 = lax.ppermute(both, "head", [(0, 1), (1, 0), (2, 3), (3, 2)])
        p2 = lax.ppermute(both, "head", [(1, 2), (2, 1)])
        p3 = lax.ppermute(p2, "head", [(2, 3), (1, 0)])
        p4 = lax.ppermute(p1, "head", [(1, 2), (2, 1)])
        p5 = lax.ppermute(p4, "head", [(2, 3), (1, 0)])
        inner = (my_head == 1) | (my_head == 2)
        others = [(p1,), (p3, p4), (p5, p2)]
    else:
        gathered = lax.all_gather(both, "head")
        inner = my_head < 0
        others = [(gathered[source],) for source in sources]

    even, odd = share_deltas(nseq)
    deltas = jnp.where(my_seq % 2 == 1, jnp.array(odd, jnp.int32), jnp.array(even, jnp.int32))
    places = deltas ^ my_seq
    table = jnp.concatenate([places + my_head * nseq, places, inner.astype(jnp.int32)[None]])
    total = own_product(table, w_query, w_key, both, nseq)
    for i, (piece, grads) in enumerate(zip(pieces, others)):
        held, got = gather_shares(piece)
        total = add_product(table, held, got, grads, total, nseq, i == nhead - 2)
    return total


def solution(mesh):
    placed = (
        P("seq", "head"),
        P("seq", "head"),
        P("seq", "head"),
        P("seq", "head"),
        P("seq", "head"),
        P(None, "head"),
        P(None, "head"),
    )
    return jax.shard_map(
        shards, mesh=mesh, in_specs=placed, out_specs=P("head", "seq"), check_vma=False
    )
```

```python
import functools

import jax
import jax.numpy as jnp
from jax import lax
from jax.experimental import pallas as pl
from jax.experimental.pallas import tpu as pltpu
from jax.sharding import PartitionSpec as P

F32 = jnp.float32
BF16 = jnp.bfloat16
VMEM_BYTES = 40 * 1024 * 1024
PACKSPACE = pltpu.VMEM
WAIT1 = int(1.0e15 * 20e-6)
WAIT2 = int(1.0e15 * 40e-6)


def contract(a, b, left, right):
    return lax.dot_general(a, b, (((left,), (right,)), ((), ())), preferred_element_type=F32)


def call(kernel, out_shape, flops, nbytes, *args, aliases=None, vmem=VMEM_BYTES, **spec):
    return pl.pallas_call(
        kernel,
        out_shape=out_shape,
        cost_estimate=pl.CostEstimate(flops=flops, bytes_accessed=nbytes, transcendentals=0),
        compiler_params=pltpu.CompilerParams(vmem_limit_bytes=vmem),
        input_output_aliases=aliases or {},
        **spec,
    )(*args)


def gate_kernel(count, *refs):
    del count, refs


def gate(passed, tokens=(), flops=0):
    return call(
        functools.partial(gate_kernel, len(passed)),
        [jax.ShapeDtypeStruct(x.shape, x.dtype) for x in passed],
        flops, 0, *passed, *tokens,
        aliases={i: i for i in range(len(passed))},
        in_specs=[pl.BlockSpec(memory_space=pl.ANY)] * (len(passed) + len(tokens)),
        out_specs=[pl.BlockSpec(memory_space=pl.ANY)] * len(passed),
    )


def whole(shape):
    return pl.BlockSpec(shape, lambda *_: (0,) * len(shape))


def thirds(x):
    high = x.astype(BF16)
    rest = x - high.astype(F32)
    middle = rest.astype(BF16)
    return high, middle, (rest - middle.astype(F32)).astype(BF16)


def triangle(span):
    rows = lax.broadcasted_iota(jnp.int32, (span, span), 0)
    cols = lax.broadcasted_iota(jnp.int32, (span, span), 1)
    return rows >= cols


def upper_half(hop):
    return ((lax.axis_index("seq") // hop) % 2).astype(F32)


def states_kernel(nheads, width, decay_ref, q_ref, k_ref, v_ref, g_ref, sent_ref, held_ref, logs_ref):
    span = q_ref.shape[0]
    tri = triangle(span).astype(F32).astype(BF16)
    cum = sum(contract(tri, part, 1, 1) for part in thirds(decay_ref[...]))
    rows = nheads * width
    row = lax.broadcasted_iota(jnp.int32, (8, width), 0)
    totals = jnp.zeros((8, width), F32)
    for h in range(nheads):
        cols = slice(h * width, (h + 1) * width)
        cum_h = cum[:, h : h + 1]
        last = cum[span - 1 : span, h : h + 1]
        key_w = (k_ref[:, cols].astype(F32) * jnp.exp(last - cum_h)).astype(BF16)
        query_w = (q_ref[:, cols].astype(F32) * jnp.exp(cum_h)).astype(BF16)
        state = contract(key_w, v_ref[:, cols], 0, 0)
        grad = contract(query_w, g_ref[:, cols], 0, 0)
        held_ref[h * width : (h + 1) * width, :] = state
        held_ref[rows + h * width : rows + (h + 1) * width, :] = grad
        sent_ref[h * width : (h + 1) * width, :] = state.astype(BF16)
        sent_ref[rows + h * width : rows + (h + 1) * width, :] = grad.astype(BF16)
        totals = jnp.where(row == h, jnp.broadcast_to(last, (8, width)), totals)
    high = totals.astype(BF16).astype(F32)
    sent_ref[2 * rows :, :] = jnp.concatenate([high, totals - high]).astype(BF16)
    logs_ref[0:8, :] = totals
    logs_ref[8:24, :] = jnp.zeros((16, width), F32)


def step_kernel(nheads, width, hop, first, final_next, got_ref, held_ref, logs_ref, *refs):
    if first:
        sent_ref, held_out, logs_out, enter_out = refs
    else:
        enter_ref, sent_ref, held_out, logs_out, enter_out = refs
    rows = nheads * width
    up = upper_half(hop)
    low = 1.0 - up
    tail = got_ref[2 * rows :, :].astype(F32)
    got_total = tail[0:8] + tail[8:16]
    total, before, after = logs_ref[0:8, :], logs_ref[8:16, :], logs_ref[16:24, :]
    own_decay, got_decay = jnp.exp(total), jnp.exp(got_total)
    from_before, from_after = up * jnp.exp(before), low * jnp.exp(after)
    total = total + got_total
    logs_out[0:8, :] = total
    logs_out[8:16, :] = before + up * got_total
    logs_out[16:24, :] = after + low * got_total
    if final_next:
        next_up = upper_half(2 * hop) > 0.5
    else:
        high = total.astype(BF16).astype(F32)
        sent_ref[2 * rows :, :] = jnp.concatenate([high, total - high]).astype(BF16)
    for h in range(nheads):
        one = slice(h * width, (h + 1) * width)
        two = slice(rows + h * width, rows + (h + 1) * width)
        got_state, got_grad = got_ref[one, :].astype(F32), got_ref[two, :].astype(F32)
        own, got = own_decay[h : h + 1, :], got_decay[h : h + 1, :]
        state = (up + low * got) * held_ref[one, :] + (up * own + low) * got_state
        grad = (low + up * got) * held_ref[two, :] + (low * own + up) * got_grad
        state_in = from_before[h : h + 1, :] * got_state
        grad_in = from_after[h : h + 1, :] * got_grad
        if not first:
            state_in = enter_ref[one, :] + state_in
            grad_in = enter_ref[two, :] + grad_in
        enter_out[one, :] = state_in
        enter_out[two, :] = grad_in
        held_out[one, :] = state
        held_out[two, :] = grad
        if final_next:
            sent_ref[one, :] = jnp.where(next_up, grad, state).astype(BF16)
        else:
            sent_ref[one, :] = state.astype(BF16)
            sent_ref[two, :] = grad.astype(BF16)


def local_kernel(nheads, width, decay_ref, q_ref, k_ref, v_ref, g_ref, out_ref):
    span = q_ref.shape[0]
    rows = nheads * width
    causal = triangle(span)
    tri = causal.astype(F32).astype(BF16)
    parts = thirds(decay_ref[...])
    cum = sum(contract(tri, part, 1, 1) for part in parts)
    cum_rows = sum(contract(part, tri, 1, 1) for part in parts)
    for h in range(nheads):
        cols = slice(h * width, (h + 1) * width)
        gap = cum[:, h : h + 1] - cum_rows[h : h + 1, :]
        decay = jnp.where(causal, jnp.exp(jnp.minimum(gap, 0.0)), 0.0)
        weighted = (contract(g_ref[:, cols], v_ref[:, cols], 1, 1) * decay).astype(BF16)
        out_ref[h * width : (h + 1) * width, :] = contract(k_ref[:, cols], weighted, 0, 1)
        out_ref[rows + h * width : rows + (h + 1) * width, :] = contract(
            q_ref[:, cols], weighted, 0, 0
        )


def carry_kernel(nheads, width, hop, decay_ref, v_ref, g_ref, got_ref, logs_ref, enter_ref, local_ref, out_ref):
    span = v_ref.shape[0]
    rows = nheads * width
    tri = triangle(span).astype(F32).astype(BF16)
    cum_rows = sum(contract(part, tri, 1, 1) for part in thirds(decay_ref[...]))
    up = upper_half(hop)
    low = 1.0 - up
    from_before = up * jnp.exp(logs_ref[8:16, :])
    from_after = low * jnp.exp(logs_ref[16:24, :])
    for h in range(nheads):
        cols = slice(h * width, (h + 1) * width)
        two = slice(rows + h * width, rows + (h + 1) * width)
        got = got_ref[cols, :].astype(F32)
        state_in = (enter_ref[cols, :] + from_before[h : h + 1, :] * got).astype(BF16)
        grad_in = (enter_ref[two, :] + from_after[h : h + 1, :] * got).astype(BF16)
        cum_h = cum_rows[h : h + 1, :]
        last = cum_h[:, span - 1 : span]
        dq = local_ref[cols, :] + contract(state_in, g_ref[:, cols], 1, 1) * jnp.exp(cum_h)
        dk = local_ref[two, :] + contract(grad_in, v_ref[:, cols], 1, 1) * jnp.exp(last - cum_h)
        out_ref[cols, :] = dq.astype(BF16)
        out_ref[two, :] = dk.astype(BF16)


def share_order(count):
    bits = []
    hop = 2
    while hop < count:
        bits.append(hop)
        hop *= 2
    return bits, bits[::-1]


def share_hop(held, number):
    count = lax.axis_size("seq")
    even, odd = share_order(count)
    even, odd = even + [1], odd + [1]
    pairs = [(i, i ^ (odd[number] if i % 2 else even[number])) for i in range(count)]
    return lax.ppermute(held, "seq", pairs)


def share_deltas(count):
    even, odd = share_order(count)

    def spread(order):
        out = [0]
        for hop in order:
            out = out + [d ^ hop for d in out]
        return out

    return tuple(
        spread(first) + [d ^ 1 for d in spread(second)] for first, second in ((even, odd), (odd, even))
    )


def pack_kernel(share, shifts, wq_ref, wk_ref, *refs):
    count, nseq = lax.axis_size("head"), lax.axis_size("seq")
    mine, my_seq = lax.axis_index("head"), lax.axis_index("seq")
    outs, sems = refs[: len(shifts)], refs[len(shifts)]
    copies = []
    for i, shift in enumerate(shifts):
        block = lax.rem(mine + shift, count) * nseq + my_seq
        rows = pl.ds(pl.multiple_of(block * share, 16), share)
        for j, src in enumerate((wq_ref, wk_ref)):
            copies.append(
                pltpu.make_async_copy(
                    src.at[rows, :], outs[i].at[pl.ds(j * share, share), :], sems.at[i, j]
                )
            )
    for copy in copies:
        copy.start()
    for copy in copies:
        copy.wait()


def pack_weights(w_query, w_key, shifts, share):
    wide = w_query.shape[1]
    if share % 16:
        count, nseq = lax.axis_size("head"), lax.axis_size("seq")
        blocks = [(lax.axis_index("head") + k) % count * nseq + lax.axis_index("seq") for k in shifts]
        return [
            jnp.concatenate(
                [lax.dynamic_slice_in_dim(w, block * share, share, 0) for w in (w_query, w_key)]
            )
            for block in blocks
        ]
    return call(
        functools.partial(pack_kernel, share, shifts),
        [jax.ShapeDtypeStruct((2 * share, wide), BF16)] * len(shifts),
        0, len(shifts) * share * wide * 8,
        w_query, w_key,
        in_specs=[pl.BlockSpec(memory_space=pl.ANY)] * 2,
        out_specs=[pl.BlockSpec(memory_space=PACKSPACE)] * len(shifts),
        scratch_shapes=[pltpu.SemaphoreType.DMA((len(shifts), 2))],
        vmem=58 * 1024 * 1024,
    )


def own_kernel(table_ref, wq_ref, wk_ref, grads_ref, out_ref):
    wide = wq_ref.shape[1]
    out_ref[...] = contract(wq_ref[...], grads_ref[:wide, :], 1, 0) + contract(
        wk_ref[...], grads_ref[wide:, :], 1, 0
    )


def add_kernel(blocks, nother, last, table_ref, held_ref, got_ref, *refs):
    others, refs = refs[:nother], refs[nother:]
    total_ref, out_ref, grads = refs
    step = pl.program_id(0)
    half = pl.num_programs(0) // 2

    @pl.when(step == 0)
    def _():
        if nother == 1:
            grads[...] = others[0][...]
        else:
            grads[...] = jnp.where(table_ref[2 * blocks] == 1, others[1][...], others[0][...])

    def finish(weights):
        wide = weights.shape[1]
        per = blocks // pl.num_programs(0)
        share = weights.shape[0] // (2 * per)
        left, right = grads[:wide, :], grads[wide:, :]
        parts = []
        for i in range(per):
            start = 2 * i * share
            parts.append(
                contract(weights[start : start + share], left, 1, 0)
                + contract(weights[start + share : start + 2 * share], right, 1, 0)
            )
        total = total_ref[...] + jnp.concatenate(parts)
        if last:
            for i in range(per):
                place = table_ref[blocks + step * per + i]
                out_ref[pl.ds(pl.multiple_of(place * share, 8), share), :] = total[
                    i * share : (i + 1) * share, :
                ].astype(BF16)
        else:
            out_ref[...] = total

    @pl.when(step < half)
    def _():
        finish(held_ref[...])

    @pl.when(step >= half)
    def _():
        finish(got_ref[...])


def own_product(table, w_query, w_key, grads, blocks):
    span = grads.shape[1]
    wide = w_query.shape[1]
    share = w_query.shape[0] // (lax.axis_size("head") * blocks)
    chunk = share * blocks
    grid_spec = pltpu.PrefetchScalarGridSpec(
        num_scalar_prefetch=1,
        grid=(blocks,),
        in_specs=[pl.BlockSpec((share, wide), lambda j, t: (t[j], 0))] * 2 + [whole(grads.shape)],
        out_specs=pl.BlockSpec((share, span), lambda j, t: (j, 0)),
    )
    return call(
        own_kernel, jax.ShapeDtypeStruct((chunk, span), F32),
        4 * chunk * span * wide, chunk * wide * 4 + chunk * span * 4,
        table, w_query, w_key, grads, grid_spec=grid_spec,
    )


def add_product(table, held, got, others, total, blocks, last):
    chunk, span = total.shape
    wide = held.shape[1]
    steps = 4
    rows = chunk // steps
    half = steps // 2
    grid_spec = pltpu.PrefetchScalarGridSpec(
        num_scalar_prefetch=1,
        grid=(steps,),
        in_specs=[
            pl.BlockSpec((2 * rows, wide), lambda j, t: (jnp.minimum(j, half - 1), 0)),
            pl.BlockSpec((2 * rows, wide), lambda j, t: (jnp.maximum(j - half, 0), 0)),
        ]
        + [whole(others[0].shape)] * len(others)
        + [pl.BlockSpec((rows, span), lambda j, t: (j, 0))],
        out_specs=whole(total.shape) if last else pl.BlockSpec((rows, span), lambda j, t: (j, 0)),
        scratch_shapes=[pltpu.VMEM(others[0].shape, BF16)],
    )
    return call(
        functools.partial(add_kernel, blocks, len(others), last),
        jax.ShapeDtypeStruct((chunk, span), BF16 if last else F32),
        4 * chunk * span * wide, chunk * wide * 4 + chunk * span * 6,
        table, held, got, *others, total, grid_spec=grid_spec,
    )


def shards(query_act, key_act, value_act, grad_output, log_decay, w_query, w_key):
    span = query_act.shape[0]
    nheads = log_decay.shape[1]
    width = query_act.shape[1] // nheads
    nseq, nhead = lax.axis_size("seq"), lax.axis_size("head")
    my_seq, my_head = lax.axis_index("seq"), lax.axis_index("head")
    chunk = w_query.shape[0] // nhead
    share = chunk // nseq
    rows = nheads * width

    shifts = [1, nhead - 1] + list(range(2, nhead - 1))
    ring = {k: [(i, (i + k) % nhead) for i in range(nhead)] for k in shifts}
    packed = pack_weights(w_query, w_key, shifts, share)
    pieces = [lax.ppermute(p, "head", ring[k]) for p, k in zip(packed, shifts)]

    decay = gate([log_decay.T], packed)[0]
    sent, held, logs = call(
        functools.partial(states_kernel, nheads, width),
        (
            jax.ShapeDtypeStruct((2 * rows + 16, width), BF16),
            jax.ShapeDtypeStruct((2 * rows, width), F32),
            jax.ShapeDtypeStruct((24, width), F32),
        ),
        4 * span * rows * width, 8 * span * rows,
        decay, query_act, key_act, value_act, grad_output,
    )
    nhops = len(share_order(nseq)[0]) + 1
    holds = [[p] for p in pieces]
    progress = [0] * len(pieces)

    def advance(which):
        for i in which:
            if progress[i] < nhops:
                held = holds[i][0] if progress[i] == 0 else jnp.concatenate(holds[i])
                holds[i] = [held, share_hop(held, progress[i])]
                progress[i] += 1

    hop, enter = 1, None
    while True:
        if 2 * hop >= nseq:
            early = range(min(2, len(holds)))
            sent, *firsts = gate([sent] + [holds[i][0] for i in early])
            for i in early:
                holds[i][0] = firsts[i]
            advance(early)
        got = lax.ppermute(sent, "seq", [(i, i ^ hop) for i in range(nseq)])
        if 2 * hop >= nseq:
            break
        final_next = 4 * hop >= nseq
        out_shape = (
            jax.ShapeDtypeStruct((rows if final_next else 2 * rows + 16, width), BF16),
            jax.ShapeDtypeStruct((2 * rows, width), F32),
            jax.ShapeDtypeStruct((24, width), F32),
            jax.ShapeDtypeStruct((2 * rows, width), F32),
        )
        args = [got, held, logs] + ([] if enter is None else [enter])
        sent, held, logs, enter = call(
            functools.partial(step_kernel, nheads, width, hop, enter is None, final_next),
            out_shape, 10 * rows * width, 16 * rows * width, *args,
        )
        hop *= 2
    local = call(
        functools.partial(local_kernel, nheads, width),
        jax.ShapeDtypeStruct((2 * rows, span), F32),
        6 * span * span * rows, 16 * span * rows,
        decay, query_act, key_act, value_act, grad_output,
    )
    both = call(
        functools.partial(carry_kernel, nheads, width, hop),
        jax.ShapeDtypeStruct((2 * rows, span), BF16),
        4 * span * rows * width, 16 * span * rows,
        decay, value_act, grad_output, got, logs, enter, local,
    )

    even, odd = share_deltas(nseq)
    deltas = jnp.where(my_seq % 2 == 1, jnp.array(odd, jnp.int32), jnp.array(even, jnp.int32))
    places = deltas ^ my_seq
    table = jnp.concatenate([places + my_head * nseq, places, (my_head >= 2).astype(jnp.int32)[None]])
    total = own_product(table, w_query, w_key, both, nseq)

    if nhead == 4:
        p1 = lax.ppermute(both, "head", ring[1])
        p3 = lax.ppermute(both, "head", ring[3])
        holds[0][1], holds[1][1] = gate([holds[0][1], holds[1][1]], [both])
        advance([0, 1])
        (holds[2][0],) = gate([holds[2][0]], [holds[0][0], holds[1][0]])
        advance([2])
        holds[0][1], holds[1][1], holds[2][1], p1, p3 = gate(
            [holds[0][1], holds[1][1], holds[2][1], p1, p3], [total]
        )
        advance([0, 1, 2])
        up = lax.ppermute(p1, "head", [(1, 2), (2, 3)])
        down = lax.ppermute(p3, "head", [(2, 1), (1, 0)])
        others = [(p1,), (p3,), (down, up)]
    else:
        gathered = lax.all_gather(both, "head")
        others = [(gathered[(my_head + nhead - k) % nhead],) for k in shifts]

    while min(progress) < nhops:
        advance(range(len(pieces)))
    for i, grads in enumerate(others):
        total = add_product(table, holds[i][0], holds[i][1], grads, total, nseq, i == nhead - 2)
    return total


def solution(mesh):
    placed = (
        P("seq", "head"),
        P("seq", "head"),
        P("seq", "head"),
        P("seq", "head"),
        P("seq", "head"),
        P(None, "head"),
        P(None, "head"),
    )
    return jax.shard_map(
        shards, mesh=mesh, in_specs=placed, out_specs=P("head", "seq"), check_vma=False
    )
```

```python
import functools

import jax
import jax.numpy as jnp
from jax import lax
from jax.experimental import pallas as pl
from jax.experimental.pallas import tpu as pltpu
from jax.sharding import PartitionSpec as P

F32 = jnp.float32
BF16 = jnp.bfloat16
VMEM_BYTES = 16 * 1024 * 1024
EARLYC = False


def contract(a, b, left, right):
    return lax.dot_general(a, b, (((left,), (right,)), ((), ())), preferred_element_type=F32)


def call(kernel, out_shape, flops, nbytes, *args, aliases=None, vmem=VMEM_BYTES, **spec):
    return pl.pallas_call(
        kernel,
        out_shape=out_shape,
        cost_estimate=pl.CostEstimate(flops=flops, bytes_accessed=nbytes, transcendentals=0),
        compiler_params=pltpu.CompilerParams(vmem_limit_bytes=vmem),
        input_output_aliases=aliases or {},
        **spec,
    )(*args)


def gate_kernel(count, *refs):
    del count, refs


def gate(passed, tokens=(), flops=0):
    return call(
        functools.partial(gate_kernel, len(passed)),
        [jax.ShapeDtypeStruct(x.shape, x.dtype) for x in passed],
        flops, 0, *passed, *tokens,
        aliases={i: i for i in range(len(passed))},
        in_specs=[pl.BlockSpec(memory_space=pl.ANY)] * (len(passed) + len(tokens)),
        out_specs=[pl.BlockSpec(memory_space=pl.ANY)] * len(passed),
    )


def whole(shape):
    return pl.BlockSpec(shape, lambda *_: (0,) * len(shape))


def thirds(x):
    high = x.astype(BF16)
    rest = x - high.astype(F32)
    middle = rest.astype(BF16)
    return high, middle, (rest - middle.astype(F32)).astype(BF16)


def triangle(span):
    rows = lax.broadcasted_iota(jnp.int32, (span, span), 0)
    cols = lax.broadcasted_iota(jnp.int32, (span, span), 1)
    return rows >= cols


def upper_half(hop):
    return ((lax.axis_index("seq") // hop) % 2).astype(F32)


def states_kernel(nheads, width, decay_ref, q_ref, k_ref, v_ref, g_ref, token_ref, sent_ref, held_ref, logs_ref):
    span = q_ref.shape[0]
    tri = triangle(span).astype(F32).astype(BF16)
    cum = sum(contract(tri, part, 1, 1) for part in thirds(decay_ref[...]))
    rows = nheads * width
    row = lax.broadcasted_iota(jnp.int32, (8, width), 0)
    totals = jnp.zeros((8, width), F32)
    for h in range(nheads):
        cols = slice(h * width, (h + 1) * width)
        cum_h = cum[:, h : h + 1]
        last = cum[span - 1 : span, h : h + 1]
        key_w = (k_ref[:, cols].astype(F32) * jnp.exp(last - cum_h)).astype(BF16)
        query_w = (q_ref[:, cols].astype(F32) * jnp.exp(cum_h)).astype(BF16)
        state = contract(key_w, v_ref[:, cols], 0, 0)
        grad = contract(query_w, g_ref[:, cols], 0, 0)
        held_ref[h * width : (h + 1) * width, :] = state
        held_ref[rows + h * width : rows + (h + 1) * width, :] = grad
        sent_ref[h * width : (h + 1) * width, :] = state.astype(BF16)
        sent_ref[rows + h * width : rows + (h + 1) * width, :] = grad.astype(BF16)
        totals = jnp.where(row == h, jnp.broadcast_to(last, (8, width)), totals)
    high = totals.astype(BF16).astype(F32)
    sent_ref[2 * rows :, :] = jnp.concatenate([high, totals - high]).astype(BF16)
    logs_ref[0:8, :] = totals
    logs_ref[8:24, :] = jnp.zeros((16, width), F32)


def step_kernel(nheads, width, hop, first, final_next, got_ref, held_ref, logs_ref, *refs):
    if first:
        sent_ref, held_out, logs_out, enter_out = refs
    else:
        enter_ref, sent_ref, held_out, logs_out, enter_out = refs
    rows = nheads * width
    up = upper_half(hop)
    low = 1.0 - up
    tail = got_ref[2 * rows :, :].astype(F32)
    got_total = tail[0:8] + tail[8:16]
    total, before, after = logs_ref[0:8, :], logs_ref[8:16, :], logs_ref[16:24, :]
    own_decay, got_decay = jnp.exp(total), jnp.exp(got_total)
    from_before, from_after = up * jnp.exp(before), low * jnp.exp(after)
    total = total + got_total
    logs_out[0:8, :] = total
    logs_out[8:16, :] = before + up * got_total
    logs_out[16:24, :] = after + low * got_total
    if final_next:
        next_up = upper_half(2 * hop) > 0.5
    else:
        high = total.astype(BF16).astype(F32)
        sent_ref[2 * rows :, :] = jnp.concatenate([high, total - high]).astype(BF16)
    for h in range(nheads):
        one = slice(h * width, (h + 1) * width)
        two = slice(rows + h * width, rows + (h + 1) * width)
        got_state, got_grad = got_ref[one, :].astype(F32), got_ref[two, :].astype(F32)
        own, got = own_decay[h : h + 1, :], got_decay[h : h + 1, :]
        state = (up + low * got) * held_ref[one, :] + (up * own + low) * got_state
        grad = (low + up * got) * held_ref[two, :] + (low * own + up) * got_grad
        state_in = from_before[h : h + 1, :] * got_state
        grad_in = from_after[h : h + 1, :] * got_grad
        if not first:
            state_in = enter_ref[one, :] + state_in
            grad_in = enter_ref[two, :] + grad_in
        enter_out[one, :] = state_in
        enter_out[two, :] = grad_in
        held_out[one, :] = state
        held_out[two, :] = grad
        if final_next:
            sent_ref[one, :] = jnp.where(next_up, grad, state).astype(BF16)
        else:
            sent_ref[one, :] = state.astype(BF16)
            sent_ref[two, :] = grad.astype(BF16)


def local_kernel(nheads, width, decay_ref, q_ref, k_ref, v_ref, g_ref, out_ref):
    span = q_ref.shape[0]
    rows = nheads * width
    causal = triangle(span)
    tri = causal.astype(F32).astype(BF16)
    parts = thirds(decay_ref[...])
    cum = sum(contract(tri, part, 1, 1) for part in parts)
    cum_rows = sum(contract(part, tri, 1, 1) for part in parts)
    for h in range(nheads):
        cols = slice(h * width, (h + 1) * width)
        gap = cum[:, h : h + 1] - cum_rows[h : h + 1, :]
        decay = jnp.where(causal, jnp.exp(jnp.minimum(gap, 0.0)), 0.0)
        weighted = (contract(g_ref[:, cols], v_ref[:, cols], 1, 1) * decay).astype(BF16)
        out_ref[h * width : (h + 1) * width, :] = contract(k_ref[:, cols], weighted, 0, 1)
        out_ref[rows + h * width : rows + (h + 1) * width, :] = contract(
            q_ref[:, cols], weighted, 0, 0
        )


def carry_kernel(nheads, width, hop, decay_ref, v_ref, g_ref, got_ref, logs_ref, enter_ref, local_ref, out_ref):
    span = v_ref.shape[0]
    rows = nheads * width
    tri = triangle(span).astype(F32).astype(BF16)
    cum_rows = sum(contract(part, tri, 1, 1) for part in thirds(decay_ref[...]))
    up = upper_half(hop)
    low = 1.0 - up
    from_before = up * jnp.exp(logs_ref[8:16, :])
    from_after = low * jnp.exp(logs_ref[16:24, :])
    for h in range(nheads):
        cols = slice(h * width, (h + 1) * width)
        two = slice(rows + h * width, rows + (h + 1) * width)
        got = got_ref[cols, :].astype(F32)
        state_in = (enter_ref[cols, :] + from_before[h : h + 1, :] * got).astype(BF16)
        grad_in = (enter_ref[two, :] + from_after[h : h + 1, :] * got).astype(BF16)
        cum_h = cum_rows[h : h + 1, :]
        last = cum_h[:, span - 1 : span]
        dq = local_ref[cols, :] + contract(state_in, g_ref[:, cols], 1, 1) * jnp.exp(cum_h)
        dk = local_ref[two, :] + contract(grad_in, v_ref[:, cols], 1, 1) * jnp.exp(last - cum_h)
        out_ref[cols, :] = dq.astype(BF16)
        out_ref[two, :] = dk.astype(BF16)


def share_order(count):
    bits = []
    hop = 2
    while hop < count:
        bits.append(hop)
        hop *= 2
    return bits, bits[::-1]


def share_hop(held, number):
    count = lax.axis_size("seq")
    even, odd = share_order(count)
    even, odd = even + [1], odd + [1]
    pairs = [(i, i ^ (odd[number] if i % 2 else even[number])) for i in range(count)]
    return lax.ppermute(held, "seq", pairs)


def share_deltas(count):
    even, odd = share_order(count)

    def spread(order):
        out = [0]
        for hop in order:
            out = out + [d ^ hop for d in out]
        return out

    return tuple(
        spread(first) + [d ^ 1 for d in spread(second)] for first, second in ((even, odd), (odd, even))
    )


def pack_kernel(share, shifts, wq_ref, wk_ref, *refs):
    count, nseq = lax.axis_size("head"), lax.axis_size("seq")
    mine, my_seq = lax.axis_index("head"), lax.axis_index("seq")
    outs, sems = refs[: len(shifts)], refs[len(shifts)]
    copies = []
    for i, shift in enumerate(shifts):
        block = lax.rem(mine + shift, count) * nseq + my_seq
        rows = pl.ds(pl.multiple_of(block * share, 16), share)
        for j, src in enumerate((wq_ref, wk_ref)):
            copies.append(
                pltpu.make_async_copy(
                    src.at[rows, :], outs[i].at[pl.ds(j * share, share), :], sems.at[i, j]
                )
            )
    for copy in copies:
        copy.start()
    for copy in copies:
        copy.wait()


def pack_weights(w_query, w_key, shifts, share):
    wide = w_query.shape[1]
    if share % 16:
        count, nseq = lax.axis_size("head"), lax.axis_size("seq")
        blocks = [(lax.axis_index("head") + k) % count * nseq + lax.axis_index("seq") for k in shifts]
        return [
            jnp.concatenate(
                [lax.dynamic_slice_in_dim(w, block * share, share, 0) for w in (w_query, w_key)]
            )
            for block in blocks
        ]
    return call(
        functools.partial(pack_kernel, share, shifts),
        [
            jax.ShapeDtypeStruct((2 * share + (16 if i == 2 else 0), wide), BF16)
            for i in range(len(shifts))
        ],
        0, len(shifts) * share * wide * 8,
        *(pltpu.with_memory_space_constraint(w, pltpu.HBM) for w in (w_query, w_key)),
        in_specs=[pl.BlockSpec(memory_space=pl.ANY)] * 2,
        out_specs=[pl.BlockSpec(memory_space=pltpu.VMEM)] * len(shifts),
        scratch_shapes=[pltpu.SemaphoreType.DMA((len(shifts), 2))],
    )


def row_block(weights, grads):
    share, wide = weights.shape[0] // 2, weights.shape[1]
    return contract(weights[:share], grads[:wide], 1, 0) + contract(weights[share:], grads[wide:], 1, 0)


def own_kernel(wq_ref, wk_ref, grads_ref, out_ref, near_q, near_k, sems):
    chunk, wide = near_q.shape
    rows = pl.ds(pl.multiple_of(lax.axis_index("head") * chunk, 16), chunk)
    copies = [
        pltpu.make_async_copy(src.at[rows, :], dst, sems.at[i])
        for i, (src, dst) in enumerate(((wq_ref, near_q), (wk_ref, near_k)))
    ]
    for copy in copies:
        copy.start()
    for copy in copies:
        copy.wait()
    out_ref[...] = contract(near_q[...], grads_ref[:wide, :], 1, 0) + contract(
        near_k[...], grads_ref[wide:, :], 1, 0
    )


def own_product(w_query, w_key, grads, chunk):
    wide = w_query.shape[1]
    return call(
        own_kernel, jax.ShapeDtypeStruct((chunk, grads.shape[1]), F32),
        4 * chunk * grads.shape[1] * wide, chunk * wide * 4,
        *(pltpu.with_memory_space_constraint(w, pltpu.HBM) for w in (w_query, w_key)), grads,
        in_specs=[pl.BlockSpec(memory_space=pl.ANY)] * 2 + [pl.BlockSpec(memory_space=pltpu.VMEM)],
        out_specs=pl.BlockSpec(memory_space=pltpu.VMEM),
        scratch_shapes=[pltpu.VMEM((chunk, wide), BF16)] * 2 + [pltpu.SemaphoreType.DMA((2,))],
    )


def add_kernel(counts, last, table_ref, total_ref, *refs):
    out_ref, refs = refs[-1], list(refs[:-1])
    groups = []
    for nblocks, nother in counts:
        blocks, refs = refs[:nblocks], refs[nblocks:]
        others, refs = refs[:nother], refs[nother:]
        grads = others[0][...]
        if nother == 2:
            grads = jnp.where(table_ref[0] == 1, others[1][...], grads)
        groups.append((blocks, grads))
    share = groups[0][0][0].shape[0]
    nshares = table_ref.shape[0] - 1
    share = out_ref.shape[0] // nshares
    for j in range(nshares):
        rows = pl.ds(pl.multiple_of(table_ref[1 + j] * share, 8), share)
        total = total_ref[rows, :]
        for blocks, grads in groups:
            at = 2 * share * j
            for block in blocks:
                if at < block.shape[0]:
                    total = total + row_block(block[at : at + 2 * share], grads)
                    break
                at -= block.shape[0]
        out_ref[rows, :] = total.astype(out_ref.dtype)


def add_product(table, total, terms, last):
    chunk, span = total.shape
    counts = tuple((len(blocks), len(others)) for blocks, others in terms)
    args = [x for blocks, others in terms for x in (*blocks, *others)]
    return call(
        functools.partial(add_kernel, counts, last),
        jax.ShapeDtypeStruct((chunk, span), BF16 if last else F32),
        2 * len(terms) * chunk * span * args[-1].shape[0], chunk * span * 8,
        table, total, *args,
        in_specs=[pl.BlockSpec(memory_space=pltpu.SMEM)]
        + [pl.BlockSpec(memory_space=pltpu.VMEM)] * (1 + len(args)),
        out_specs=pl.BlockSpec(memory_space=pltpu.VMEM),
        vmem=24 * 1024 * 1024,
    )


def shards(query_act, key_act, value_act, grad_output, log_decay, w_query, w_key):
    span = query_act.shape[0]
    nheads = log_decay.shape[1]
    width = query_act.shape[1] // nheads
    nseq, nhead = lax.axis_size("seq"), lax.axis_size("head")
    my_seq, my_head = lax.axis_index("seq"), lax.axis_index("head")
    chunk = w_query.shape[0] // nhead
    share = chunk // nseq
    rows = nheads * width

    shifts = [1, nhead - 1] + list(range(2, nhead - 1))
    ring = {k: [(i, (i + k) % nhead) for i in range(nhead)] for k in shifts}
    packed = pack_weights(w_query, w_key, shifts, share)
    pieces = [lax.ppermute(p, "head", ring[k])[: 2 * share] for p, k in zip(packed, shifts)]

    decay = log_decay.T
    sent, held, logs = call(
        functools.partial(states_kernel, nheads, width),
        (
            jax.ShapeDtypeStruct((2 * rows + 16, width), BF16),
            jax.ShapeDtypeStruct((2 * rows, width), F32),
            jax.ShapeDtypeStruct((24, width), F32),
        ),
        4 * span * rows * width, 8 * span * rows,
        decay, query_act, key_act, value_act, grad_output, packed[0],
        in_specs=[pl.BlockSpec(memory_space=pltpu.VMEM)] * 5 + [pl.BlockSpec(memory_space=pl.ANY)],
    )
    nhops = len(share_order(nseq)[0]) + 1
    holds = [[p] for p in pieces]
    progress = [0] * len(pieces)

    def advance(which):
        for i in which:
            if progress[i] < nhops:
                held = holds[i][0] if progress[i] == 0 else jnp.concatenate(holds[i])
                holds[i] = [held, share_hop(held, progress[i])]
                progress[i] += 1

    local = call(
        functools.partial(local_kernel, nheads, width),
        jax.ShapeDtypeStruct((2 * rows, span), F32),
        6 * span * span * rows, 16 * span * rows,
        decay, query_act, key_act, value_act, grad_output,
    )
    hop, enter = 1, None
    while True:
        if 2 * hop >= nseq:
            early = range(min(2, len(holds)))
            sent, *firsts = gate([sent] + [holds[i][0] for i in early], [local])
            for i in early:
                holds[i][0] = firsts[i]
            advance(early)
        got = lax.ppermute(sent, "seq", [(i, i ^ hop) for i in range(nseq)])
        if 2 * hop >= nseq:
            break
        final_next = 4 * hop >= nseq
        out_shape = (
            jax.ShapeDtypeStruct((rows if final_next else 2 * rows + 16, width), BF16),
            jax.ShapeDtypeStruct((2 * rows, width), F32),
            jax.ShapeDtypeStruct((24, width), F32),
            jax.ShapeDtypeStruct((2 * rows, width), F32),
        )
        args = [got, held, logs] + ([] if enter is None else [enter])
        sent, held, logs, enter = call(
            functools.partial(step_kernel, nheads, width, hop, enter is None, final_next),
            out_shape, 10 * rows * width, 16 * rows * width, *args,
        )
        hop *= 2
    both = call(
        functools.partial(carry_kernel, nheads, width, hop),
        jax.ShapeDtypeStruct((2 * rows, span), BF16),
        4 * span * rows * width, 16 * span * rows,
        decay, value_act, grad_output, got, logs, enter, local,
    )

    even, odd = share_deltas(nseq)
    deltas = jnp.where(my_seq % 2 == 1, jnp.array(odd, jnp.int32), jnp.array(even, jnp.int32))
    table = jnp.concatenate([(my_head >= 2).astype(jnp.int32)[None], deltas ^ my_seq])
    total = own_product(w_query, w_key, both, chunk)

    if nhead == 4 and nhops == 3:
        p1 = lax.ppermute(both, "head", ring[1])
        p3 = lax.ppermute(both, "head", ring[3])
        if EARLYC:
            holds[0][1], holds[1][1], holds[2][0] = gate([holds[0][1], holds[1][1], holds[2][0]], [both])
        else:
            holds[0][1], holds[1][1] = gate([holds[0][1], holds[1][1]], [both])
        advance([0, 1])
        if not EARLYC:
            (holds[2][0],) = gate([holds[2][0]], [holds[0][0], holds[1][0]])
        advance([2])
        holds[0][1], holds[1][1], holds[2][1], p1, p3 = gate(
            [holds[0][1], holds[1][1], holds[2][1], p1, p3], [total]
        )
        advance([0, 1, 2])
        up = lax.ppermute(p1, "head", [(1, 2), (2, 3)])
        down = lax.ppermute(p3, "head", [(2, 1), (1, 0)])
        total = add_product(table, total, [(holds[0], (p1,)), (holds[1], (p3,))], False)
        holds[2][1], up, down = gate([holds[2][1], up, down], [total])
        near, far = holds[2]
        blocks = [near, far] + [share_hop(x, 2) for x in (near, far)]
        return add_product(table, total, [(blocks, (down, up))], True)

    gathered = lax.all_gather(both, "head")
    while min(progress) < nhops:
        advance(range(len(pieces)))
    for i, k in enumerate(shifts):
        grads = gathered[(my_head + nhead - k) % nhead]
        total = add_product(table, total, [(holds[i], (grads,))], i == nhead - 2)
    return total


def solution(mesh):
    placed = (
        P("seq", "head"),
        P("seq", "head"),
        P("seq", "head"),
        P("seq", "head"),
        P("seq", "head"),
        P(None, "head"),
        P(None, "head"),
    )
    return jax.shard_map(
        shards, mesh=mesh, in_specs=placed, out_specs=P("head", "seq"), check_vma=False
    )
```

```python
import functools

import jax
import jax.numpy as jnp
from jax import lax
from jax.experimental import pallas as pl
from jax.experimental.pallas import tpu as pltpu
from jax.sharding import PartitionSpec as P

F32 = jnp.float32
BF16 = jnp.bfloat16
VMEM_BYTES = 16 * 1024 * 1024
CUT = 592
HOP = 624
FAR = 1152


def contract(a, b, left, right):
    return lax.dot_general(a, b, (((left,), (right,)), ((), ())), preferred_element_type=F32)


def call(kernel, out_shape, flops, nbytes, *args, aliases=None, vmem=VMEM_BYTES, **spec):
    return pl.pallas_call(
        kernel,
        out_shape=out_shape,
        cost_estimate=pl.CostEstimate(flops=flops, bytes_accessed=nbytes, transcendentals=0),
        compiler_params=pltpu.CompilerParams(vmem_limit_bytes=vmem),
        input_output_aliases=aliases or {},
        **spec,
    )(*args)


def gate_kernel(count, *refs):
    del count, refs


def gate(passed, tokens=(), flops=0):
    return call(
        functools.partial(gate_kernel, len(passed)),
        [jax.ShapeDtypeStruct(x.shape, x.dtype) for x in passed],
        flops, 0, *passed, *tokens,
        aliases={i: i for i in range(len(passed))},
        in_specs=[pl.BlockSpec(memory_space=pl.ANY)] * (len(passed) + len(tokens)),
        out_specs=[pl.BlockSpec(memory_space=pl.ANY)] * len(passed),
    )


def thirds(x):
    high = x.astype(BF16)
    rest = x - high.astype(F32)
    middle = rest.astype(BF16)
    return high, middle, (rest - middle.astype(F32)).astype(BF16)


def triangle(span):
    rows = lax.broadcasted_iota(jnp.int32, (span, span), 0)
    cols = lax.broadcasted_iota(jnp.int32, (span, span), 1)
    return rows >= cols


def upper_half(hop):
    return ((lax.axis_index("seq") // hop) % 2).astype(F32)


def states_kernel(nheads, width, decay_ref, q_ref, k_ref, v_ref, g_ref, token_ref, sent_ref, held_ref, logs_ref):
    span = q_ref.shape[0]
    tri = triangle(span).astype(F32).astype(BF16)
    cum = sum(contract(tri, part, 1, 1) for part in thirds(decay_ref[...]))
    rows = nheads * width
    row = lax.broadcasted_iota(jnp.int32, (8, width), 0)
    totals = jnp.zeros((8, width), F32)
    for h in range(nheads):
        cols = slice(h * width, (h + 1) * width)
        cum_h = cum[:, h : h + 1]
        last = cum[span - 1 : span, h : h + 1]
        key_w = (k_ref[:, cols].astype(F32) * jnp.exp(last - cum_h)).astype(BF16)
        query_w = (q_ref[:, cols].astype(F32) * jnp.exp(cum_h)).astype(BF16)
        state = contract(key_w, v_ref[:, cols], 0, 0)
        grad = contract(query_w, g_ref[:, cols], 0, 0)
        held_ref[h * width : (h + 1) * width, :] = state
        held_ref[rows + h * width : rows + (h + 1) * width, :] = grad
        sent_ref[h * width : (h + 1) * width, :] = state.astype(BF16)
        sent_ref[rows + h * width : rows + (h + 1) * width, :] = grad.astype(BF16)
        totals = jnp.where(row == h, jnp.broadcast_to(last, (8, width)), totals)
    high = totals.astype(BF16).astype(F32)
    sent_ref[2 * rows :, :] = jnp.concatenate([high, totals - high]).astype(BF16)
    logs_ref[0:8, :] = totals
    logs_ref[8:24, :] = jnp.zeros((16, width), F32)


def step_kernel(nheads, width, hop, first, final_next, got_ref, held_ref, logs_ref, *refs):
    if first:
        sent_ref, held_out, logs_out, enter_out = refs
    else:
        enter_ref, sent_ref, held_out, logs_out, enter_out = refs
    rows = nheads * width
    up = upper_half(hop)
    low = 1.0 - up
    tail = got_ref[2 * rows :, :].astype(F32)
    got_total = tail[0:8] + tail[8:16]
    total, before, after = logs_ref[0:8, :], logs_ref[8:16, :], logs_ref[16:24, :]
    own_decay, got_decay = jnp.exp(total), jnp.exp(got_total)
    from_before, from_after = up * jnp.exp(before), low * jnp.exp(after)
    total = total + got_total
    logs_out[0:8, :] = total
    logs_out[8:16, :] = before + up * got_total
    logs_out[16:24, :] = after + low * got_total
    if final_next:
        next_up = upper_half(2 * hop) > 0.5
    else:
        high = total.astype(BF16).astype(F32)
        sent_ref[2 * rows :, :] = jnp.concatenate([high, total - high]).astype(BF16)
    for h in range(nheads):
        one = slice(h * width, (h + 1) * width)
        two = slice(rows + h * width, rows + (h + 1) * width)
        got_state, got_grad = got_ref[one, :].astype(F32), got_ref[two, :].astype(F32)
        own, got = own_decay[h : h + 1, :], got_decay[h : h + 1, :]
        state = (up + low * got) * held_ref[one, :] + (up * own + low) * got_state
        grad = (low + up * got) * held_ref[two, :] + (low * own + up) * got_grad
        state_in = from_before[h : h + 1, :] * got_state
        grad_in = from_after[h : h + 1, :] * got_grad
        if not first:
            state_in = enter_ref[one, :] + state_in
            grad_in = enter_ref[two, :] + grad_in
        enter_out[one, :] = state_in
        enter_out[two, :] = grad_in
        held_out[one, :] = state
        held_out[two, :] = grad
        if final_next:
            sent_ref[one, :] = jnp.where(next_up, grad, state).astype(BF16)
        else:
            sent_ref[one, :] = state.astype(BF16)
            sent_ref[two, :] = grad.astype(BF16)


def local_kernel(nheads, width, decay_ref, q_ref, k_ref, v_ref, g_ref, out_ref):
    span = q_ref.shape[0]
    rows = nheads * width
    causal = triangle(span)
    tri = causal.astype(F32).astype(BF16)
    parts = thirds(decay_ref[...])
    cum = sum(contract(tri, part, 1, 1) for part in parts)
    cum_rows = sum(contract(part, tri, 1, 1) for part in parts)
    for h in range(nheads):
        cols = slice(h * width, (h + 1) * width)
        gap = cum[:, h : h + 1] - cum_rows[h : h + 1, :]
        decay = jnp.where(causal, jnp.exp(jnp.minimum(gap, 0.0)), 0.0)
        weighted = (contract(g_ref[:, cols], v_ref[:, cols], 1, 1) * decay).astype(BF16)
        out_ref[h * width : (h + 1) * width, :] = contract(k_ref[:, cols], weighted, 0, 1)
        out_ref[rows + h * width : rows + (h + 1) * width, :] = contract(
            q_ref[:, cols], weighted, 0, 0
        )


def carry_kernel(nheads, width, hop, decay_ref, v_ref, g_ref, got_ref, logs_ref, enter_ref, local_ref, out_ref):
    span = v_ref.shape[0]
    rows = nheads * width
    tri = triangle(span).astype(F32).astype(BF16)
    cum_rows = sum(contract(part, tri, 1, 1) for part in thirds(decay_ref[...]))
    up = upper_half(hop)
    low = 1.0 - up
    from_before = up * jnp.exp(logs_ref[8:16, :])
    from_after = low * jnp.exp(logs_ref[16:24, :])
    for h in range(nheads):
        cols = slice(h * width, (h + 1) * width)
        two = slice(rows + h * width, rows + (h + 1) * width)
        got = got_ref[cols, :].astype(F32)
        state_in = (enter_ref[cols, :] + from_before[h : h + 1, :] * got).astype(BF16)
        grad_in = (enter_ref[two, :] + from_after[h : h + 1, :] * got).astype(BF16)
        cum_h = cum_rows[h : h + 1, :]
        last = cum_h[:, span - 1 : span]
        dq = local_ref[cols, :] + contract(state_in, g_ref[:, cols], 1, 1) * jnp.exp(cum_h)
        dk = local_ref[two, :] + contract(grad_in, v_ref[:, cols], 1, 1) * jnp.exp(last - cum_h)
        out_ref[cols, :] = dq.astype(BF16)
        out_ref[two, :] = dk.astype(BF16)


def share_order(count):
    bits = []
    hop = 2
    while hop < count:
        bits.append(hop)
        hop *= 2
    return bits, bits[::-1]


def share_hop(held, number):
    count = lax.axis_size("seq")
    even, odd = share_order(count)
    even, odd = even + [1], odd + [1]
    pairs = [(i, i ^ (odd[number] if i % 2 else even[number])) for i in range(count)]
    return lax.ppermute(held, "seq", pairs)


def share_deltas(count):
    even, odd = share_order(count)

    def spread(order):
        out = [0]
        for hop in order:
            out = out + [d ^ hop for d in out]
        return out

    return tuple(
        spread(first) + [d ^ 1 for d in spread(second)] for first, second in ((even, odd), (odd, even))
    )


def pack_kernel(share, plan, wq_ref, wk_ref, *refs):
    count, nseq = lax.axis_size("head"), lax.axis_size("seq")
    mine, my_seq = lax.axis_index("head"), lax.axis_index("seq")
    odd = lax.rem(my_seq, 2)
    outs, sems = refs[: len(plan)], refs[len(plan)]
    copies = []
    for i, (even_shift, odd_shift, many) in enumerate(plan):
        shift = even_shift + odd * (odd_shift - even_shift)
        block = lax.rem(mine + shift, count) * nseq + my_seq // many * many
        rows = pl.ds(pl.multiple_of(block * share, 16), many * share)
        for j, src in enumerate((wq_ref, wk_ref)):
            copies.append(
                pltpu.make_async_copy(
                    src.at[rows, :], outs[i].at[pl.ds(j * many * share, many * share), :], sems.at[i, j]
                )
            )
    for copy in copies:
        copy.start()
    for copy in copies:
        copy.wait()


def pack_weights(w_query, w_key, plan, share, pad=0):
    wide = w_query.shape[1]
    if share % 16:
        count, nseq = lax.axis_size("head"), lax.axis_size("seq")
        mine, my_seq = lax.axis_index("head"), lax.axis_index("seq")
        out = []
        for even_shift, odd_shift, many in plan:
            shift = jnp.where(my_seq % 2 == 1, odd_shift, even_shift)
            start = ((mine + shift) % count * nseq + my_seq // many * many) * share
            out.append(
                jnp.concatenate(
                    [lax.dynamic_slice_in_dim(w, start, many * share, 0) for w in (w_query, w_key)]
                )
            )
        return out
    heights = [2 * many * share for _, _, many in plan]
    heights[-1] += pad
    return call(
        functools.partial(pack_kernel, share, tuple(plan)),
        [jax.ShapeDtypeStruct((height, wide), BF16) for height in heights],
        0, sum(heights) * wide * 4,
        *(pltpu.with_memory_space_constraint(w, pltpu.HBM) for w in (w_query, w_key)),
        in_specs=[pl.BlockSpec(memory_space=pl.ANY)] * 2,
        out_specs=[pl.BlockSpec(memory_space=pltpu.VMEM)] * len(plan),
        scratch_shapes=[pltpu.SemaphoreType.DMA((len(plan), 2))],
    )


def join_kernel(groups, nargs, *refs):
    for group, out_ref in zip(groups, refs[-len(groups) :]):
        at = 0
        for i, start, size in group:
            out_ref[at : at + size, :] = refs[i][start : start + size, :]
            at += size


def join(*groups, tokens=()):
    args, spec = [], []
    for group in groups:
        spec.append(tuple((place_in(args, x), start, size) for x, start, size in group))
    return call(
        functools.partial(join_kernel, tuple(spec), len(args)),
        [jax.ShapeDtypeStruct((sum(size for _, _, size in group), args[0].shape[1]), BF16) for group in spec],
        0, 0, *args, *tokens,
        in_specs=[pl.BlockSpec(memory_space=pltpu.VMEM)] * len(args)
        + [pl.BlockSpec(memory_space=pl.ANY)] * len(tokens),
        out_specs=[pl.BlockSpec(memory_space=pltpu.VMEM)] * len(groups),
    )


def place_in(args, x):
    for i, y in enumerate(args):
        if y is x:
            return i
    args.append(x)
    return len(args) - 1


def rows_of(refs, low, high):
    parts, at = [], 0
    for ref in refs:
        first, last = max(low, at), min(high, at + ref.shape[0])
        if first < last:
            parts.append(ref[first - at : last - at, :])
        at += ref.shape[0]
    return parts[0] if len(parts) == 1 else jnp.concatenate(parts)


def row_block(weights, grads):
    share, wide = weights.shape[0] // 2, weights.shape[1]
    return contract(weights[:share], grads[:wide], 1, 0) + contract(weights[share:], grads[wide:], 1, 0)


def own_kernel(wq_ref, wk_ref, grads_ref, out_ref, near_q, near_k, sems):
    chunk, wide = near_q.shape
    rows = pl.ds(pl.multiple_of(lax.axis_index("head") * chunk, 16), chunk)
    copies = [
        pltpu.make_async_copy(src.at[rows, :], dst, sems.at[i])
        for i, (src, dst) in enumerate(((wq_ref, near_q), (wk_ref, near_k)))
    ]
    for copy in copies:
        copy.start()
    for copy in copies:
        copy.wait()
    out_ref[...] = contract(near_q[...], grads_ref[:wide, :], 1, 0) + contract(
        near_k[...], grads_ref[wide:, :], 1, 0
    )


def own_product(w_query, w_key, grads, chunk):
    wide = w_query.shape[1]
    return call(
        own_kernel, jax.ShapeDtypeStruct((chunk, grads.shape[1]), F32),
        4 * chunk * grads.shape[1] * wide, chunk * wide * 4,
        *(pltpu.with_memory_space_constraint(w, pltpu.HBM) for w in (w_query, w_key)), grads,
        in_specs=[pl.BlockSpec(memory_space=pl.ANY)] * 2 + [pl.BlockSpec(memory_space=pltpu.VMEM)],
        out_specs=pl.BlockSpec(memory_space=pltpu.VMEM),
        scratch_shapes=[pltpu.VMEM((chunk, wide), BF16)] * 2 + [pltpu.SemaphoreType.DMA((2,))],
    )


def relay_kernel(own_ref, lower_ref, upper_ref, token_ref, relay_ref, kept_ref, sent_ref):
    mine, odd = lax.axis_index("head"), lax.rem(lax.axis_index("seq"), 2)

    @pl.when(mine == 1)
    def _():
        relay_ref[...] = upper_ref[...]

    @pl.when(mine == 2)
    def _():
        relay_ref[...] = lower_ref[...]

    @pl.when((mine != 1) & (mine != 2))
    def _():
        relay_ref[...] = own_ref[...]

    @pl.when(odd == 0)
    def _():
        kept_ref[...] = lower_ref[...]
        sent_ref[...] = upper_ref[...]

    @pl.when(odd == 1)
    def _():
        kept_ref[...] = upper_ref[...]
        sent_ref[...] = lower_ref[...]


def split_kernel(both_ref, token_ref, theirs_ref):
    odd = lax.rem(lax.axis_index("seq"), 2)
    share = theirs_ref.shape[0] // 2
    for parity in range(2):

        @pl.when(odd == parity)
        def _():
            for j in range(2):
                at = (2 * j + 1 - parity) * share
                theirs_ref[j * share : (j + 1) * share, :] = both_ref[at : at + share, :]


def pick_kernel(both_ref, got_ref, out_ref):
    odd = lax.rem(lax.axis_index("seq"), 2)
    upper = lax.axis_index("head") // 2
    share = out_ref.shape[0] // 2

    @pl.when(odd + upper != 1)
    def _():
        out_ref[...] = got_ref[...]

    for parity in range(2):

        @pl.when((odd == parity) & (upper == 1 - parity))
        def _():
            for j in range(2):
                at = (2 * j + parity) * share
                out_ref[j * share : (j + 1) * share, :] = both_ref[at : at + share, :]


def pair_kernel(table_ref, total_ref, *refs):
    weights, (kept_ref, got_ref, out_ref, sent_ref) = refs[:-4], refs[-4:]
    nblocks = table_ref.shape[0]
    size = out_ref.shape[0] // nblocks
    for j in range(nblocks):
        block = rows_of(weights, 2 * size * j, 2 * size * (j + 1))
        rows = pl.ds(pl.multiple_of(table_ref[j] * size, 16), size)
        out_ref[rows, :] = total_ref[rows, :] + row_block(block, kept_ref[...])
        sent_ref[rows, :] = row_block(block, got_ref[...]).astype(BF16)


def pair_product(table, total, weights, kept, got):
    chunk, span = total.shape
    return call(
        pair_kernel,
        (jax.ShapeDtypeStruct((chunk, span), F32), jax.ShapeDtypeStruct((chunk, span), BF16)),
        4 * chunk * span * kept.shape[0], chunk * span * 10,
        table, total, *weights, kept, got,
        in_specs=[pl.BlockSpec(memory_space=pltpu.SMEM)]
        + [pl.BlockSpec(memory_space=pltpu.VMEM)] * (3 + len(weights)),
        out_specs=[pl.BlockSpec(memory_space=pltpu.VMEM)] * 2,
        vmem=24 * 1024 * 1024,
    )


def add_kernel(terms, plus, table_ref, total_ref, *refs):
    args, out_ref = refs[:-1], refs[-1]
    nshares = table_ref.shape[0]
    share = out_ref.shape[0] // nshares
    for j in range(nshares):
        rows = pl.ds(pl.multiple_of(table_ref[j] * share, 8), share)
        total = total_ref[rows, :]
        if plus is not None:
            total = total + args[plus][rows, :].astype(F32)
        for blocks, grads in terms:
            weights = rows_of([args[i] for i in blocks], 2 * share * j, 2 * share * (j + 1))
            total = total + row_block(weights, args[grads][...])
        out_ref[rows, :] = total.astype(out_ref.dtype)


def add_product(table, total, terms, last, plus=None):
    chunk, span = total.shape
    args = []

    spec = tuple(
        (tuple(place_in(args, x) for x in blocks), place_in(args, grads))
        for blocks, grads in terms
    )
    plus = None if plus is None else place_in(args, plus)
    return call(
        functools.partial(add_kernel, spec, plus),
        jax.ShapeDtypeStruct((chunk, span), BF16 if last else F32),
        2 * len(terms) * chunk * span * terms[0][1].shape[0], chunk * span * 8,
        table, total, *args,
        in_specs=[pl.BlockSpec(memory_space=pltpu.SMEM)]
        + [pl.BlockSpec(memory_space=pltpu.VMEM)] * (1 + len(args)),
        out_specs=pl.BlockSpec(memory_space=pltpu.VMEM),
        vmem=24 * 1024 * 1024,
    )


def shards(query_act, key_act, value_act, grad_output, log_decay, w_query, w_key):
    span = query_act.shape[0]
    nheads = log_decay.shape[1]
    width = query_act.shape[1] // nheads
    nseq, nhead = lax.axis_size("seq"), lax.axis_size("head")
    my_seq, my_head = lax.axis_index("seq"), lax.axis_index("head")
    chunk = w_query.shape[0] // nhead
    share = chunk // nseq
    rows = nheads * width

    shifts = [1, nhead - 1] + list(range(2, nhead - 1))
    ring = {k: [(i, (i + k) % nhead) for i in range(nhead)] for k in shifts}
    fast = nhead == 4 and nseq == 8
    if fast:
        packed = pack_weights(w_query, w_key, [(1, 3, 2), (2, 2, 2)], share)

        def moves(even, odd):
            return [
                (i * nhead + j, i * nhead + k) for i in range(nseq) for j, k in (odd if i % 2 else even)
            ]

        axes = ("seq", "head")
        first = lax.ppermute(packed[0], axes, moves(ring[1], ring[3]))
        passing = lax.ppermute(packed[1], axes, moves([(0, 1), (1, 2)], [(3, 2), (2, 1)]))
    else:
        packed = pack_weights(w_query, w_key, [(k, k, 1) for k in shifts], share)
        pieces = [lax.ppermute(p, "head", ring[k]) for p, k in zip(packed, shifts)]

    decay = log_decay.T
    sent, held, logs = call(
        functools.partial(states_kernel, nheads, width),
        (
            jax.ShapeDtypeStruct((2 * rows + 16, width), BF16),
            jax.ShapeDtypeStruct((2 * rows, width), F32),
            jax.ShapeDtypeStruct((24, width), F32),
        ),
        4 * span * rows * width, 8 * span * rows,
        decay, query_act, key_act, value_act, grad_output, packed[0],
        in_specs=[pl.BlockSpec(memory_space=pltpu.VMEM)] * 5 + [pl.BlockSpec(memory_space=pl.ANY)],
    )
    local = call(
        functools.partial(local_kernel, nheads, width),
        jax.ShapeDtypeStruct((2 * rows, span), F32),
        6 * span * span * rows, 16 * span * rows,
        decay, query_act, key_act, value_act, grad_output,
    )
    hop, enter = 1, None
    while True:
        got = lax.ppermute(sent, "seq", [(i, i ^ hop) for i in range(nseq)])
        if 2 * hop >= nseq:
            break
        final_next = 4 * hop >= nseq
        out_shape = (
            jax.ShapeDtypeStruct((rows if final_next else 2 * rows + 16, width), BF16),
            jax.ShapeDtypeStruct((2 * rows, width), F32),
            jax.ShapeDtypeStruct((24, width), F32),
            jax.ShapeDtypeStruct((2 * rows, width), F32),
        )
        args = [got, held, logs] + ([] if enter is None else [enter])
        sent, held, logs, enter = call(
            functools.partial(step_kernel, nheads, width, hop, enter is None, final_next),
            out_shape, 10 * rows * width, 16 * rows * width, *args,
        )
        hop *= 2
    both = call(
        functools.partial(carry_kernel, nheads, width, hop),
        jax.ShapeDtypeStruct((2 * rows, span), BF16),
        4 * span * rows * width, 16 * span * rows,
        decay, value_act, grad_output, got, logs, enter, local,
    )

    even, odd = share_deltas(nseq)
    deltas = jnp.where(my_seq % 2 == 1, jnp.array(odd, jnp.int32), jnp.array(even, jnp.int32))
    table = deltas ^ my_seq
    total = own_product(w_query, w_key, both, chunk)

    if fast:
        p1 = lax.ppermute(both, "head", ring[1])
        p3 = lax.ppermute(both, "head", ring[3])
        one, two, cut = 2 * share, 4 * share, CUT
        (first,) = gate([first], [both])
        second = share_hop(first, 0)
        sent = join(
            ((first, 0, two), (second, 0, FAR - two)), ((second, FAR - two, 2 * two - FAR),),
        )
        blocks = [first, second] + [share_hop(x, 1) for x in sent]
        (passing,) = gate([passing], [first])
        passing = lax.ppermute(passing, axes, moves([(1, 2), (2, 3)], [(2, 1), (1, 0)]))
        theirs = call(
            split_kernel, jax.ShapeDtypeStruct((one, passing.shape[1]), BF16), 0, 0, passing, total,
            in_specs=[pl.BlockSpec(memory_space=pltpu.VMEM), pl.BlockSpec(memory_space=pl.ANY)],
            out_specs=pl.BlockSpec(memory_space=pltpu.VMEM),
        )
        theirs = lax.ppermute(
            theirs, axes,
            [(i * nhead + j, (i ^ 1) * nhead + j) for i in range(nseq) for j in range(nhead) if (j < 2) == (i % 2)],
        )
        third = call(
            pick_kernel, jax.ShapeDtypeStruct(theirs.shape, BF16), 0, 0, passing, theirs,
            in_specs=[pl.BlockSpec(memory_space=pltpu.VMEM)] * 2,
            out_specs=pl.BlockSpec(memory_space=pltpu.VMEM),
        )
        fourth = share_hop(third, 0)
        near, head_rows, tail_rows = join(
            ((third, 0, one), (fourth, 0, one)),
            ((third, 0, one), (fourth, 0, cut - one)),
            ((fourth, cut - one, two - cut),),
        )
        far = [share_hop(x, 1) for x in (head_rows, tail_rows)]
        relay, kept, handed = call(
            relay_kernel, [jax.ShapeDtypeStruct(both.shape, BF16)] * 3, 0, 0, both, p1, p3, total,
            in_specs=[pl.BlockSpec(memory_space=pltpu.VMEM)] * 3 + [pl.BlockSpec(memory_space=pl.ANY)],
            out_specs=[pl.BlockSpec(memory_space=pltpu.VMEM)] * 3,
        )
        p2 = lax.ppermute(relay, "head", [(0, 2), (1, 0), (2, 3), (3, 1)])
        got = share_hop(handed, 2)
        total, handed = pair_product(table[: nseq // 2] // 2, total, blocks, kept, got)
        got = share_hop(handed, 2)
        far, far_head, far_tail = join(
            ((far[0], 0, cut), (far[1], 0, two - cut)),
            ((far[0], 0, cut), (far[1], 0, HOP - cut)),
            ((far[1], HOP - cut, two - HOP),),
            tokens=[p2, total],
        )
        term = (near, far, *(share_hop(x, 2) for x in (near, far_head, far_tail)))
        return add_product(table, total, [(term, p2)], True, got)

    gathered = lax.all_gather(both, "head")
    for i, k in enumerate(shifts):
        held = [pieces[i]]
        for number in range(len(share_order(nseq)[0]) + 1):
            whole = held[0] if number == 0 else jnp.concatenate(held)
            held = [whole, share_hop(whole, number)]
        grads = gathered[(my_head + nhead - k) % nhead]
        total = add_product(table, total, [(held, grads)], i == nhead - 2)
    return total


def solution(mesh):
    placed = (
        P("seq", "head"),
        P("seq", "head"),
        P("seq", "head"),
        P("seq", "head"),
        P("seq", "head"),
        P(None, "head"),
        P(None, "head"),
    )
    return jax.shard_map(
        shards, mesh=mesh, in_specs=placed, out_specs=P("head", "seq"), check_vma=False
    )
```

```python
import functools

import jax
import jax.numpy as jnp
from jax import lax
from jax.experimental import pallas as pl
from jax.experimental.pallas import tpu as pltpu
from jax.sharding import PartitionSpec as P

F32 = jnp.float32
BF16 = jnp.bfloat16
VMEM_BYTES = 16 * 1024 * 1024
CUT = 144
SPLIT = 1152


def contract(a, b, left, right):
    return lax.dot_general(a, b, (((left,), (right,)), ((), ())), preferred_element_type=F32)


def call(kernel, out_shape, flops, nbytes, *args, aliases=None, vmem=VMEM_BYTES, **spec):
    return pl.pallas_call(
        kernel,
        out_shape=out_shape,
        cost_estimate=pl.CostEstimate(flops=flops, bytes_accessed=nbytes, transcendentals=0),
        compiler_params=pltpu.CompilerParams(vmem_limit_bytes=vmem),
        input_output_aliases=aliases or {},
        **spec,
    )(*args)


def gate_kernel(count, *refs):
    del count, refs


def gate(passed, tokens=(), flops=0):
    return call(
        functools.partial(gate_kernel, len(passed)),
        [jax.ShapeDtypeStruct(x.shape, x.dtype) for x in passed],
        flops, 0, *passed, *tokens,
        aliases={i: i for i in range(len(passed))},
        in_specs=[pl.BlockSpec(memory_space=pl.ANY)] * (len(passed) + len(tokens)),
        out_specs=[pl.BlockSpec(memory_space=pl.ANY)] * len(passed),
    )


def thirds(x):
    high = x.astype(BF16)
    rest = x - high.astype(F32)
    middle = rest.astype(BF16)
    return high, middle, (rest - middle.astype(F32)).astype(BF16)


def triangle(span):
    rows = lax.broadcasted_iota(jnp.int32, (span, span), 0)
    cols = lax.broadcasted_iota(jnp.int32, (span, span), 1)
    return rows >= cols


def upper_half(hop):
    return ((lax.axis_index("seq") // hop) % 2).astype(F32)


def states_kernel(nheads, width, decay_ref, q_ref, k_ref, v_ref, g_ref, token_ref, sent_ref, held_ref, logs_ref):
    span = q_ref.shape[0]
    tri = triangle(span).astype(F32).astype(BF16)
    cum = sum(contract(tri, part, 1, 1) for part in thirds(decay_ref[...]))
    rows = nheads * width
    row = lax.broadcasted_iota(jnp.int32, (8, width), 0)
    totals = jnp.zeros((8, width), F32)
    for h in range(nheads):
        cols = slice(h * width, (h + 1) * width)
        cum_h = cum[:, h : h + 1]
        last = cum[span - 1 : span, h : h + 1]
        key_w = (k_ref[:, cols].astype(F32) * jnp.exp(last - cum_h)).astype(BF16)
        query_w = (q_ref[:, cols].astype(F32) * jnp.exp(cum_h)).astype(BF16)
        state = contract(key_w, v_ref[:, cols], 0, 0)
        grad = contract(query_w, g_ref[:, cols], 0, 0)
        held_ref[h * width : (h + 1) * width, :] = state
        held_ref[rows + h * width : rows + (h + 1) * width, :] = grad
        sent_ref[h * width : (h + 1) * width, :] = state.astype(BF16)
        sent_ref[rows + h * width : rows + (h + 1) * width, :] = grad.astype(BF16)
        totals = jnp.where(row == h, jnp.broadcast_to(last, (8, width)), totals)
    high = totals.astype(BF16).astype(F32)
    sent_ref[2 * rows :, :] = jnp.concatenate([high, totals - high]).astype(BF16)
    logs_ref[0:8, :] = totals
    logs_ref[8:24, :] = jnp.zeros((16, width), F32)


def step_kernel(nheads, width, hop, first, final_next, got_ref, held_ref, logs_ref, *refs):
    if first:
        sent_ref, held_out, logs_out, enter_out = refs
    else:
        enter_ref, sent_ref, held_out, logs_out, enter_out = refs
    rows = nheads * width
    up = upper_half(hop)
    low = 1.0 - up
    tail = got_ref[2 * rows :, :].astype(F32)
    got_total = tail[0:8] + tail[8:16]
    total, before, after = logs_ref[0:8, :], logs_ref[8:16, :], logs_ref[16:24, :]
    own_decay, got_decay = jnp.exp(total), jnp.exp(got_total)
    from_before, from_after = up * jnp.exp(before), low * jnp.exp(after)
    total = total + got_total
    logs_out[0:8, :] = total
    logs_out[8:16, :] = before + up * got_total
    logs_out[16:24, :] = after + low * got_total
    if final_next:
        next_up = upper_half(2 * hop) > 0.5
    else:
        high = total.astype(BF16).astype(F32)
        sent_ref[2 * rows :, :] = jnp.concatenate([high, total - high]).astype(BF16)
    for h in range(nheads):
        one = slice(h * width, (h + 1) * width)
        two = slice(rows + h * width, rows + (h + 1) * width)
        got_state, got_grad = got_ref[one, :].astype(F32), got_ref[two, :].astype(F32)
        own, got = own_decay[h : h + 1, :], got_decay[h : h + 1, :]
        state = (up + low * got) * held_ref[one, :] + (up * own + low) * got_state
        grad = (low + up * got) * held_ref[two, :] + (low * own + up) * got_grad
        state_in = from_before[h : h + 1, :] * got_state
        grad_in = from_after[h : h + 1, :] * got_grad
        if not first:
            state_in = enter_ref[one, :] + state_in
            grad_in = enter_ref[two, :] + grad_in
        enter_out[one, :] = state_in
        enter_out[two, :] = grad_in
        held_out[one, :] = state
        held_out[two, :] = grad
        if final_next:
            sent_ref[one, :] = jnp.where(next_up, grad, state).astype(BF16)
        else:
            sent_ref[one, :] = state.astype(BF16)
            sent_ref[two, :] = grad.astype(BF16)


def local_kernel(nheads, width, decay_ref, q_ref, k_ref, v_ref, g_ref, out_ref):
    span = q_ref.shape[0]
    rows = nheads * width
    causal = triangle(span)
    tri = causal.astype(F32).astype(BF16)
    parts = thirds(decay_ref[...])
    cum = sum(contract(tri, part, 1, 1) for part in parts)
    cum_rows = sum(contract(part, tri, 1, 1) for part in parts)
    for h in range(nheads):
        cols = slice(h * width, (h + 1) * width)
        gap = cum[:, h : h + 1] - cum_rows[h : h + 1, :]
        decay = jnp.where(causal, jnp.exp(jnp.minimum(gap, 0.0)), 0.0)
        weighted = (contract(g_ref[:, cols], v_ref[:, cols], 1, 1) * decay).astype(BF16)
        out_ref[h * width : (h + 1) * width, :] = contract(k_ref[:, cols], weighted, 0, 1)
        out_ref[rows + h * width : rows + (h + 1) * width, :] = contract(
            q_ref[:, cols], weighted, 0, 0
        )


def carry_kernel(nheads, width, hop, decay_ref, v_ref, g_ref, got_ref, logs_ref, enter_ref, local_ref, out_ref):
    span = v_ref.shape[0]
    rows = nheads * width
    tri = triangle(span).astype(F32).astype(BF16)
    cum_rows = sum(contract(part, tri, 1, 1) for part in thirds(decay_ref[...]))
    up = upper_half(hop)
    low = 1.0 - up
    from_before = up * jnp.exp(logs_ref[8:16, :])
    from_after = low * jnp.exp(logs_ref[16:24, :])
    for h in range(nheads):
        cols = slice(h * width, (h + 1) * width)
        two = slice(rows + h * width, rows + (h + 1) * width)
        got = got_ref[cols, :].astype(F32)
        state_in = (enter_ref[cols, :] + from_before[h : h + 1, :] * got).astype(BF16)
        grad_in = (enter_ref[two, :] + from_after[h : h + 1, :] * got).astype(BF16)
        cum_h = cum_rows[h : h + 1, :]
        last = cum_h[:, span - 1 : span]
        dq = local_ref[cols, :] + contract(state_in, g_ref[:, cols], 1, 1) * jnp.exp(cum_h)
        dk = local_ref[two, :] + contract(grad_in, v_ref[:, cols], 1, 1) * jnp.exp(last - cum_h)
        out_ref[cols, :] = dq.astype(BF16)
        out_ref[two, :] = dk.astype(BF16)


def share_order(count):
    bits = []
    hop = 2
    while hop < count:
        bits.append(hop)
        hop *= 2
    return bits, bits[::-1]


def share_hop(held, number):
    count = lax.axis_size("seq")
    even, odd = share_order(count)
    even, odd = even + [1], odd + [1]
    pairs = [(i, i ^ (odd[number] if i % 2 else even[number])) for i in range(count)]
    return lax.ppermute(held, "seq", pairs)


def share_deltas(count):
    even, odd = share_order(count)

    def spread(order):
        out = [0]
        for hop in order:
            out = out + [d ^ hop for d in out]
        return out

    return tuple(
        spread(first) + [d ^ 1 for d in spread(second)] for first, second in ((even, odd), (odd, even))
    )


def pack_kernel(share, plan, wq_ref, wk_ref, *refs):
    count, nseq = lax.axis_size("head"), lax.axis_size("seq")
    mine, my_seq = lax.axis_index("head"), lax.axis_index("seq")
    odd = lax.rem(my_seq, 2)
    outs, sems = refs[: len(plan)], refs[len(plan)]
    copies = []
    for i, (even_shift, odd_shift, many) in enumerate(plan):
        shift = even_shift + odd * (odd_shift - even_shift)
        block = lax.rem(mine + shift, count) * nseq + my_seq // many * many
        rows = pl.ds(pl.multiple_of(block * share, 16), many * share)
        for j, src in enumerate((wq_ref, wk_ref)):
            copies.append(
                pltpu.make_async_copy(
                    src.at[rows, :], outs[i].at[pl.ds(j * many * share, many * share), :], sems.at[i, j]
                )
            )
    for copy in copies:
        copy.start()
    for copy in copies:
        copy.wait()


def pack_weights(w_query, w_key, plan, share, pad=0):
    wide = w_query.shape[1]
    if share % 16:
        count, nseq = lax.axis_size("head"), lax.axis_size("seq")
        mine, my_seq = lax.axis_index("head"), lax.axis_index("seq")
        out = []
        for even_shift, odd_shift, many in plan:
            shift = jnp.where(my_seq % 2 == 1, odd_shift, even_shift)
            start = ((mine + shift) % count * nseq + my_seq // many * many) * share
            out.append(
                jnp.concatenate(
                    [lax.dynamic_slice_in_dim(w, start, many * share, 0) for w in (w_query, w_key)]
                )
            )
        return out
    heights = [2 * many * share for _, _, many in plan]
    heights[-1] += pad
    return call(
        functools.partial(pack_kernel, share, tuple(plan)),
        [jax.ShapeDtypeStruct((height, wide), BF16) for height in heights],
        0, sum(heights) * wide * 4,
        *(pltpu.with_memory_space_constraint(w, pltpu.HBM) for w in (w_query, w_key)),
        in_specs=[pl.BlockSpec(memory_space=pl.ANY)] * 2,
        out_specs=[pl.BlockSpec(memory_space=pltpu.VMEM)] * len(plan),
        scratch_shapes=[pltpu.SemaphoreType.DMA((len(plan), 2))],
    )


def join_kernel(groups, nargs, *refs):
    for group, out_ref in zip(groups, refs[-len(groups) :]):
        at = 0
        for i, start, size in group:
            out_ref[at : at + size, :] = refs[i][start : start + size, :]
            at += size


def join(*groups, tokens=()):
    args, spec = [], []
    for group in groups:
        spec.append(tuple((place_in(args, x), start, size) for x, start, size in group))
    return call(
        functools.partial(join_kernel, tuple(spec), len(args)),
        [jax.ShapeDtypeStruct((sum(size for _, _, size in group), args[0].shape[1]), BF16) for group in spec],
        0, 0, *args, *tokens,
        in_specs=[pl.BlockSpec(memory_space=pltpu.VMEM)] * len(args)
        + [pl.BlockSpec(memory_space=pl.ANY)] * len(tokens),
        out_specs=[pl.BlockSpec(memory_space=pltpu.VMEM)] * len(groups),
    )


def place_in(args, x):
    for i, y in enumerate(args):
        if y is x:
            return i
    args.append(x)
    return len(args) - 1


def rows_of(refs, low, high):
    parts, at = [], 0
    for ref in refs:
        first, last = max(low, at), min(high, at + ref.shape[0])
        if first < last:
            parts.append(ref[first - at : last - at, :])
        at += ref.shape[0]
    return parts[0] if len(parts) == 1 else jnp.concatenate(parts)


def row_block(weights, grads):
    share, wide = weights.shape[0] // 2, weights.shape[1]
    return contract(weights[:share], grads[:wide], 1, 0) + contract(weights[share:], grads[wide:], 1, 0)


def own_kernel(wq_ref, wk_ref, grads_ref, out_ref, near_q, near_k, sems):
    chunk, wide = near_q.shape
    rows = pl.ds(pl.multiple_of(lax.axis_index("head") * chunk, 16), chunk)
    copies = [
        pltpu.make_async_copy(src.at[rows, :], dst, sems.at[i])
        for i, (src, dst) in enumerate(((wq_ref, near_q), (wk_ref, near_k)))
    ]
    for copy in copies:
        copy.start()
    for copy in copies:
        copy.wait()
    out_ref[...] = contract(near_q[...], grads_ref[:wide, :], 1, 0) + contract(
        near_k[...], grads_ref[wide:, :], 1, 0
    )


def own_product(w_query, w_key, grads, chunk):
    wide = w_query.shape[1]
    return call(
        own_kernel, jax.ShapeDtypeStruct((chunk, grads.shape[1]), F32),
        4 * chunk * grads.shape[1] * wide, chunk * wide * 4,
        *(pltpu.with_memory_space_constraint(w, pltpu.HBM) for w in (w_query, w_key)), grads,
        in_specs=[pl.BlockSpec(memory_space=pl.ANY)] * 2 + [pl.BlockSpec(memory_space=pltpu.VMEM)],
        out_specs=pl.BlockSpec(memory_space=pltpu.VMEM),
        scratch_shapes=[pltpu.VMEM((chunk, wide), BF16)] * 2 + [pltpu.SemaphoreType.DMA((2,))],
    )


def relay_kernel(own_ref, lower_ref, upper_ref, token_ref, relay_ref, kept_ref, sent_ref):
    mine, odd = lax.axis_index("head"), lax.rem(lax.axis_index("seq"), 2)

    @pl.when(mine == 1)
    def _():
        relay_ref[...] = upper_ref[...]

    @pl.when(mine == 2)
    def _():
        relay_ref[...] = lower_ref[...]

    @pl.when((mine != 1) & (mine != 2))
    def _():
        relay_ref[...] = own_ref[...]

    @pl.when(odd == 0)
    def _():
        kept_ref[...] = lower_ref[...]
        sent_ref[...] = upper_ref[...]

    @pl.when(odd == 1)
    def _():
        kept_ref[...] = upper_ref[...]
        sent_ref[...] = lower_ref[...]


def split_kernel(both_ref, token_ref, theirs_ref):
    odd = lax.rem(lax.axis_index("seq"), 2)
    share = theirs_ref.shape[0] // 2
    for parity in range(2):

        @pl.when(odd == parity)
        def _():
            for j in range(2):
                at = (2 * j + 1 - parity) * share
                theirs_ref[j * share : (j + 1) * share, :] = both_ref[at : at + share, :]


def pick_kernel(both_ref, got_ref, out_ref):
    odd = lax.rem(lax.axis_index("seq"), 2)
    upper = lax.axis_index("head") // 2
    share = out_ref.shape[0] // 2

    @pl.when(odd + upper != 1)
    def _():
        out_ref[...] = got_ref[...]

    for parity in range(2):

        @pl.when((odd == parity) & (upper == 1 - parity))
        def _():
            for j in range(2):
                at = (2 * j + parity) * share
                out_ref[j * share : (j + 1) * share, :] = both_ref[at : at + share, :]


def pair_kernel(count, table_ref, total_ref, *refs):
    weights, (kept_ref, got_ref), (out_ref, head_ref, tail_ref) = refs[:count], refs[count : count + 2], refs[count + 2 :]
    nblocks = table_ref.shape[0]
    size = out_ref.shape[0] // nblocks
    split = head_ref.shape[0] // size
    for j in range(nblocks):
        block = rows_of(weights, 2 * size * j, 2 * size * (j + 1))
        place = table_ref[j]
        rows = pl.ds(pl.multiple_of(place * size, 16), size)
        out_ref[rows, :] = total_ref[rows, :] + row_block(block, kept_ref[...])
        sent = row_block(block, got_ref[...]).astype(BF16)

        @pl.when(place < split)
        def _(sent=sent, place=place):
            head_ref[pl.ds(pl.multiple_of(place * size, 16), size), :] = sent

        @pl.when(place >= split)
        def _(sent=sent, place=place):
            tail_ref[pl.ds(pl.multiple_of((place - split) * size, 16), size), :] = sent


def pair_product(table, total, weights, kept, got, split):
    chunk, span = total.shape
    return call(
        functools.partial(pair_kernel, len(weights)),
        (
            jax.ShapeDtypeStruct((chunk, span), F32),
            jax.ShapeDtypeStruct((split, span), BF16),
            jax.ShapeDtypeStruct((chunk - split, span), BF16),
        ),
        4 * chunk * span * kept.shape[0], chunk * span * 10,
        table, total, *weights, kept, got,
        in_specs=[pl.BlockSpec(memory_space=pltpu.SMEM)]
        + [pl.BlockSpec(memory_space=pltpu.VMEM)] * (3 + len(weights)),
        out_specs=[pl.BlockSpec(memory_space=pltpu.VMEM)] * 3,
        vmem=24 * 1024 * 1024,
    )


def add_kernel(blocks, base, low, high, plus, table_ref, total_ref, grads_ref, *refs):
    args, out_ref = refs[:-1], refs[-1]
    nshares = table_ref.shape[0]
    share = out_ref.shape[0] // nshares
    for j in range(nshares):
        rows = pl.ds(pl.multiple_of(table_ref[j] * share, 8), share)
        total = total_ref[rows, :]
        if plus:
            head, tail = (args[i] for i in plus)
            split, place = head.shape[0] // share, table_ref[j]
            from_head = head[pl.ds(pl.multiple_of(jnp.minimum(place, split - 1) * share, 16), share), :]
            from_tail = tail[pl.ds(pl.multiple_of(jnp.maximum(place - split, 0) * share, 16), share), :]
            total = total + jnp.where(place < split, from_head, from_tail).astype(F32)
        if low <= j < high:
            weights = rows_of([args[i] for i in blocks], 2 * share * (j - base), 2 * share * (j + 1 - base))
            total = total + row_block(weights, grads_ref[...])
        out_ref[rows, :] = total.astype(out_ref.dtype)


def add_product(table, total, blocks, grads, last, plus=(), base=0, low=0, high=None):
    chunk, span = total.shape
    args = []
    blocks = tuple(place_in(args, x) for x in blocks)
    plus = tuple(place_in(args, x) for x in plus)
    high = table.shape[0] if high is None else high
    return call(
        functools.partial(add_kernel, blocks, base, low, high, plus),
        jax.ShapeDtypeStruct((chunk, span), BF16 if last else F32),
        2 * chunk * span * grads.shape[0], chunk * span * 8,
        table, total, grads, *args,
        in_specs=[pl.BlockSpec(memory_space=pltpu.SMEM)]
        + [pl.BlockSpec(memory_space=pltpu.VMEM)] * (2 + len(args)),
        out_specs=pl.BlockSpec(memory_space=pltpu.VMEM),
        vmem=24 * 1024 * 1024,
    )


def shards(query_act, key_act, value_act, grad_output, log_decay, w_query, w_key):
    span = query_act.shape[0]
    nheads = log_decay.shape[1]
    width = query_act.shape[1] // nheads
    nseq, nhead = lax.axis_size("seq"), lax.axis_size("head")
    my_seq, my_head = lax.axis_index("seq"), lax.axis_index("head")
    chunk = w_query.shape[0] // nhead
    share = chunk // nseq
    rows = nheads * width

    shifts = [1, nhead - 1] + list(range(2, nhead - 1))
    ring = {k: [(i, (i + k) % nhead) for i in range(nhead)] for k in shifts}
    fast = nhead == 4 and nseq == 8
    if fast:
        packed = pack_weights(w_query, w_key, [(1, 3, 2), (2, 2, 2)], share)

        def moves(even, odd):
            return [
                (i * nhead + j, i * nhead + k) for i in range(nseq) for j, k in (odd if i % 2 else even)
            ]

        axes = ("seq", "head")
        first = lax.ppermute(packed[0], axes, moves(ring[1], ring[3]))
        passing = lax.ppermute(packed[1], axes, moves([(0, 1), (1, 2)], [(3, 2), (2, 1)]))
    else:
        packed = pack_weights(w_query, w_key, [(k, k, 1) for k in shifts], share)
        pieces = [lax.ppermute(p, "head", ring[k]) for p, k in zip(packed, shifts)]

    decay = log_decay.T
    sent, held, logs = call(
        functools.partial(states_kernel, nheads, width),
        (
            jax.ShapeDtypeStruct((2 * rows + 16, width), BF16),
            jax.ShapeDtypeStruct((2 * rows, width), F32),
            jax.ShapeDtypeStruct((24, width), F32),
        ),
        4 * span * rows * width, 8 * span * rows,
        decay, query_act, key_act, value_act, grad_output, packed[0],
        in_specs=[pl.BlockSpec(memory_space=pltpu.VMEM)] * 5 + [pl.BlockSpec(memory_space=pl.ANY)],
    )
    local = call(
        functools.partial(local_kernel, nheads, width),
        jax.ShapeDtypeStruct((2 * rows, span), F32),
        6 * span * span * rows, 16 * span * rows,
        decay, query_act, key_act, value_act, grad_output,
    )
    hop, enter = 1, None
    while True:
        got = lax.ppermute(sent, "seq", [(i, i ^ hop) for i in range(nseq)])
        if 2 * hop >= nseq:
            break
        final_next = 4 * hop >= nseq
        out_shape = (
            jax.ShapeDtypeStruct((rows if final_next else 2 * rows + 16, width), BF16),
            jax.ShapeDtypeStruct((2 * rows, width), F32),
            jax.ShapeDtypeStruct((24, width), F32),
            jax.ShapeDtypeStruct((2 * rows, width), F32),
        )
        args = [got, held, logs] + ([] if enter is None else [enter])
        sent, held, logs, enter = call(
            functools.partial(step_kernel, nheads, width, hop, enter is None, final_next),
            out_shape, 10 * rows * width, 16 * rows * width, *args,
        )
        hop *= 2
    both = call(
        functools.partial(carry_kernel, nheads, width, hop),
        jax.ShapeDtypeStruct((2 * rows, span), BF16),
        4 * span * rows * width, 16 * span * rows,
        decay, value_act, grad_output, got, logs, enter, local,
    )

    even, odd = share_deltas(nseq)
    deltas = jnp.where(my_seq % 2 == 1, jnp.array(odd, jnp.int32), jnp.array(even, jnp.int32))
    table = deltas ^ my_seq
    total = own_product(w_query, w_key, both, chunk)

    if fast:
        one, two = 2 * share, 4 * share
        (first,) = gate([first], [both])
        second = share_hop(first, 0)
        (near,) = join(((first, 0, two), (second, 0, two)))
        blocks = [near, share_hop(near, 1)]
        (ready,) = gate([both], [total, near])
        p1 = lax.ppermute(ready, "head", ring[1])
        p3 = lax.ppermute(ready, "head", ring[3])
        (passing,) = gate([passing], [first])
        passing = lax.ppermute(passing, axes, moves([(1, 2), (2, 3)], [(2, 1), (1, 0)]))
        theirs = call(
            split_kernel, jax.ShapeDtypeStruct((one, passing.shape[1]), BF16), 0, 0, passing, total,
            in_specs=[pl.BlockSpec(memory_space=pltpu.VMEM), pl.BlockSpec(memory_space=pl.ANY)],
            out_specs=pl.BlockSpec(memory_space=pltpu.VMEM),
        )
        theirs = lax.ppermute(
            theirs, axes,
            [(i * nhead + j, (i ^ 1) * nhead + j) for i in range(nseq) for j in range(nhead) if (j < 2) == (i % 2)],
        )
        third = call(
            pick_kernel, jax.ShapeDtypeStruct(theirs.shape, BF16), 0, 0, passing, theirs,
            in_specs=[pl.BlockSpec(memory_space=pltpu.VMEM)] * 2,
            out_specs=pl.BlockSpec(memory_space=pltpu.VMEM),
        )
        fourth, fifth = share_hop(third, 0), share_hop(third, 1)
        fourth, fifth = gate([fourth, fifth])
        sixth = share_hop(fourth, 1)
        (early,) = join(((third, 0, one), (fourth, 0, one), (fifth, 0, CUT)))
        relay, kept, handed = call(
            relay_kernel, [jax.ShapeDtypeStruct(both.shape, BF16)] * 3, 0, 0, ready, p1, p3, total,
            in_specs=[pl.BlockSpec(memory_space=pltpu.VMEM)] * 3 + [pl.BlockSpec(memory_space=pl.ANY)],
            out_specs=[pl.BlockSpec(memory_space=pltpu.VMEM)] * 3,
        )
        p2 = lax.ppermute(relay, "head", [(0, 2), (1, 0), (2, 3), (3, 1)])
        got = share_hop(handed, 2)
        total, *handed = pair_product(table[: nseq // 2] // 2, total, blocks, kept, got, SPLIT)
        got = [share_hop(x, 2) for x in handed]
        (late,) = join(((fifth, CUT, one - CUT), (sixth, 0, one)), tokens=[p2])
        early, late = share_hop(early, 2), share_hop(late, 2)
        total = add_product(table, total, (third, fourth, fifth, sixth, early), p2, False, high=6)
        return add_product(table, total, (early, late), p2, True, plus=got, base=4, low=6)

    gathered = lax.all_gather(both, "head")
    for i, k in enumerate(shifts):
        held = [pieces[i]]
        for number in range(len(share_order(nseq)[0]) + 1):
            whole = held[0] if number == 0 else jnp.concatenate(held)
            held = [whole, share_hop(whole, number)]
        grads = gathered[(my_head + nhead - k) % nhead]
        total = add_product(table, total, held, grads, i == nhead - 2)
    return total


def solution(mesh):
    placed = (
        P("seq", "head"),
        P("seq", "head"),
        P("seq", "head"),
        P("seq", "head"),
        P("seq", "head"),
        P(None, "head"),
        P(None, "head"),
    )
    return jax.shard_map(
        shards, mesh=mesh, in_specs=placed, out_specs=P("head", "seq"), check_vma=False
    )
```

```python
import functools

import jax
import jax.numpy as jnp
from jax import lax
from jax.experimental import pallas as pl
from jax.experimental.pallas import tpu as pltpu
from jax.sharding import PartitionSpec as P

F32 = jnp.float32
BF16 = jnp.bfloat16
VMEM_BYTES = 16 * 1024 * 1024
CUT = 144
SPLIT = 1152


def contract(a, b, left, right):
    return lax.dot_general(a, b, (((left,), (right,)), ((), ())), preferred_element_type=F32)


def call(kernel, out_shape, flops, nbytes, *args, aliases=None, vmem=VMEM_BYTES, **spec):
    return pl.pallas_call(
        kernel,
        out_shape=out_shape,
        cost_estimate=pl.CostEstimate(flops=flops, bytes_accessed=nbytes, transcendentals=0),
        compiler_params=pltpu.CompilerParams(vmem_limit_bytes=vmem),
        input_output_aliases=aliases or {},
        **spec,
    )(*args)


def gate_kernel(count, *refs):
    del count, refs


def gate(passed, tokens=(), flops=0):
    return call(
        functools.partial(gate_kernel, len(passed)),
        [jax.ShapeDtypeStruct(x.shape, x.dtype) for x in passed],
        flops, 0, *passed, *tokens,
        aliases={i: i for i in range(len(passed))},
        in_specs=[pl.BlockSpec(memory_space=pl.ANY)] * (len(passed) + len(tokens)),
        out_specs=[pl.BlockSpec(memory_space=pl.ANY)] * len(passed),
    )


def thirds(x):
    high = x.astype(BF16)
    rest = x - high.astype(F32)
    middle = rest.astype(BF16)
    return high, middle, (rest - middle.astype(F32)).astype(BF16)


def triangle(span):
    rows = lax.broadcasted_iota(jnp.int32, (span, span), 0)
    cols = lax.broadcasted_iota(jnp.int32, (span, span), 1)
    return rows >= cols


def upper_half(hop):
    return ((lax.axis_index("seq") // hop) % 2).astype(F32)


def states_kernel(nheads, width, decay_ref, q_ref, k_ref, v_ref, g_ref, token_ref, sent_ref, held_ref, logs_ref):
    span = q_ref.shape[0]
    tri = triangle(span).astype(F32).astype(BF16)
    cum = sum(contract(tri, part, 1, 1) for part in thirds(decay_ref[...]))
    rows = nheads * width
    row = lax.broadcasted_iota(jnp.int32, (8, width), 0)
    totals = jnp.zeros((8, width), F32)
    for h in range(nheads):
        cols = slice(h * width, (h + 1) * width)
        cum_h = cum[:, h : h + 1]
        last = cum[span - 1 : span, h : h + 1]
        key_w = (k_ref[:, cols].astype(F32) * jnp.exp(last - cum_h)).astype(BF16)
        query_w = (q_ref[:, cols].astype(F32) * jnp.exp(cum_h)).astype(BF16)
        state = contract(key_w, v_ref[:, cols], 0, 0)
        grad = contract(query_w, g_ref[:, cols], 0, 0)
        held_ref[h * width : (h + 1) * width, :] = state
        held_ref[rows + h * width : rows + (h + 1) * width, :] = grad
        sent_ref[h * width : (h + 1) * width, :] = state.astype(BF16)
        sent_ref[rows + h * width : rows + (h + 1) * width, :] = grad.astype(BF16)
        totals = jnp.where(row == h, jnp.broadcast_to(last, (8, width)), totals)
    high = totals.astype(BF16).astype(F32)
    sent_ref[2 * rows :, :] = jnp.concatenate([high, totals - high]).astype(BF16)
    logs_ref[0:8, :] = totals
    logs_ref[8:24, :] = jnp.zeros((16, width), F32)


def step_kernel(nheads, width, hop, first, final_next, got_ref, held_ref, logs_ref, *refs):
    if first:
        sent_ref, held_out, logs_out, enter_out = refs
    else:
        enter_ref, sent_ref, held_out, logs_out, enter_out = refs
    rows = nheads * width
    up = upper_half(hop)
    low = 1.0 - up
    tail = got_ref[2 * rows :, :].astype(F32)
    got_total = tail[0:8] + tail[8:16]
    total, before, after = logs_ref[0:8, :], logs_ref[8:16, :], logs_ref[16:24, :]
    own_decay, got_decay = jnp.exp(total), jnp.exp(got_total)
    from_before, from_after = up * jnp.exp(before), low * jnp.exp(after)
    total = total + got_total
    logs_out[0:8, :] = total
    logs_out[8:16, :] = before + up * got_total
    logs_out[16:24, :] = after + low * got_total
    if final_next:
        next_up = upper_half(2 * hop) > 0.5
    else:
        high = total.astype(BF16).astype(F32)
        sent_ref[2 * rows :, :] = jnp.concatenate([high, total - high]).astype(BF16)
    for h in range(nheads):
        one = slice(h * width, (h + 1) * width)
        two = slice(rows + h * width, rows + (h + 1) * width)
        got_state, got_grad = got_ref[one, :].astype(F32), got_ref[two, :].astype(F32)
        own, got = own_decay[h : h + 1, :], got_decay[h : h + 1, :]
        state = (up + low * got) * held_ref[one, :] + (up * own + low) * got_state
        grad = (low + up * got) * held_ref[two, :] + (low * own + up) * got_grad
        state_in = from_before[h : h + 1, :] * got_state
        grad_in = from_after[h : h + 1, :] * got_grad
        if not first:
            state_in = enter_ref[one, :] + state_in
            grad_in = enter_ref[two, :] + grad_in
        enter_out[one, :] = state_in
        enter_out[two, :] = grad_in
        held_out[one, :] = state
        held_out[two, :] = grad
        if final_next:
            sent_ref[one, :] = jnp.where(next_up, grad, state).astype(BF16)
        else:
            sent_ref[one, :] = state.astype(BF16)
            sent_ref[two, :] = grad.astype(BF16)


def local_kernel(nheads, width, decay_ref, q_ref, k_ref, v_ref, g_ref, out_ref):
    span = q_ref.shape[0]
    rows = nheads * width
    causal = triangle(span)
    tri = causal.astype(F32).astype(BF16)
    parts = thirds(decay_ref[...])
    cum = sum(contract(tri, part, 1, 1) for part in parts)
    cum_rows = sum(contract(part, tri, 1, 1) for part in parts)
    for h in range(nheads):
        cols = slice(h * width, (h + 1) * width)
        gap = cum[:, h : h + 1] - cum_rows[h : h + 1, :]
        decay = jnp.where(causal, jnp.exp(jnp.minimum(gap, 0.0)), 0.0)
        weighted = (contract(g_ref[:, cols], v_ref[:, cols], 1, 1) * decay).astype(BF16)
        out_ref[h * width : (h + 1) * width, :] = contract(k_ref[:, cols], weighted, 0, 1)
        out_ref[rows + h * width : rows + (h + 1) * width, :] = contract(
            q_ref[:, cols], weighted, 0, 0
        )


def carry_kernel(nheads, width, hop, decay_ref, v_ref, g_ref, got_ref, logs_ref, enter_ref, local_ref, out_ref):
    span = v_ref.shape[0]
    rows = nheads * width
    tri = triangle(span).astype(F32).astype(BF16)
    cum_rows = sum(contract(part, tri, 1, 1) for part in thirds(decay_ref[...]))
    up = upper_half(hop)
    low = 1.0 - up
    from_before = up * jnp.exp(logs_ref[8:16, :])
    from_after = low * jnp.exp(logs_ref[16:24, :])
    for h in range(nheads):
        cols = slice(h * width, (h + 1) * width)
        two = slice(rows + h * width, rows + (h + 1) * width)
        got = got_ref[cols, :].astype(F32)
        state_in = (enter_ref[cols, :] + from_before[h : h + 1, :] * got).astype(BF16)
        grad_in = (enter_ref[two, :] + from_after[h : h + 1, :] * got).astype(BF16)
        cum_h = cum_rows[h : h + 1, :]
        last = cum_h[:, span - 1 : span]
        dq = local_ref[cols, :] + contract(state_in, g_ref[:, cols], 1, 1) * jnp.exp(cum_h)
        dk = local_ref[two, :] + contract(grad_in, v_ref[:, cols], 1, 1) * jnp.exp(last - cum_h)
        out_ref[cols, :] = dq.astype(BF16)
        out_ref[two, :] = dk.astype(BF16)


def share_order(count):
    bits = []
    hop = 2
    while hop < count:
        bits.append(hop)
        hop *= 2
    return bits, bits[::-1]


def share_hop(held, number):
    count = lax.axis_size("seq")
    even, odd = share_order(count)
    even, odd = even + [1], odd + [1]
    pairs = [(i, i ^ (odd[number] if i % 2 else even[number])) for i in range(count)]
    return lax.ppermute(held, "seq", pairs)


def share_deltas(count):
    even, odd = share_order(count)

    def spread(order):
        out = [0]
        for hop in order:
            out = out + [d ^ hop for d in out]
        return out

    return tuple(
        spread(first) + [d ^ 1 for d in spread(second)] for first, second in ((even, odd), (odd, even))
    )


def pack_kernel(share, plan, wq_ref, wk_ref, *refs):
    count, nseq = lax.axis_size("head"), lax.axis_size("seq")
    mine, my_seq = lax.axis_index("head"), lax.axis_index("seq")
    odd = lax.rem(my_seq, 2)
    outs, sems = refs[: len(plan)], refs[len(plan)]
    copies = []
    for i, (even_shift, odd_shift, many) in enumerate(plan):
        shift = even_shift + odd * (odd_shift - even_shift)
        block = lax.rem(mine + shift, count) * nseq + my_seq // many * many
        rows = pl.ds(pl.multiple_of(block * share, 16), many * share)
        for j, src in enumerate((wq_ref, wk_ref)):
            copies.append(
                pltpu.make_async_copy(
                    src.at[rows, :], outs[i].at[pl.ds(j * many * share, many * share), :], sems.at[i, j]
                )
            )
    for copy in copies:
        copy.start()
    for copy in copies:
        copy.wait()


def pack_weights(w_query, w_key, plan, share, pad=0):
    wide = w_query.shape[1]
    if share % 16:
        count, nseq = lax.axis_size("head"), lax.axis_size("seq")
        mine, my_seq = lax.axis_index("head"), lax.axis_index("seq")
        out = []
        for even_shift, odd_shift, many in plan:
            shift = jnp.where(my_seq % 2 == 1, odd_shift, even_shift)
            start = ((mine + shift) % count * nseq + my_seq // many * many) * share
            out.append(
                jnp.concatenate(
                    [lax.dynamic_slice_in_dim(w, start, many * share, 0) for w in (w_query, w_key)]
                )
            )
        return out
    heights = [2 * many * share for _, _, many in plan]
    heights[-1] += pad
    return call(
        functools.partial(pack_kernel, share, tuple(plan)),
        [jax.ShapeDtypeStruct((height, wide), BF16) for height in heights],
        0, sum(heights) * wide * 4,
        *(pltpu.with_memory_space_constraint(w, pltpu.HBM) for w in (w_query, w_key)),
        in_specs=[pl.BlockSpec(memory_space=pl.ANY)] * 2,
        out_specs=[pl.BlockSpec(memory_space=pltpu.VMEM)] * len(plan),
        scratch_shapes=[pltpu.SemaphoreType.DMA((len(plan), 2))],
    )


def join_kernel(groups, nargs, *refs):
    for group, out_ref in zip(groups, refs[-len(groups) :]):
        at = 0
        for i, start, size in group:
            out_ref[at : at + size, :] = refs[i][start : start + size, :]
            at += size


def join(*groups, tokens=()):
    args, spec = [], []
    for group in groups:
        spec.append(tuple((place_in(args, x), start, size) for x, start, size in group))
    return call(
        functools.partial(join_kernel, tuple(spec), len(args)),
        [jax.ShapeDtypeStruct((sum(size for _, _, size in group), args[0].shape[1]), BF16) for group in spec],
        0, 0, *args, *tokens,
        in_specs=[pl.BlockSpec(memory_space=pltpu.VMEM)] * len(args)
        + [pl.BlockSpec(memory_space=pl.ANY)] * len(tokens),
        out_specs=[pl.BlockSpec(memory_space=pltpu.VMEM)] * len(groups),
    )


def place_in(args, x):
    for i, y in enumerate(args):
        if y is x:
            return i
    args.append(x)
    return len(args) - 1


def rows_of(refs, low, high):
    parts, at = [], 0
    for ref in refs:
        first, last = max(low, at), min(high, at + ref.shape[0])
        if first < last:
            parts.append(ref[first - at : last - at, :])
        at += ref.shape[0]
    return parts[0] if len(parts) == 1 else jnp.concatenate(parts)


def row_block(weights, grads):
    share, wide = weights.shape[0] // 2, weights.shape[1]
    return contract(weights[:share], grads[:wide], 1, 0) + contract(weights[share:], grads[wide:], 1, 0)


def own_kernel(wq_ref, wk_ref, grads_ref, out_ref, near_q, near_k, sems):
    chunk, wide = near_q.shape
    rows = pl.ds(pl.multiple_of(lax.axis_index("head") * chunk, 16), chunk)
    copies = [
        pltpu.make_async_copy(src.at[rows, :], dst, sems.at[i])
        for i, (src, dst) in enumerate(((wq_ref, near_q), (wk_ref, near_k)))
    ]
    for copy in copies:
        copy.start()
    for copy in copies:
        copy.wait()
    out_ref[...] = contract(near_q[...], grads_ref[:wide, :], 1, 0) + contract(
        near_k[...], grads_ref[wide:, :], 1, 0
    )


def own_product(w_query, w_key, grads, chunk):
    wide = w_query.shape[1]
    return call(
        own_kernel, jax.ShapeDtypeStruct((chunk, grads.shape[1]), F32),
        4 * chunk * grads.shape[1] * wide, chunk * wide * 4,
        *(pltpu.with_memory_space_constraint(w, pltpu.HBM) for w in (w_query, w_key)), grads,
        in_specs=[pl.BlockSpec(memory_space=pl.ANY)] * 2 + [pl.BlockSpec(memory_space=pltpu.VMEM)],
        out_specs=pl.BlockSpec(memory_space=pltpu.VMEM),
        scratch_shapes=[pltpu.VMEM((chunk, wide), BF16)] * 2 + [pltpu.SemaphoreType.DMA((2,))],
    )


def relay_kernel(own_ref, lower_ref, upper_ref, token_ref, relay_ref, kept_ref, sent_ref):
    mine, odd = lax.axis_index("head"), lax.rem(lax.axis_index("seq"), 2)

    @pl.when(mine == 1)
    def _():
        relay_ref[...] = upper_ref[...]

    @pl.when(mine == 2)
    def _():
        relay_ref[...] = lower_ref[...]

    @pl.when((mine != 1) & (mine != 2))
    def _():
        relay_ref[...] = own_ref[...]

    @pl.when(odd == 0)
    def _():
        kept_ref[...] = lower_ref[...]
        sent_ref[...] = upper_ref[...]

    @pl.when(odd == 1)
    def _():
        kept_ref[...] = upper_ref[...]
        sent_ref[...] = lower_ref[...]


def split_kernel(both_ref, token_ref, theirs_ref):
    odd = lax.rem(lax.axis_index("seq"), 2)
    share = theirs_ref.shape[0] // 2
    for parity in range(2):

        @pl.when(odd == parity)
        def _():
            for j in range(2):
                at = (2 * j + 1 - parity) * share
                theirs_ref[j * share : (j + 1) * share, :] = both_ref[at : at + share, :]


def pick_kernel(both_ref, got_ref, out_ref):
    odd = lax.rem(lax.axis_index("seq"), 2)
    upper = lax.axis_index("head") // 2
    share = out_ref.shape[0] // 2

    @pl.when(odd != upper)
    def _():
        out_ref[...] = got_ref[...]

    for parity in range(2):

        @pl.when((odd == parity) & (upper == parity))
        def _():
            for j in range(2):
                at = (2 * j + parity) * share
                out_ref[j * share : (j + 1) * share, :] = both_ref[at : at + share, :]


def pair_kernel(count, table_ref, total_ref, *refs):
    weights, (kept_ref, got_ref), (out_ref, head_ref, tail_ref) = refs[:count], refs[count : count + 2], refs[count + 2 :]
    nblocks = table_ref.shape[0]
    size = out_ref.shape[0] // nblocks
    split = head_ref.shape[0] // size
    for j in range(nblocks):
        block = rows_of(weights, 2 * size * j, 2 * size * (j + 1))
        place = table_ref[j]
        rows = pl.ds(pl.multiple_of(place * size, 16), size)
        out_ref[rows, :] = total_ref[rows, :] + row_block(block, kept_ref[...])
        sent = row_block(block, got_ref[...]).astype(BF16)

        @pl.when(place < split)
        def _(sent=sent, place=place):
            head_ref[pl.ds(pl.multiple_of(place * size, 16), size), :] = sent

        @pl.when(place >= split)
        def _(sent=sent, place=place):
            tail_ref[pl.ds(pl.multiple_of((place - split) * size, 16), size), :] = sent


def pair_product(table, total, weights, kept, got, split):
    chunk, span = total.shape
    return call(
        functools.partial(pair_kernel, len(weights)),
        (
            jax.ShapeDtypeStruct((chunk, span), F32),
            jax.ShapeDtypeStruct((split, span), BF16),
            jax.ShapeDtypeStruct((chunk - split, span), BF16),
        ),
        4 * chunk * span * kept.shape[0], chunk * span * 10,
        table, total, *weights, kept, got,
        in_specs=[pl.BlockSpec(memory_space=pltpu.SMEM)]
        + [pl.BlockSpec(memory_space=pltpu.VMEM)] * (3 + len(weights)),
        out_specs=[pl.BlockSpec(memory_space=pltpu.VMEM)] * 3,
        vmem=24 * 1024 * 1024,
    )


def add_kernel(blocks, base, low, high, plus, table_ref, total_ref, grads_ref, *refs):
    args, out_ref = refs[:-1], refs[-1]
    nshares = table_ref.shape[0]
    share = out_ref.shape[0] // nshares
    for j in range(nshares):
        rows = pl.ds(pl.multiple_of(table_ref[j] * share, 8), share)
        total = total_ref[rows, :]
        if plus:
            head, tail = (args[i] for i in plus)
            split, place = head.shape[0] // share, table_ref[j]
            from_head = head[pl.ds(pl.multiple_of(jnp.minimum(place, split - 1) * share, 16), share), :]
            from_tail = tail[pl.ds(pl.multiple_of(jnp.maximum(place - split, 0) * share, 16), share), :]
            total = total + jnp.where(place < split, from_head, from_tail).astype(F32)
        if low <= j < high:
            weights = rows_of([args[i] for i in blocks], 2 * share * (j - base), 2 * share * (j + 1 - base))
            total = total + row_block(weights, grads_ref[...])
        out_ref[rows, :] = total.astype(out_ref.dtype)


def add_product(table, total, blocks, grads, last, plus=(), base=0, low=0, high=None):
    chunk, span = total.shape
    args = []
    blocks = tuple(place_in(args, x) for x in blocks)
    plus = tuple(place_in(args, x) for x in plus)
    high = table.shape[0] if high is None else high
    return call(
        functools.partial(add_kernel, blocks, base, low, high, plus),
        jax.ShapeDtypeStruct((chunk, span), BF16 if last else F32),
        2 * chunk * span * grads.shape[0], chunk * span * 8,
        table, total, grads, *args,
        in_specs=[pl.BlockSpec(memory_space=pltpu.SMEM)]
        + [pl.BlockSpec(memory_space=pltpu.VMEM)] * (2 + len(args)),
        out_specs=pl.BlockSpec(memory_space=pltpu.VMEM),
        vmem=24 * 1024 * 1024,
    )


def shards(query_act, key_act, value_act, grad_output, log_decay, w_query, w_key):
    span = query_act.shape[0]
    nheads = log_decay.shape[1]
    width = query_act.shape[1] // nheads
    nseq, nhead = lax.axis_size("seq"), lax.axis_size("head")
    my_seq, my_head = lax.axis_index("seq"), lax.axis_index("head")
    chunk = w_query.shape[0] // nhead
    share = chunk // nseq
    rows = nheads * width

    shifts = [1, nhead - 1] + list(range(2, nhead - 1))
    ring = {k: [(i, (i + k) % nhead) for i in range(nhead)] for k in shifts}
    fast = nhead == 4 and nseq == 8
    if fast:
        packed = pack_weights(w_query, w_key, [(1, 3, 2), (2, 2, 2)], share)

        def moves(even, odd):
            return [
                (i * nhead + j, i * nhead + k) for i in range(nseq) for j, k in (odd if i % 2 else even)
            ]

        axes = ("seq", "head")
        first = lax.ppermute(packed[0], axes, moves(ring[1], ring[3]))
        passing = lax.ppermute(packed[1], axes, moves([(3, 2), (2, 1)], [(0, 1), (1, 2)]))
    else:
        packed = pack_weights(w_query, w_key, [(k, k, 1) for k in shifts], share)
        pieces = [lax.ppermute(p, "head", ring[k]) for p, k in zip(packed, shifts)]

    decay = log_decay.T
    sent, held, logs = call(
        functools.partial(states_kernel, nheads, width),
        (
            jax.ShapeDtypeStruct((2 * rows + 16, width), BF16),
            jax.ShapeDtypeStruct((2 * rows, width), F32),
            jax.ShapeDtypeStruct((24, width), F32),
        ),
        4 * span * rows * width, 8 * span * rows,
        decay, query_act, key_act, value_act, grad_output, packed[0],
        in_specs=[pl.BlockSpec(memory_space=pltpu.VMEM)] * 5 + [pl.BlockSpec(memory_space=pl.ANY)],
    )
    local = call(
        functools.partial(local_kernel, nheads, width),
        jax.ShapeDtypeStruct((2 * rows, span), F32),
        6 * span * span * rows, 16 * span * rows,
        decay, query_act, key_act, value_act, grad_output,
    )
    hop, enter = 1, None
    while True:
        got = lax.ppermute(sent, "seq", [(i, i ^ hop) for i in range(nseq)])
        if 2 * hop >= nseq:
            break
        final_next = 4 * hop >= nseq
        out_shape = (
            jax.ShapeDtypeStruct((rows if final_next else 2 * rows + 16, width), BF16),
            jax.ShapeDtypeStruct((2 * rows, width), F32),
            jax.ShapeDtypeStruct((24, width), F32),
            jax.ShapeDtypeStruct((2 * rows, width), F32),
        )
        args = [got, held, logs] + ([] if enter is None else [enter])
        sent, held, logs, enter = call(
            functools.partial(step_kernel, nheads, width, hop, enter is None, final_next),
            out_shape, 10 * rows * width, 16 * rows * width, *args,
        )
        hop *= 2
    both = call(
        functools.partial(carry_kernel, nheads, width, hop),
        jax.ShapeDtypeStruct((2 * rows, span), BF16),
        4 * span * rows * width, 16 * span * rows,
        decay, value_act, grad_output, got, logs, enter, local,
    )

    even, odd = share_deltas(nseq)
    deltas = jnp.where(my_seq % 2 == 1, jnp.array(odd, jnp.int32), jnp.array(even, jnp.int32))
    table = deltas ^ my_seq
    total = own_product(w_query, w_key, both, chunk)

    if fast:
        one, two = 2 * share, 4 * share
        (first,) = gate([first], [both])
        second = share_hop(first, 0)
        (near,) = join(((first, 0, two), (second, 0, two)))
        blocks = [near, share_hop(near, 1)]
        (ready,) = gate([both], [total, near])
        p1 = lax.ppermute(ready, "head", ring[1])
        p3 = lax.ppermute(ready, "head", ring[3])
        (passing,) = gate([passing], [first])
        passing = lax.ppermute(passing, axes, moves([(2, 1), (1, 0)], [(1, 2), (2, 3)]))
        theirs = call(
            split_kernel, jax.ShapeDtypeStruct((one, passing.shape[1]), BF16), 0, 0, passing, total,
            in_specs=[pl.BlockSpec(memory_space=pltpu.VMEM), pl.BlockSpec(memory_space=pl.ANY)],
            out_specs=pl.BlockSpec(memory_space=pltpu.VMEM),
        )
        theirs = lax.ppermute(
            theirs, axes,
            [(i * nhead + j, (i ^ 1) * nhead + j) for i in range(nseq) for j in range(nhead) if (j >= 2) == (i % 2)],
        )
        third = call(
            pick_kernel, jax.ShapeDtypeStruct(theirs.shape, BF16), 0, 0, passing, theirs,
            in_specs=[pl.BlockSpec(memory_space=pltpu.VMEM)] * 2,
            out_specs=pl.BlockSpec(memory_space=pltpu.VMEM),
        )
        fourth, fifth = share_hop(third, 0), share_hop(third, 1)
        fourth, fifth = gate([fourth, fifth])
        sixth = share_hop(fourth, 1)
        (early,) = join(((third, 0, one), (fourth, 0, one), (fifth, 0, CUT)))
        relay, kept, handed = call(
            relay_kernel, [jax.ShapeDtypeStruct(both.shape, BF16)] * 3, 0, 0, ready, p1, p3, total,
            in_specs=[pl.BlockSpec(memory_space=pltpu.VMEM)] * 3 + [pl.BlockSpec(memory_space=pl.ANY)],
            out_specs=[pl.BlockSpec(memory_space=pltpu.VMEM)] * 3,
        )
        p2 = lax.ppermute(relay, "head", [(0, 2), (1, 0), (2, 3), (3, 1)])
        got = share_hop(handed, 2)
        total, *handed = pair_product(table[: nseq // 2] // 2, total, blocks, kept, got, SPLIT)
        got = [share_hop(x, 2) for x in handed]
        (late,) = join(((fifth, CUT, one - CUT), (sixth, 0, one)), tokens=[p2])
        early, late = share_hop(early, 2), share_hop(late, 2)
        total = add_product(table, total, (third, fourth, fifth, sixth, early), p2, False, high=6)
        return add_product(table, total, (early, late), p2, True, plus=got, base=4, low=6)

    gathered = lax.all_gather(both, "head")
    for i, k in enumerate(shifts):
        held = [pieces[i]]
        for number in range(len(share_order(nseq)[0]) + 1):
            whole = held[0] if number == 0 else jnp.concatenate(held)
            held = [whole, share_hop(whole, number)]
        grads = gathered[(my_head + nhead - k) % nhead]
        total = add_product(table, total, held, grads, i == nhead - 2)
    return total


def solution(mesh):
    placed = (
        P("seq", "head"),
        P("seq", "head"),
        P("seq", "head"),
        P("seq", "head"),
        P("seq", "head"),
        P(None, "head"),
        P(None, "head"),
    )
    return jax.shard_map(
        shards, mesh=mesh, in_specs=placed, out_specs=P("head", "seq"), check_vma=False
    )
```

```python
import functools

import jax
import jax.numpy as jnp
from jax import lax
from jax.experimental import pallas as pl
from jax.experimental.pallas import tpu as pltpu
from jax.sharding import PartitionSpec as P

F32 = jnp.float32
BF16 = jnp.bfloat16
VMEM_BYTES = 16 * 1024 * 1024
CUT = 144
SPLIT = 1152


def contract(a, b, left, right):
    return lax.dot_general(a, b, (((left,), (right,)), ((), ())), preferred_element_type=F32)


def call(kernel, out_shape, flops, nbytes, *args, aliases=None, vmem=VMEM_BYTES, **spec):
    return pl.pallas_call(
        kernel,
        out_shape=out_shape,
        cost_estimate=pl.CostEstimate(flops=flops, bytes_accessed=nbytes, transcendentals=0),
        compiler_params=pltpu.CompilerParams(vmem_limit_bytes=vmem),
        input_output_aliases=aliases or {},
        **spec,
    )(*args)


def gate_kernel(count, *refs):
    del count, refs


def gate(passed, tokens=(), flops=0):
    return call(
        functools.partial(gate_kernel, len(passed)),
        [jax.ShapeDtypeStruct(x.shape, x.dtype) for x in passed],
        flops, 0, *passed, *tokens,
        aliases={i: i for i in range(len(passed))},
        in_specs=[pl.BlockSpec(memory_space=pl.ANY)] * (len(passed) + len(tokens)),
        out_specs=[pl.BlockSpec(memory_space=pl.ANY)] * len(passed),
    )


def thirds(x):
    high = x.astype(BF16)
    rest = x - high.astype(F32)
    middle = rest.astype(BF16)
    return high, middle, (rest - middle.astype(F32)).astype(BF16)


def triangle(span):
    rows = lax.broadcasted_iota(jnp.int32, (span, span), 0)
    cols = lax.broadcasted_iota(jnp.int32, (span, span), 1)
    return rows >= cols


def upper_half(hop):
    return ((lax.axis_index("seq") // hop) % 2).astype(F32)


def states_kernel(nheads, width, decay_ref, q_ref, k_ref, v_ref, g_ref, token_ref, sent_ref, held_ref, logs_ref):
    span = q_ref.shape[0]
    tri = triangle(span).astype(F32).astype(BF16)
    cum = sum(contract(tri, part, 1, 1) for part in thirds(decay_ref[...]))
    rows = nheads * width
    row = lax.broadcasted_iota(jnp.int32, (8, width), 0)
    totals = jnp.zeros((8, width), F32)
    for h in range(nheads):
        cols = slice(h * width, (h + 1) * width)
        cum_h = cum[:, h : h + 1]
        last = cum[span - 1 : span, h : h + 1]
        key_w = (k_ref[:, cols].astype(F32) * jnp.exp(last - cum_h)).astype(BF16)
        query_w = (q_ref[:, cols].astype(F32) * jnp.exp(cum_h)).astype(BF16)
        state = contract(key_w, v_ref[:, cols], 0, 0)
        grad = contract(query_w, g_ref[:, cols], 0, 0)
        held_ref[h * width : (h + 1) * width, :] = state
        held_ref[rows + h * width : rows + (h + 1) * width, :] = grad
        sent_ref[h * width : (h + 1) * width, :] = state.astype(BF16)
        sent_ref[rows + h * width : rows + (h + 1) * width, :] = grad.astype(BF16)
        totals = jnp.where(row == h, jnp.broadcast_to(last, (8, width)), totals)
    high = totals.astype(BF16).astype(F32)
    sent_ref[2 * rows :, :] = jnp.concatenate([high, totals - high]).astype(BF16)
    logs_ref[0:8, :] = totals
    logs_ref[8:24, :] = jnp.zeros((16, width), F32)


def step_kernel(nheads, width, hop, first, final_next, got_ref, held_ref, logs_ref, *refs):
    if first:
        sent_ref, held_out, logs_out, enter_out = refs
    else:
        enter_ref, sent_ref, held_out, logs_out, enter_out = refs
    rows = nheads * width
    up = upper_half(hop)
    low = 1.0 - up
    tail = got_ref[2 * rows :, :].astype(F32)
    got_total = tail[0:8] + tail[8:16]
    total, before, after = logs_ref[0:8, :], logs_ref[8:16, :], logs_ref[16:24, :]
    own_decay, got_decay = jnp.exp(total), jnp.exp(got_total)
    from_before, from_after = up * jnp.exp(before), low * jnp.exp(after)
    total = total + got_total
    logs_out[0:8, :] = total
    logs_out[8:16, :] = before + up * got_total
    logs_out[16:24, :] = after + low * got_total
    if final_next:
        next_up = upper_half(2 * hop) > 0.5
    else:
        high = total.astype(BF16).astype(F32)
        sent_ref[2 * rows :, :] = jnp.concatenate([high, total - high]).astype(BF16)
    for h in range(nheads):
        one = slice(h * width, (h + 1) * width)
        two = slice(rows + h * width, rows + (h + 1) * width)
        got_state, got_grad = got_ref[one, :].astype(F32), got_ref[two, :].astype(F32)
        own, got = own_decay[h : h + 1, :], got_decay[h : h + 1, :]
        state = (up + low * got) * held_ref[one, :] + (up * own + low) * got_state
        grad = (low + up * got) * held_ref[two, :] + (low * own + up) * got_grad
        state_in = from_before[h : h + 1, :] * got_state
        grad_in = from_after[h : h + 1, :] * got_grad
        if not first:
            state_in = enter_ref[one, :] + state_in
            grad_in = enter_ref[two, :] + grad_in
        enter_out[one, :] = state_in
        enter_out[two, :] = grad_in
        held_out[one, :] = state
        held_out[two, :] = grad
        if final_next:
            sent_ref[one, :] = jnp.where(next_up, grad, state).astype(BF16)
        else:
            sent_ref[one, :] = state.astype(BF16)
            sent_ref[two, :] = grad.astype(BF16)


def local_kernel(nheads, width, decay_ref, q_ref, k_ref, v_ref, g_ref, out_ref):
    span = q_ref.shape[0]
    rows = nheads * width
    causal = triangle(span)
    tri = causal.astype(F32).astype(BF16)
    parts = thirds(decay_ref[...])
    cum = sum(contract(tri, part, 1, 1) for part in parts)
    cum_rows = sum(contract(part, tri, 1, 1) for part in parts)
    for h in range(nheads):
        cols = slice(h * width, (h + 1) * width)
        gap = cum[:, h : h + 1] - cum_rows[h : h + 1, :]
        decay = jnp.where(causal, jnp.exp(jnp.minimum(gap, 0.0)), 0.0)
        weighted = (contract(g_ref[:, cols], v_ref[:, cols], 1, 1) * decay).astype(BF16)
        out_ref[h * width : (h + 1) * width, :] = contract(k_ref[:, cols], weighted, 0, 1)
        out_ref[rows + h * width : rows + (h + 1) * width, :] = contract(
            q_ref[:, cols], weighted, 0, 0
        )


def carry_kernel(nheads, width, hop, decay_ref, v_ref, g_ref, got_ref, logs_ref, enter_ref, local_ref, out_ref):
    span = v_ref.shape[0]
    rows = nheads * width
    tri = triangle(span).astype(F32).astype(BF16)
    cum_rows = sum(contract(part, tri, 1, 1) for part in thirds(decay_ref[...]))
    up = upper_half(hop)
    low = 1.0 - up
    from_before = up * jnp.exp(logs_ref[8:16, :])
    from_after = low * jnp.exp(logs_ref[16:24, :])
    for h in range(nheads):
        cols = slice(h * width, (h + 1) * width)
        two = slice(rows + h * width, rows + (h + 1) * width)
        got = got_ref[cols, :].astype(F32)
        state_in = (enter_ref[cols, :] + from_before[h : h + 1, :] * got).astype(BF16)
        grad_in = (enter_ref[two, :] + from_after[h : h + 1, :] * got).astype(BF16)
        cum_h = cum_rows[h : h + 1, :]
        last = cum_h[:, span - 1 : span]
        dq = local_ref[cols, :] + contract(state_in, g_ref[:, cols], 1, 1) * jnp.exp(cum_h)
        dk = local_ref[two, :] + contract(grad_in, v_ref[:, cols], 1, 1) * jnp.exp(last - cum_h)
        out_ref[cols, :] = dq.astype(BF16)
        out_ref[two, :] = dk.astype(BF16)


def share_order(count):
    bits = []
    hop = 2
    while hop < count:
        bits.append(hop)
        hop *= 2
    return bits, bits[::-1]


def share_hop(held, number):
    count = lax.axis_size("seq")
    even, odd = share_order(count)
    even, odd = even + [1], odd + [1]
    pairs = [(i, i ^ (odd[number] if i % 2 else even[number])) for i in range(count)]
    return lax.ppermute(held, "seq", pairs)


def share_deltas(count):
    even, odd = share_order(count)

    def spread(order):
        out = [0]
        for hop in order:
            out = out + [d ^ hop for d in out]
        return out

    return tuple(
        spread(first) + [d ^ 1 for d in spread(second)] for first, second in ((even, odd), (odd, even))
    )


def pack_kernel(share, plan, wq_ref, wk_ref, *refs):
    count, nseq = lax.axis_size("head"), lax.axis_size("seq")
    mine, my_seq = lax.axis_index("head"), lax.axis_index("seq")
    odd = lax.rem(my_seq, 2)
    outs, sems = refs[: len(plan)], refs[len(plan)]
    copies = []
    for i, (even_shift, odd_shift, many) in enumerate(plan):
        shift = even_shift + odd * (odd_shift - even_shift)
        block = lax.rem(mine + shift, count) * nseq + my_seq // many * many
        rows = pl.ds(pl.multiple_of(block * share, 16), many * share)
        for j, src in enumerate((wq_ref, wk_ref)):
            copies.append(
                pltpu.make_async_copy(
                    src.at[rows, :], outs[i].at[pl.ds(j * many * share, many * share), :], sems.at[i, j]
                )
            )
    for copy in copies:
        copy.start()
    for copy in copies:
        copy.wait()


def pack_weights(w_query, w_key, plan, share, pad=0):
    wide = w_query.shape[1]
    if share % 16:
        count, nseq = lax.axis_size("head"), lax.axis_size("seq")
        mine, my_seq = lax.axis_index("head"), lax.axis_index("seq")
        out = []
        for even_shift, odd_shift, many in plan:
            shift = jnp.where(my_seq % 2 == 1, odd_shift, even_shift)
            start = ((mine + shift) % count * nseq + my_seq // many * many) * share
            out.append(
                jnp.concatenate(
                    [lax.dynamic_slice_in_dim(w, start, many * share, 0) for w in (w_query, w_key)]
                )
            )
        return out
    heights = [2 * many * share for _, _, many in plan]
    heights[-1] += pad
    return call(
        functools.partial(pack_kernel, share, tuple(plan)),
        [jax.ShapeDtypeStruct((height, wide), BF16) for height in heights],
        0, sum(heights) * wide * 4,
        *(pltpu.with_memory_space_constraint(w, pltpu.HBM) for w in (w_query, w_key)),
        in_specs=[pl.BlockSpec(memory_space=pl.ANY)] * 2,
        out_specs=[pl.BlockSpec(memory_space=pltpu.VMEM)] * len(plan),
        scratch_shapes=[pltpu.SemaphoreType.DMA((len(plan), 2))],
    )


def join_kernel(groups, nargs, *refs):
    for group, out_ref in zip(groups, refs[-len(groups) :]):
        at = 0
        for i, start, size in group:
            out_ref[at : at + size, :] = refs[i][start : start + size, :]
            at += size


def join(*groups, tokens=()):
    args, spec = [], []
    for group in groups:
        spec.append(tuple((place_in(args, x), start, size) for x, start, size in group))
    return call(
        functools.partial(join_kernel, tuple(spec), len(args)),
        [jax.ShapeDtypeStruct((sum(size for _, _, size in group), args[0].shape[1]), BF16) for group in spec],
        0, 0, *args, *tokens,
        in_specs=[pl.BlockSpec(memory_space=pltpu.VMEM)] * len(args)
        + [pl.BlockSpec(memory_space=pl.ANY)] * len(tokens),
        out_specs=[pl.BlockSpec(memory_space=pltpu.VMEM)] * len(groups),
    )


def place_in(args, x):
    for i, y in enumerate(args):
        if y is x:
            return i
    args.append(x)
    return len(args) - 1


def rows_of(refs, low, high):
    parts, at = [], 0
    for ref in refs:
        first, last = max(low, at), min(high, at + ref.shape[0])
        if first < last:
            parts.append(ref[first - at : last - at, :])
        at += ref.shape[0]
    return parts[0] if len(parts) == 1 else jnp.concatenate(parts)


def row_block(weights, grads):
    share = weights.shape[0] // 2
    return contract(jnp.concatenate([weights[:share], weights[share:]], axis=1), grads, 1, 0)


def own_kernel(wq_ref, wk_ref, grads_ref, out_ref, near_q, near_k, sems):
    chunk, wide = near_q.shape
    rows = pl.ds(pl.multiple_of(lax.axis_index("head") * chunk, 16), chunk)
    copies = [
        pltpu.make_async_copy(src.at[rows, :], dst, sems.at[i])
        for i, (src, dst) in enumerate(((wq_ref, near_q), (wk_ref, near_k)))
    ]
    for copy in copies:
        copy.start()
    for copy in copies:
        copy.wait()
    out_ref[...] = contract(near_q[...], grads_ref[:wide, :], 1, 0) + contract(
        near_k[...], grads_ref[wide:, :], 1, 0
    )


def own_product(w_query, w_key, grads, chunk):
    wide = w_query.shape[1]
    return call(
        own_kernel, jax.ShapeDtypeStruct((chunk, grads.shape[1]), F32),
        4 * chunk * grads.shape[1] * wide, chunk * wide * 4,
        *(pltpu.with_memory_space_constraint(w, pltpu.HBM) for w in (w_query, w_key)), grads,
        in_specs=[pl.BlockSpec(memory_space=pl.ANY)] * 2 + [pl.BlockSpec(memory_space=pltpu.VMEM)],
        out_specs=pl.BlockSpec(memory_space=pltpu.VMEM),
        scratch_shapes=[pltpu.VMEM((chunk, wide), BF16)] * 2 + [pltpu.SemaphoreType.DMA((2,))],
    )


def relay_kernel(own_ref, lower_ref, upper_ref, token_ref, relay_ref, kept_ref, sent_ref):
    mine, odd = lax.axis_index("head"), lax.rem(lax.axis_index("seq"), 2)

    @pl.when(mine == 1)
    def _():
        relay_ref[...] = upper_ref[...]

    @pl.when(mine == 2)
    def _():
        relay_ref[...] = lower_ref[...]

    @pl.when((mine != 1) & (mine != 2))
    def _():
        relay_ref[...] = own_ref[...]

    @pl.when(odd == 0)
    def _():
        kept_ref[...] = lower_ref[...]
        sent_ref[...] = upper_ref[...]

    @pl.when(odd == 1)
    def _():
        kept_ref[...] = upper_ref[...]
        sent_ref[...] = lower_ref[...]


def split_kernel(both_ref, token_ref, theirs_ref):
    odd = lax.rem(lax.axis_index("seq"), 2)
    share = theirs_ref.shape[0] // 2
    for parity in range(2):

        @pl.when(odd == parity)
        def _():
            for j in range(2):
                at = (2 * j + 1 - parity) * share
                theirs_ref[j * share : (j + 1) * share, :] = both_ref[at : at + share, :]


def pick_kernel(both_ref, got_ref, out_ref):
    odd = lax.rem(lax.axis_index("seq"), 2)
    upper = lax.axis_index("head") // 2
    share = out_ref.shape[0] // 2

    @pl.when(odd != upper)
    def _():
        out_ref[...] = got_ref[...]

    for parity in range(2):

        @pl.when((odd == parity) & (upper == parity))
        def _():
            for j in range(2):
                at = (2 * j + parity) * share
                out_ref[j * share : (j + 1) * share, :] = both_ref[at : at + share, :]


def pair_kernel(count, table_ref, total_ref, *refs):
    weights, (kept_ref, got_ref), (out_ref, head_ref, tail_ref) = refs[:count], refs[count : count + 2], refs[count + 2 :]
    nblocks = table_ref.shape[0]
    size = out_ref.shape[0] // nblocks
    split = head_ref.shape[0] // size
    span = out_ref.shape[1]
    grads = jnp.concatenate([kept_ref[...], got_ref[...]], axis=1)
    for j in range(nblocks):
        both = row_block(rows_of(weights, 2 * size * j, 2 * size * (j + 1)), grads)
        place = table_ref[j]
        rows = pl.ds(pl.multiple_of(place * size, 16), size)
        out_ref[rows, :] = total_ref[rows, :] + both[:, :span]
        sent = both[:, span:].astype(BF16)

        @pl.when(place < split)
        def _(sent=sent, place=place):
            head_ref[pl.ds(pl.multiple_of(place * size, 16), size), :] = sent

        @pl.when(place >= split)
        def _(sent=sent, place=place):
            tail_ref[pl.ds(pl.multiple_of((place - split) * size, 16), size), :] = sent


def pair_product(table, total, weights, kept, got, split):
    chunk, span = total.shape
    return call(
        functools.partial(pair_kernel, len(weights)),
        (
            jax.ShapeDtypeStruct((chunk, span), F32),
            jax.ShapeDtypeStruct((split, span), BF16),
            jax.ShapeDtypeStruct((chunk - split, span), BF16),
        ),
        4 * chunk * span * kept.shape[0], chunk * span * 10,
        table, total, *weights, kept, got,
        in_specs=[pl.BlockSpec(memory_space=pltpu.SMEM)]
        + [pl.BlockSpec(memory_space=pltpu.VMEM)] * (3 + len(weights)),
        out_specs=[pl.BlockSpec(memory_space=pltpu.VMEM)] * 3,
        vmem=24 * 1024 * 1024,
    )


def add_kernel(blocks, base, low, high, plus, table_ref, total_ref, grads_ref, *refs):
    args, out_ref = refs[:-1], refs[-1]
    nshares = table_ref.shape[0]
    share = out_ref.shape[0] // nshares
    for j in range(nshares):
        rows = pl.ds(pl.multiple_of(table_ref[j] * share, 8), share)
        total = total_ref[rows, :]
        if plus:
            head, tail = (args[i] for i in plus)
            split, place = head.shape[0] // share, table_ref[j]
            from_head = head[pl.ds(pl.multiple_of(jnp.minimum(place, split - 1) * share, 16), share), :]
            from_tail = tail[pl.ds(pl.multiple_of(jnp.maximum(place - split, 0) * share, 16), share), :]
            total = total + jnp.where(place < split, from_head, from_tail).astype(F32)
        if low <= j < high:
            weights = rows_of([args[i] for i in blocks], 2 * share * (j - base), 2 * share * (j + 1 - base))
            total = total + row_block(weights, grads_ref[...])
        out_ref[rows, :] = total.astype(out_ref.dtype)


def add_product(table, total, blocks, grads, last, plus=(), base=0, low=0, high=None):
    chunk, span = total.shape
    args = []
    blocks = tuple(place_in(args, x) for x in blocks)
    plus = tuple(place_in(args, x) for x in plus)
    high = table.shape[0] if high is None else high
    return call(
        functools.partial(add_kernel, blocks, base, low, high, plus),
        jax.ShapeDtypeStruct((chunk, span), BF16 if last else F32),
        2 * chunk * span * grads.shape[0], chunk * span * 8,
        table, total, grads, *args,
        in_specs=[pl.BlockSpec(memory_space=pltpu.SMEM)]
        + [pl.BlockSpec(memory_space=pltpu.VMEM)] * (2 + len(args)),
        out_specs=pl.BlockSpec(memory_space=pltpu.VMEM),
        vmem=24 * 1024 * 1024,
    )


def shards(query_act, key_act, value_act, grad_output, log_decay, w_query, w_key):
    span = query_act.shape[0]
    nheads = log_decay.shape[1]
    width = query_act.shape[1] // nheads
    nseq, nhead = lax.axis_size("seq"), lax.axis_size("head")
    my_seq, my_head = lax.axis_index("seq"), lax.axis_index("head")
    chunk = w_query.shape[0] // nhead
    share = chunk // nseq
    rows = nheads * width

    shifts = [1, nhead - 1] + list(range(2, nhead - 1))
    ring = {k: [(i, (i + k) % nhead) for i in range(nhead)] for k in shifts}
    fast = nhead == 4 and nseq == 8
    if fast:
        packed = pack_weights(w_query, w_key, [(1, 3, 2), (2, 2, 2)], share)

        def moves(even, odd):
            return [
                (i * nhead + j, i * nhead + k) for i in range(nseq) for j, k in (odd if i % 2 else even)
            ]

        axes = ("seq", "head")
        first = lax.ppermute(packed[0], axes, moves(ring[1], ring[3]))
        passing = lax.ppermute(packed[1], axes, moves([(3, 2), (2, 1)], [(0, 1), (1, 2)]))
    else:
        packed = pack_weights(w_query, w_key, [(k, k, 1) for k in shifts], share)
        pieces = [lax.ppermute(p, "head", ring[k]) for p, k in zip(packed, shifts)]

    decay = log_decay.T
    sent, held, logs = call(
        functools.partial(states_kernel, nheads, width),
        (
            jax.ShapeDtypeStruct((2 * rows + 16, width), BF16),
            jax.ShapeDtypeStruct((2 * rows, width), F32),
            jax.ShapeDtypeStruct((24, width), F32),
        ),
        4 * span * rows * width, 8 * span * rows,
        decay, query_act, key_act, value_act, grad_output, packed[0],
        in_specs=[pl.BlockSpec(memory_space=pltpu.VMEM)] * 5 + [pl.BlockSpec(memory_space=pl.ANY)],
    )
    local = call(
        functools.partial(local_kernel, nheads, width),
        jax.ShapeDtypeStruct((2 * rows, span), F32),
        6 * span * span * rows, 16 * span * rows,
        decay, query_act, key_act, value_act, grad_output,
    )
    hop, enter = 1, None
    while True:
        got = lax.ppermute(sent, "seq", [(i, i ^ hop) for i in range(nseq)])
        if 2 * hop >= nseq:
            break
        final_next = 4 * hop >= nseq
        out_shape = (
            jax.ShapeDtypeStruct((rows if final_next else 2 * rows + 16, width), BF16),
            jax.ShapeDtypeStruct((2 * rows, width), F32),
            jax.ShapeDtypeStruct((24, width), F32),
            jax.ShapeDtypeStruct((2 * rows, width), F32),
        )
        args = [got, held, logs] + ([] if enter is None else [enter])
        sent, held, logs, enter = call(
            functools.partial(step_kernel, nheads, width, hop, enter is None, final_next),
            out_shape, 10 * rows * width, 16 * rows * width, *args,
        )
        hop *= 2
    both = call(
        functools.partial(carry_kernel, nheads, width, hop),
        jax.ShapeDtypeStruct((2 * rows, span), BF16),
        4 * span * rows * width, 16 * span * rows,
        decay, value_act, grad_output, got, logs, enter, local,
    )

    even, odd = share_deltas(nseq)
    deltas = jnp.where(my_seq % 2 == 1, jnp.array(odd, jnp.int32), jnp.array(even, jnp.int32))
    table = deltas ^ my_seq
    total = own_product(w_query, w_key, both, chunk)

    if fast:
        one, two = 2 * share, 4 * share
        (first,) = gate([first], [both])
        second = share_hop(first, 0)
        (near,) = join(((first, 0, two), (second, 0, two)))
        blocks = [near, share_hop(near, 1)]
        (ready,) = gate([both], [total])
        p1 = lax.ppermute(ready, "head", ring[1])
        p3 = lax.ppermute(ready, "head", ring[3])
        (passing,) = gate([passing], [first])
        passing = lax.ppermute(passing, axes, moves([(2, 1), (1, 0)], [(1, 2), (2, 3)]))
        theirs = call(
            split_kernel, jax.ShapeDtypeStruct((one, passing.shape[1]), BF16), 0, 0, passing, total,
            in_specs=[pl.BlockSpec(memory_space=pltpu.VMEM), pl.BlockSpec(memory_space=pl.ANY)],
            out_specs=pl.BlockSpec(memory_space=pltpu.VMEM),
        )
        theirs = lax.ppermute(
            theirs, axes,
            [(i * nhead + j, (i ^ 1) * nhead + j) for i in range(nseq) for j in range(nhead) if (j >= 2) == (i % 2)],
        )
        third = call(
            pick_kernel, jax.ShapeDtypeStruct(theirs.shape, BF16), 0, 0, passing, theirs,
            in_specs=[pl.BlockSpec(memory_space=pltpu.VMEM)] * 2,
            out_specs=pl.BlockSpec(memory_space=pltpu.VMEM),
        )
        fourth, fifth = share_hop(third, 0), share_hop(third, 1)
        fourth, fifth = gate([fourth, fifth])
        sixth = share_hop(fourth, 1)
        (early,) = join(((third, 0, one), (fourth, 0, one), (fifth, 0, CUT)))
        relay, kept, handed = call(
            relay_kernel, [jax.ShapeDtypeStruct(both.shape, BF16)] * 3, 0, 0, ready, p1, p3, total,
            in_specs=[pl.BlockSpec(memory_space=pltpu.VMEM)] * 3 + [pl.BlockSpec(memory_space=pl.ANY)],
            out_specs=[pl.BlockSpec(memory_space=pltpu.VMEM)] * 3,
        )
        p2 = lax.ppermute(relay, "head", [(0, 2), (1, 0), (2, 3), (3, 1)])
        got = share_hop(handed, 2)
        total, *handed = pair_product(table[: nseq // 2] // 2, total, blocks, kept, got, SPLIT)
        got = [share_hop(x, 2) for x in handed]
        (late,) = join(((fifth, CUT, one - CUT), (sixth, 0, one)), tokens=[p2])
        early, late = share_hop(early, 2), share_hop(late, 2)
        total = add_product(table, total, (third, fourth, fifth, sixth, early), p2, False, high=6)
        return add_product(table, total, (early, late), p2, True, plus=got, base=4, low=6)

    gathered = lax.all_gather(both, "head")
    for i, k in enumerate(shifts):
        held = [pieces[i]]
        for number in range(len(share_order(nseq)[0]) + 1):
            whole = held[0] if number == 0 else jnp.concatenate(held)
            held = [whole, share_hop(whole, number)]
        grads = gathered[(my_head + nhead - k) % nhead]
        total = add_product(table, total, held, grads, i == nhead - 2)
    return total


def solution(mesh):
    placed = (
        P("seq", "head"),
        P("seq", "head"),
        P("seq", "head"),
        P("seq", "head"),
        P("seq", "head"),
        P(None, "head"),
        P(None, "head"),
    )
    return jax.shard_map(
        shards, mesh=mesh, in_specs=placed, out_specs=P("head", "seq"), check_vma=False
    )
```

```python
import functools

import jax
import jax.numpy as jnp
from jax import lax
from jax.experimental import pallas as pl
from jax.experimental.pallas import tpu as pltpu
from jax.sharding import PartitionSpec as P

F32 = jnp.float32
BF16 = jnp.bfloat16
VMEM_BYTES = 10 * 1024 * 1024
CUT = 144
SPLIT = 1152


def contract(a, b, left, right):
    return lax.dot_general(a, b, (((left,), (right,)), ((), ())), preferred_element_type=F32)


def call(kernel, out_shape, flops, nbytes, *args, aliases=None, vmem=VMEM_BYTES, **spec):
    return pl.pallas_call(
        kernel,
        out_shape=out_shape,
        cost_estimate=pl.CostEstimate(flops=flops, bytes_accessed=nbytes, transcendentals=0),
        compiler_params=pltpu.CompilerParams(vmem_limit_bytes=vmem),
        input_output_aliases=aliases or {},
        **spec,
    )(*args)


def gate_kernel(count, *refs):
    del count, refs


def gate(passed, tokens=(), flops=0):
    return call(
        functools.partial(gate_kernel, len(passed)),
        [jax.ShapeDtypeStruct(x.shape, x.dtype) for x in passed],
        flops, 0, *passed, *tokens,
        aliases={i: i for i in range(len(passed))},
        in_specs=[pl.BlockSpec(memory_space=pl.ANY)] * (len(passed) + len(tokens)),
        out_specs=[pl.BlockSpec(memory_space=pl.ANY)] * len(passed),
    )


def thirds(x):
    high = x.astype(BF16)
    rest = x - high.astype(F32)
    middle = rest.astype(BF16)
    return high, middle, (rest - middle.astype(F32)).astype(BF16)


def triangle(span):
    rows = lax.broadcasted_iota(jnp.int32, (span, span), 0)
    cols = lax.broadcasted_iota(jnp.int32, (span, span), 1)
    return rows >= cols


def upper_half(hop):
    return ((lax.axis_index("seq") // hop) % 2).astype(F32)


def states_kernel(nheads, width, decay_ref, q_ref, k_ref, v_ref, g_ref, token_ref, sent_ref, held_ref, logs_ref):
    span = q_ref.shape[0]
    tri = triangle(span).astype(F32).astype(BF16)
    cum = sum(contract(tri, part, 1, 1) for part in thirds(decay_ref[...]))
    rows = nheads * width
    row = lax.broadcasted_iota(jnp.int32, (8, width), 0)
    totals = jnp.zeros((8, width), F32)
    for h in range(nheads):
        cols = slice(h * width, (h + 1) * width)
        cum_h = cum[:, h : h + 1]
        last = cum[span - 1 : span, h : h + 1]
        key_w = (k_ref[:, cols].astype(F32) * jnp.exp(last - cum_h)).astype(BF16)
        query_w = (q_ref[:, cols].astype(F32) * jnp.exp(cum_h)).astype(BF16)
        state = contract(key_w, v_ref[:, cols], 0, 0)
        grad = contract(query_w, g_ref[:, cols], 0, 0)
        held_ref[h * width : (h + 1) * width, :] = state
        held_ref[rows + h * width : rows + (h + 1) * width, :] = grad
        sent_ref[h * width : (h + 1) * width, :] = state.astype(BF16)
        sent_ref[rows + h * width : rows + (h + 1) * width, :] = grad.astype(BF16)
        totals = jnp.where(row == h, jnp.broadcast_to(last, (8, width)), totals)
    high = totals.astype(BF16).astype(F32)
    sent_ref[2 * rows :, :] = jnp.concatenate([high, totals - high]).astype(BF16)
    logs_ref[0:8, :] = totals
    logs_ref[8:24, :] = jnp.zeros((16, width), F32)


def step_kernel(nheads, width, hop, first, final_next, got_ref, held_ref, logs_ref, *refs):
    if first:
        sent_ref, held_out, logs_out, enter_out = refs
    else:
        enter_ref, sent_ref, held_out, logs_out, enter_out = refs
    rows = nheads * width
    up = upper_half(hop)
    low = 1.0 - up
    tail = got_ref[2 * rows :, :].astype(F32)
    got_total = tail[0:8] + tail[8:16]
    total, before, after = logs_ref[0:8, :], logs_ref[8:16, :], logs_ref[16:24, :]
    own_decay, got_decay = jnp.exp(total), jnp.exp(got_total)
    from_before, from_after = up * jnp.exp(before), low * jnp.exp(after)
    total = total + got_total
    logs_out[0:8, :] = total
    logs_out[8:16, :] = before + up * got_total
    logs_out[16:24, :] = after + low * got_total
    if final_next:
        next_up = upper_half(2 * hop) > 0.5
    else:
        high = total.astype(BF16).astype(F32)
        sent_ref[2 * rows :, :] = jnp.concatenate([high, total - high]).astype(BF16)
    for h in range(nheads):
        one = slice(h * width, (h + 1) * width)
        two = slice(rows + h * width, rows + (h + 1) * width)
        got_state, got_grad = got_ref[one, :].astype(F32), got_ref[two, :].astype(F32)
        own, got = own_decay[h : h + 1, :], got_decay[h : h + 1, :]
        state = (up + low * got) * held_ref[one, :] + (up * own + low) * got_state
        grad = (low + up * got) * held_ref[two, :] + (low * own + up) * got_grad
        state_in = from_before[h : h + 1, :] * got_state
        grad_in = from_after[h : h + 1, :] * got_grad
        if not first:
            state_in = enter_ref[one, :] + state_in
            grad_in = enter_ref[two, :] + grad_in
        enter_out[one, :] = state_in
        enter_out[two, :] = grad_in
        held_out[one, :] = state
        held_out[two, :] = grad
        if final_next:
            sent_ref[one, :] = jnp.where(next_up, grad, state).astype(BF16)
        else:
            sent_ref[one, :] = state.astype(BF16)
            sent_ref[two, :] = grad.astype(BF16)


def local_kernel(nheads, width, decay_ref, q_ref, k_ref, v_ref, g_ref, out_ref):
    span = q_ref.shape[0]
    rows = nheads * width
    causal = triangle(span)
    tri = causal.astype(F32).astype(BF16)
    parts = thirds(decay_ref[...])
    cum = sum(contract(tri, part, 1, 1) for part in parts)
    cum_rows = sum(contract(part, tri, 1, 1) for part in parts)
    for h in range(nheads):
        cols = slice(h * width, (h + 1) * width)
        gap = cum[:, h : h + 1] - cum_rows[h : h + 1, :]
        decay = jnp.where(causal, jnp.exp(jnp.minimum(gap, 0.0)), 0.0)
        weighted = (contract(g_ref[:, cols], v_ref[:, cols], 1, 1) * decay).astype(BF16)
        out_ref[h * width : (h + 1) * width, :] = contract(k_ref[:, cols], weighted, 0, 1)
        out_ref[rows + h * width : rows + (h + 1) * width, :] = contract(
            q_ref[:, cols], weighted, 0, 0
        )


def carry_kernel(nheads, width, hop, decay_ref, v_ref, g_ref, got_ref, logs_ref, enter_ref, local_ref, out_ref):
    span = v_ref.shape[0]
    rows = nheads * width
    tri = triangle(span).astype(F32).astype(BF16)
    cum_rows = sum(contract(part, tri, 1, 1) for part in thirds(decay_ref[...]))
    up = upper_half(hop)
    low = 1.0 - up
    from_before = up * jnp.exp(logs_ref[8:16, :])
    from_after = low * jnp.exp(logs_ref[16:24, :])
    for h in range(nheads):
        cols = slice(h * width, (h + 1) * width)
        two = slice(rows + h * width, rows + (h + 1) * width)
        got = got_ref[cols, :].astype(F32)
        state_in = (enter_ref[cols, :] + from_before[h : h + 1, :] * got).astype(BF16)
        grad_in = (enter_ref[two, :] + from_after[h : h + 1, :] * got).astype(BF16)
        cum_h = cum_rows[h : h + 1, :]
        last = cum_h[:, span - 1 : span]
        dq = local_ref[cols, :] + contract(state_in, g_ref[:, cols], 1, 1) * jnp.exp(cum_h)
        dk = local_ref[two, :] + contract(grad_in, v_ref[:, cols], 1, 1) * jnp.exp(last - cum_h)
        out_ref[cols, :] = dq.astype(BF16)
        out_ref[two, :] = dk.astype(BF16)


def share_order(count):
    bits = []
    hop = 2
    while hop < count:
        bits.append(hop)
        hop *= 2
    return bits, bits[::-1]


def share_hop(held, number):
    count = lax.axis_size("seq")
    even, odd = share_order(count)
    even, odd = even + [1], odd + [1]
    pairs = [(i, i ^ (odd[number] if i % 2 else even[number])) for i in range(count)]
    return lax.ppermute(held, "seq", pairs)


def share_deltas(count):
    even, odd = share_order(count)

    def spread(order):
        out = [0]
        for hop in order:
            out = out + [d ^ hop for d in out]
        return out

    return tuple(
        spread(first) + [d ^ 1 for d in spread(second)] for first, second in ((even, odd), (odd, even))
    )


def pack_kernel(share, plan, wq_ref, wk_ref, *refs):
    count, nseq = lax.axis_size("head"), lax.axis_size("seq")
    mine, my_seq = lax.axis_index("head"), lax.axis_index("seq")
    odd = lax.rem(my_seq, 2)
    outs, sems = refs[: len(plan)], refs[len(plan)]
    copies = []
    for i, (even_shift, odd_shift, many) in enumerate(plan):
        shift = even_shift + odd * (odd_shift - even_shift)
        block = lax.rem(mine + shift, count) * nseq + my_seq // many * many
        rows = pl.ds(pl.multiple_of(block * share, 16), many * share)
        for j, src in enumerate((wq_ref, wk_ref)):
            copies.append(
                pltpu.make_async_copy(
                    src.at[rows, :], outs[i].at[pl.ds(j * many * share, many * share), :], sems.at[i, j]
                )
            )
    for copy in copies:
        copy.start()
    for copy in copies:
        copy.wait()


def pack_weights(w_query, w_key, plan, share, pad=0):
    wide = w_query.shape[1]
    if share % 16:
        count, nseq = lax.axis_size("head"), lax.axis_size("seq")
        mine, my_seq = lax.axis_index("head"), lax.axis_index("seq")
        out = []
        for even_shift, odd_shift, many in plan:
            shift = jnp.where(my_seq % 2 == 1, odd_shift, even_shift)
            start = ((mine + shift) % count * nseq + my_seq // many * many) * share
            out.append(
                jnp.concatenate(
                    [lax.dynamic_slice_in_dim(w, start, many * share, 0) for w in (w_query, w_key)]
                )
            )
        return out
    heights = [2 * many * share for _, _, many in plan]
    heights[-1] += pad
    return call(
        functools.partial(pack_kernel, share, tuple(plan)),
        [jax.ShapeDtypeStruct((height, wide), BF16) for height in heights],
        0, sum(heights) * wide * 4,
        *(pltpu.with_memory_space_constraint(w, pltpu.HBM) for w in (w_query, w_key)),
        in_specs=[pl.BlockSpec(memory_space=pl.ANY)] * 2,
        out_specs=[pl.BlockSpec(memory_space=pltpu.VMEM)] * len(plan),
        scratch_shapes=[pltpu.SemaphoreType.DMA((len(plan), 2))],
    )


def join_kernel(groups, nargs, *refs):
    for group, out_ref in zip(groups, refs[-len(groups) :]):
        at = 0
        for i, start, size in group:
            out_ref[at : at + size, :] = refs[i][start : start + size, :]
            at += size


def join(*groups, tokens=()):
    args, spec = [], []
    for group in groups:
        spec.append(tuple((place_in(args, x), start, size) for x, start, size in group))
    return call(
        functools.partial(join_kernel, tuple(spec), len(args)),
        [jax.ShapeDtypeStruct((sum(size for _, _, size in group), args[0].shape[1]), BF16) for group in spec],
        0, 0, *args, *tokens,
        in_specs=[pl.BlockSpec(memory_space=pltpu.VMEM)] * len(args)
        + [pl.BlockSpec(memory_space=pl.ANY)] * len(tokens),
        out_specs=[pl.BlockSpec(memory_space=pltpu.VMEM)] * len(groups),
    )


def place_in(args, x):
    for i, y in enumerate(args):
        if y is x:
            return i
    args.append(x)
    return len(args) - 1


def rows_of(refs, low, high):
    parts, at = [], 0
    for ref in refs:
        first, last = max(low, at), min(high, at + ref.shape[0])
        if first < last:
            parts.append(ref[first - at : last - at, :])
        at += ref.shape[0]
    return parts[0] if len(parts) == 1 else jnp.concatenate(parts)


def row_block(weights, grads):
    share = weights.shape[0] // 2
    return contract(jnp.concatenate([weights[:share], weights[share:]], axis=1), grads, 1, 0)


def own_kernel(wq_ref, wk_ref, grads_ref, out_ref, near_q, near_k, sems):
    chunk, wide = near_q.shape
    rows = pl.ds(pl.multiple_of(lax.axis_index("head") * chunk, 16), chunk)
    copies = [
        pltpu.make_async_copy(src.at[rows, :], dst, sems.at[i])
        for i, (src, dst) in enumerate(((wq_ref, near_q), (wk_ref, near_k)))
    ]
    for copy in copies:
        copy.start()
    for copy in copies:
        copy.wait()
    out_ref[...] = contract(near_q[...], grads_ref[:wide, :], 1, 0) + contract(
        near_k[...], grads_ref[wide:, :], 1, 0
    )


def own_product(w_query, w_key, grads, chunk):
    wide = w_query.shape[1]
    return call(
        own_kernel, jax.ShapeDtypeStruct((chunk, grads.shape[1]), F32),
        4 * chunk * grads.shape[1] * wide, chunk * wide * 4,
        *(pltpu.with_memory_space_constraint(w, pltpu.HBM) for w in (w_query, w_key)), grads,
        in_specs=[pl.BlockSpec(memory_space=pl.ANY)] * 2 + [pl.BlockSpec(memory_space=pltpu.VMEM)],
        out_specs=pl.BlockSpec(memory_space=pltpu.VMEM),
        scratch_shapes=[pltpu.VMEM((chunk, wide), BF16)] * 2 + [pltpu.SemaphoreType.DMA((2,))],
    )


def relay_kernel(own_ref, lower_ref, upper_ref, token_ref, relay_ref, kept_ref, sent_ref):
    mine, odd = lax.axis_index("head"), lax.rem(lax.axis_index("seq"), 2)

    @pl.when(mine == 1)
    def _():
        relay_ref[...] = upper_ref[...]

    @pl.when(mine == 2)
    def _():
        relay_ref[...] = lower_ref[...]

    @pl.when((mine != 1) & (mine != 2))
    def _():
        relay_ref[...] = own_ref[...]

    @pl.when(odd == 0)
    def _():
        kept_ref[...] = lower_ref[...]
        sent_ref[...] = upper_ref[...]

    @pl.when(odd == 1)
    def _():
        kept_ref[...] = upper_ref[...]
        sent_ref[...] = lower_ref[...]


def split_kernel(both_ref, token_ref, theirs_ref):
    odd = lax.rem(lax.axis_index("seq"), 2)
    share = theirs_ref.shape[0] // 2
    for parity in range(2):

        @pl.when(odd == parity)
        def _():
            for j in range(2):
                at = (2 * j + 1 - parity) * share
                theirs_ref[j * share : (j + 1) * share, :] = both_ref[at : at + share, :]


def pick_kernel(both_ref, got_ref, out_ref):
    odd = lax.rem(lax.axis_index("seq"), 2)
    upper = lax.axis_index("head") // 2
    share = out_ref.shape[0] // 2

    @pl.when(odd != upper)
    def _():
        out_ref[...] = got_ref[...]

    for parity in range(2):

        @pl.when((odd == parity) & (upper == parity))
        def _():
            for j in range(2):
                at = (2 * j + parity) * share
                out_ref[j * share : (j + 1) * share, :] = both_ref[at : at + share, :]


def pair_kernel(count, table_ref, total_ref, *refs):
    weights, (kept_ref, got_ref), (out_ref, head_ref, tail_ref) = refs[:count], refs[count : count + 2], refs[count + 2 :]
    nblocks = table_ref.shape[0]
    size = out_ref.shape[0] // nblocks
    split = head_ref.shape[0] // size
    span = out_ref.shape[1]
    grads = jnp.concatenate([kept_ref[...], got_ref[...]], axis=1)
    for j in range(nblocks):
        both = row_block(rows_of(weights, 2 * size * j, 2 * size * (j + 1)), grads)
        place = table_ref[j]
        rows = pl.ds(pl.multiple_of(place * size, 16), size)
        out_ref[rows, :] = total_ref[rows, :] + both[:, :span]
        sent = both[:, span:].astype(BF16)

        @pl.when(place < split)
        def _(sent=sent, place=place):
            head_ref[pl.ds(pl.multiple_of(place * size, 16), size), :] = sent

        @pl.when(place >= split)
        def _(sent=sent, place=place):
            tail_ref[pl.ds(pl.multiple_of((place - split) * size, 16), size), :] = sent


def pair_product(table, total, weights, kept, got, split):
    chunk, span = total.shape
    return call(
        functools.partial(pair_kernel, len(weights)),
        (
            jax.ShapeDtypeStruct((chunk, span), F32),
            jax.ShapeDtypeStruct((split, span), BF16),
            jax.ShapeDtypeStruct((chunk - split, span), BF16),
        ),
        0, 0,
        table, total, *weights, kept, got,
        in_specs=[pl.BlockSpec(memory_space=pltpu.SMEM)]
        + [pl.BlockSpec(memory_space=pltpu.VMEM)] * (3 + len(weights)),
        out_specs=[pl.BlockSpec(memory_space=pltpu.VMEM)] * 3,
        vmem=14 * 1024 * 1024,
    )


def add_kernel(blocks, base, low, high, plus, table_ref, total_ref, grads_ref, *refs):
    args, out_ref = refs[:-1], refs[-1]
    nshares = table_ref.shape[0]
    share = out_ref.shape[0] // nshares
    for j in range(nshares):
        rows = pl.ds(pl.multiple_of(table_ref[j] * share, 8), share)
        total = total_ref[rows, :]
        if plus:
            head, tail = (args[i] for i in plus)
            split, place = head.shape[0] // share, table_ref[j]
            from_head = head[pl.ds(pl.multiple_of(jnp.minimum(place, split - 1) * share, 16), share), :]
            from_tail = tail[pl.ds(pl.multiple_of(jnp.maximum(place - split, 0) * share, 16), share), :]
            total = total + jnp.where(place < split, from_head, from_tail).astype(F32)
        if low <= j < high:
            weights = rows_of([args[i] for i in blocks], 2 * share * (j - base), 2 * share * (j + 1 - base))
            total = total + row_block(weights, grads_ref[...])
        out_ref[rows, :] = total.astype(out_ref.dtype)


def add_product(table, total, blocks, grads, last, plus=(), base=0, low=0, high=None):
    chunk, span = total.shape
    args = []
    blocks = tuple(place_in(args, x) for x in blocks)
    plus = tuple(place_in(args, x) for x in plus)
    high = table.shape[0] if high is None else high
    return call(
        functools.partial(add_kernel, blocks, base, low, high, plus),
        jax.ShapeDtypeStruct((chunk, span), BF16 if last else F32),
        2 * chunk * span * grads.shape[0], chunk * span * 8,
        table, total, grads, *args,
        in_specs=[pl.BlockSpec(memory_space=pltpu.SMEM)]
        + [pl.BlockSpec(memory_space=pltpu.VMEM)] * (2 + len(args)),
        out_specs=pl.BlockSpec(memory_space=pltpu.VMEM),
        vmem=14 * 1024 * 1024,
    )


def shards(query_act, key_act, value_act, grad_output, log_decay, w_query, w_key):
    span = query_act.shape[0]
    nheads = log_decay.shape[1]
    width = query_act.shape[1] // nheads
    nseq, nhead = lax.axis_size("seq"), lax.axis_size("head")
    my_seq, my_head = lax.axis_index("seq"), lax.axis_index("head")
    chunk = w_query.shape[0] // nhead
    share = chunk // nseq
    rows = nheads * width

    shifts = [1, nhead - 1] + list(range(2, nhead - 1))
    ring = {k: [(i, (i + k) % nhead) for i in range(nhead)] for k in shifts}
    fast = nhead == 4 and nseq == 8
    if fast:
        packed = pack_weights(w_query, w_key, [(1, 3, 2), (2, 2, 2)], share)

        def moves(even, odd):
            return [
                (i * nhead + j, i * nhead + k) for i in range(nseq) for j, k in (odd if i % 2 else even)
            ]

        axes = ("seq", "head")
        first = lax.ppermute(packed[0], axes, moves(ring[1], ring[3]))
        passing = lax.ppermute(packed[1], axes, moves([(3, 2), (2, 1)], [(0, 1), (1, 2)]))
    else:
        packed = pack_weights(w_query, w_key, [(k, k, 1) for k in shifts], share)
        pieces = [lax.ppermute(p, "head", ring[k]) for p, k in zip(packed, shifts)]

    decay = log_decay.T
    sent, held, logs = call(
        functools.partial(states_kernel, nheads, width),
        (
            jax.ShapeDtypeStruct((2 * rows + 16, width), BF16),
            jax.ShapeDtypeStruct((2 * rows, width), F32),
            jax.ShapeDtypeStruct((24, width), F32),
        ),
        4 * span * rows * width, 8 * span * rows,
        decay, query_act, key_act, value_act, grad_output, packed[0],
        in_specs=[pl.BlockSpec(memory_space=pltpu.VMEM)] * 5 + [pl.BlockSpec(memory_space=pl.ANY)],
    )
    local = call(
        functools.partial(local_kernel, nheads, width),
        jax.ShapeDtypeStruct((2 * rows, span), F32),
        6 * span * span * rows, 16 * span * rows,
        decay, query_act, key_act, value_act, grad_output,
    )
    hop, enter = 1, None
    while True:
        got = lax.ppermute(sent, "seq", [(i, i ^ hop) for i in range(nseq)])
        if 2 * hop >= nseq:
            break
        final_next = 4 * hop >= nseq
        out_shape = (
            jax.ShapeDtypeStruct((rows if final_next else 2 * rows + 16, width), BF16),
            jax.ShapeDtypeStruct((2 * rows, width), F32),
            jax.ShapeDtypeStruct((24, width), F32),
            jax.ShapeDtypeStruct((2 * rows, width), F32),
        )
        args = [got, held, logs] + ([] if enter is None else [enter])
        sent, held, logs, enter = call(
            functools.partial(step_kernel, nheads, width, hop, enter is None, final_next),
            out_shape, 10 * rows * width, 16 * rows * width, *args,
        )
        hop *= 2
    both = call(
        functools.partial(carry_kernel, nheads, width, hop),
        jax.ShapeDtypeStruct((2 * rows, span), BF16),
        4 * span * rows * width, 16 * span * rows,
        decay, value_act, grad_output, got, logs, enter, local,
    )

    even, odd = share_deltas(nseq)
    deltas = jnp.where(my_seq % 2 == 1, jnp.array(odd, jnp.int32), jnp.array(even, jnp.int32))
    table = deltas ^ my_seq
    total = own_product(w_query, w_key, both, chunk)

    if fast:
        one, two = 2 * share, 4 * share
        (first,) = gate([first], [both])
        second = share_hop(first, 0)
        (near,) = join(((first, 0, two), (second, 0, two)))
        blocks = [near, share_hop(near, 1)]
        (ready,) = gate([both], [total])
        p1 = lax.ppermute(ready, "head", ring[1])
        p3 = lax.ppermute(ready, "head", ring[3])
        (passing,) = gate([passing], [first])
        passing = lax.ppermute(passing, axes, moves([(2, 1), (1, 0)], [(1, 2), (2, 3)]))
        theirs = call(
            split_kernel, jax.ShapeDtypeStruct((one, passing.shape[1]), BF16), 0, 0, passing, total,
            in_specs=[pl.BlockSpec(memory_space=pltpu.VMEM), pl.BlockSpec(memory_space=pl.ANY)],
            out_specs=pl.BlockSpec(memory_space=pltpu.VMEM),
        )
        theirs = lax.ppermute(
            theirs, axes,
            [(i * nhead + j, (i ^ 1) * nhead + j) for i in range(nseq) for j in range(nhead) if (j >= 2) == (i % 2)],
        )
        third = call(
            pick_kernel, jax.ShapeDtypeStruct(theirs.shape, BF16), 0, 0, passing, theirs,
            in_specs=[pl.BlockSpec(memory_space=pltpu.VMEM)] * 2,
            out_specs=pl.BlockSpec(memory_space=pltpu.VMEM),
        )
        fourth, fifth = share_hop(third, 0), share_hop(third, 1)
        fourth, fifth = gate([fourth, fifth])
        sixth = share_hop(fourth, 1)
        (early,) = join(((third, 0, one), (fourth, 0, one), (fifth, 0, CUT)))
        relay, kept, handed = call(
            relay_kernel, [jax.ShapeDtypeStruct(both.shape, BF16)] * 3, 0, 0, ready, p1, p3, total,
            in_specs=[pl.BlockSpec(memory_space=pltpu.VMEM)] * 3 + [pl.BlockSpec(memory_space=pl.ANY)],
            out_specs=[pl.BlockSpec(memory_space=pltpu.VMEM)] * 3,
        )
        p2 = lax.ppermute(relay, "head", [(0, 2), (1, 0), (2, 3), (3, 1)])
        got = share_hop(handed, 2)
        total, *handed = pair_product(table[: nseq // 2] // 2, total, blocks, kept, got, SPLIT)
        got = [share_hop(x, 2) for x in handed]
        (late,) = join(((fifth, CUT, one - CUT), (sixth, 0, one)), tokens=[p2])
        early, late = share_hop(early, 2), share_hop(late, 2)
        total = add_product(table, total, (third, fourth, fifth, sixth, early), p2, False, high=6)
        return add_product(table, total, (early, late), p2, True, plus=got, base=4, low=6)

    gathered = lax.all_gather(both, "head")
    for i, k in enumerate(shifts):
        held = [pieces[i]]
        for number in range(len(share_order(nseq)[0]) + 1):
            whole = held[0] if number == 0 else jnp.concatenate(held)
            held = [whole, share_hop(whole, number)]
        grads = gathered[(my_head + nhead - k) % nhead]
        total = add_product(table, total, held, grads, i == nhead - 2)
    return total


def solution(mesh):
    placed = (
        P("seq", "head"),
        P("seq", "head"),
        P("seq", "head"),
        P("seq", "head"),
        P("seq", "head"),
        P(None, "head"),
        P(None, "head"),
    )
    return jax.shard_map(
        shards, mesh=mesh, in_specs=placed, out_specs=P("head", "seq"), check_vma=False
    )
```

```python
import functools

import jax
import jax.numpy as jnp
from jax import lax
from jax.experimental import pallas as pl
from jax.experimental.pallas import tpu as pltpu
from jax.sharding import PartitionSpec as P

F32 = jnp.float32
BF16 = jnp.bfloat16
VMEM_BYTES = 10 * 1024 * 1024
CUT = 144
SPLIT = 1152


def contract(a, b, left, right):
    return lax.dot_general(a, b, (((left,), (right,)), ((), ())), preferred_element_type=F32)


def call(kernel, out_shape, flops, nbytes, *args, aliases=None, vmem=VMEM_BYTES, **spec):
    return pl.pallas_call(
        kernel,
        out_shape=out_shape,
        cost_estimate=pl.CostEstimate(flops=flops, bytes_accessed=nbytes, transcendentals=0),
        compiler_params=pltpu.CompilerParams(vmem_limit_bytes=vmem),
        input_output_aliases=aliases or {},
        **spec,
    )(*args)


def gate_kernel(count, *refs):
    del count, refs


def gate(passed, tokens=(), flops=0):
    return call(
        functools.partial(gate_kernel, len(passed)),
        [jax.ShapeDtypeStruct(x.shape, x.dtype) for x in passed],
        flops, 0, *passed, *tokens,
        aliases={i: i for i in range(len(passed))},
        in_specs=[pl.BlockSpec(memory_space=pl.ANY)] * (len(passed) + len(tokens)),
        out_specs=[pl.BlockSpec(memory_space=pl.ANY)] * len(passed),
    )


def thirds(x):
    high = x.astype(BF16)
    rest = x - high.astype(F32)
    middle = rest.astype(BF16)
    return high, middle, (rest - middle.astype(F32)).astype(BF16)


def triangle(span):
    rows = lax.broadcasted_iota(jnp.int32, (span, span), 0)
    cols = lax.broadcasted_iota(jnp.int32, (span, span), 1)
    return rows >= cols


def upper_half(hop):
    return ((lax.axis_index("seq") // hop) % 2).astype(F32)


def states_kernel(nheads, width, decay_ref, q_ref, k_ref, v_ref, g_ref, token_ref, sent_ref, held_ref, logs_ref):
    span = q_ref.shape[0]
    tri = triangle(span).astype(F32).astype(BF16)
    cum = sum(contract(tri, part, 1, 1) for part in thirds(decay_ref[...]))
    rows = nheads * width
    row = lax.broadcasted_iota(jnp.int32, (8, width), 0)
    totals = jnp.zeros((8, width), F32)
    for h in range(nheads):
        cols = slice(h * width, (h + 1) * width)
        cum_h = cum[:, h : h + 1]
        last = cum[span - 1 : span, h : h + 1]
        key_w = (k_ref[:, cols].astype(F32) * jnp.exp(last - cum_h)).astype(BF16)
        query_w = (q_ref[:, cols].astype(F32) * jnp.exp(cum_h)).astype(BF16)
        state = contract(key_w, v_ref[:, cols], 0, 0)
        grad = contract(query_w, g_ref[:, cols], 0, 0)
        held_ref[h * width : (h + 1) * width, :] = state
        held_ref[rows + h * width : rows + (h + 1) * width, :] = grad
        sent_ref[h * width : (h + 1) * width, :] = state.astype(BF16)
        sent_ref[rows + h * width : rows + (h + 1) * width, :] = grad.astype(BF16)
        totals = jnp.where(row == h, jnp.broadcast_to(last, (8, width)), totals)
    high = totals.astype(BF16).astype(F32)
    sent_ref[2 * rows :, :] = jnp.concatenate([high, totals - high]).astype(BF16)
    logs_ref[0:8, :] = totals
    logs_ref[8:24, :] = jnp.zeros((16, width), F32)


def step_kernel(nheads, width, hop, first, final_next, got_ref, held_ref, logs_ref, *refs):
    if first:
        sent_ref, held_out, logs_out, enter_out = refs
    else:
        enter_ref, sent_ref, held_out, logs_out, enter_out = refs
    rows = nheads * width
    up = upper_half(hop)
    low = 1.0 - up
    tail = got_ref[2 * rows :, :].astype(F32)
    got_total = tail[0:8] + tail[8:16]
    total, before, after = logs_ref[0:8, :], logs_ref[8:16, :], logs_ref[16:24, :]
    own_decay, got_decay = jnp.exp(total), jnp.exp(got_total)
    from_before, from_after = up * jnp.exp(before), low * jnp.exp(after)
    total = total + got_total
    logs_out[0:8, :] = total
    logs_out[8:16, :] = before + up * got_total
    logs_out[16:24, :] = after + low * got_total
    if final_next:
        next_up = upper_half(2 * hop) > 0.5
    else:
        high = total.astype(BF16).astype(F32)
        sent_ref[2 * rows :, :] = jnp.concatenate([high, total - high]).astype(BF16)
    for h in range(nheads):
        one = slice(h * width, (h + 1) * width)
        two = slice(rows + h * width, rows + (h + 1) * width)
        got_state, got_grad = got_ref[one, :].astype(F32), got_ref[two, :].astype(F32)
        own, got = own_decay[h : h + 1, :], got_decay[h : h + 1, :]
        state = (up + low * got) * held_ref[one, :] + (up * own + low) * got_state
        grad = (low + up * got) * held_ref[two, :] + (low * own + up) * got_grad
        state_in = from_before[h : h + 1, :] * got_state
        grad_in = from_after[h : h + 1, :] * got_grad
        if not first:
            state_in = enter_ref[one, :] + state_in
            grad_in = enter_ref[two, :] + grad_in
        enter_out[one, :] = state_in
        enter_out[two, :] = grad_in
        held_out[one, :] = state
        held_out[two, :] = grad
        if final_next:
            sent_ref[one, :] = jnp.where(next_up, grad, state).astype(BF16)
        else:
            sent_ref[one, :] = state.astype(BF16)
            sent_ref[two, :] = grad.astype(BF16)


def local_kernel(nheads, width, decay_ref, q_ref, k_ref, v_ref, g_ref, out_ref):
    span = q_ref.shape[0]
    rows = nheads * width
    causal = triangle(span)
    tri = causal.astype(F32).astype(BF16)
    parts = thirds(decay_ref[...])
    cum = sum(contract(tri, part, 1, 1) for part in parts)
    cum_rows = sum(contract(part, tri, 1, 1) for part in parts)
    for h in range(nheads):
        cols = slice(h * width, (h + 1) * width)
        gap = cum[:, h : h + 1] - cum_rows[h : h + 1, :]
        decay = jnp.where(causal, jnp.exp(jnp.minimum(gap, 0.0)), 0.0)
        weighted = (contract(g_ref[:, cols], v_ref[:, cols], 1, 1) * decay).astype(BF16)
        out_ref[h * width : (h + 1) * width, :] = contract(k_ref[:, cols], weighted, 0, 1)
        out_ref[rows + h * width : rows + (h + 1) * width, :] = contract(
            q_ref[:, cols], weighted, 0, 0
        )


def carry_kernel(nheads, width, hop, decay_ref, v_ref, g_ref, got_ref, logs_ref, enter_ref, local_ref, out_ref):
    span = v_ref.shape[0]
    rows = nheads * width
    tri = triangle(span).astype(F32).astype(BF16)
    cum_rows = sum(contract(part, tri, 1, 1) for part in thirds(decay_ref[...]))
    up = upper_half(hop)
    low = 1.0 - up
    from_before = up * jnp.exp(logs_ref[8:16, :])
    from_after = low * jnp.exp(logs_ref[16:24, :])
    for h in range(nheads):
        cols = slice(h * width, (h + 1) * width)
        two = slice(rows + h * width, rows + (h + 1) * width)
        got = got_ref[cols, :].astype(F32)
        state_in = (enter_ref[cols, :] + from_before[h : h + 1, :] * got).astype(BF16)
        grad_in = (enter_ref[two, :] + from_after[h : h + 1, :] * got).astype(BF16)
        cum_h = cum_rows[h : h + 1, :]
        last = cum_h[:, span - 1 : span]
        dq = local_ref[cols, :] + contract(state_in, g_ref[:, cols], 1, 1) * jnp.exp(cum_h)
        dk = local_ref[two, :] + contract(grad_in, v_ref[:, cols], 1, 1) * jnp.exp(last - cum_h)
        out_ref[cols, :] = dq.astype(BF16)
        out_ref[two, :] = dk.astype(BF16)


def share_order(count):
    bits = []
    hop = 2
    while hop < count:
        bits.append(hop)
        hop *= 2
    return bits, bits[::-1]


def share_hop(held, number):
    count = lax.axis_size("seq")
    even, odd = share_order(count)
    even, odd = even + [1], odd + [1]
    pairs = [(i, i ^ (odd[number] if i % 2 else even[number])) for i in range(count)]
    return lax.ppermute(held, "seq", pairs)


def share_deltas(count):
    even, odd = share_order(count)

    def spread(order):
        out = [0]
        for hop in order:
            out = out + [d ^ hop for d in out]
        return out

    return tuple(
        spread(first) + [d ^ 1 for d in spread(second)] for first, second in ((even, odd), (odd, even))
    )


def pack_kernel(share, plan, wq_ref, wk_ref, *refs):
    count, nseq = lax.axis_size("head"), lax.axis_size("seq")
    mine, my_seq = lax.axis_index("head"), lax.axis_index("seq")
    odd = lax.rem(my_seq, 2)
    outs, sems = refs[: len(plan)], refs[len(plan)]
    copies = []
    for i, (even_shift, odd_shift, many) in enumerate(plan):
        shift = even_shift + odd * (odd_shift - even_shift)
        block = lax.rem(mine + shift, count) * nseq + my_seq // many * many
        rows = pl.ds(pl.multiple_of(block * share, 16), many * share)
        for j, src in enumerate((wq_ref, wk_ref)):
            copies.append(
                pltpu.make_async_copy(
                    src.at[rows, :], outs[i].at[pl.ds(j * many * share, many * share), :], sems.at[i, j]
                )
            )
    for copy in copies:
        copy.start()
    for copy in copies:
        copy.wait()


def pack_weights(w_query, w_key, plan, share, pad=0):
    wide = w_query.shape[1]
    if share % 16:
        count, nseq = lax.axis_size("head"), lax.axis_size("seq")
        mine, my_seq = lax.axis_index("head"), lax.axis_index("seq")
        out = []
        for even_shift, odd_shift, many in plan:
            shift = jnp.where(my_seq % 2 == 1, odd_shift, even_shift)
            start = ((mine + shift) % count * nseq + my_seq // many * many) * share
            out.append(
                jnp.concatenate(
                    [lax.dynamic_slice_in_dim(w, start, many * share, 0) for w in (w_query, w_key)]
                )
            )
        return out
    heights = [2 * many * share for _, _, many in plan]
    heights[-1] += pad
    return call(
        functools.partial(pack_kernel, share, tuple(plan)),
        [jax.ShapeDtypeStruct((height, wide), BF16) for height in heights],
        0, sum(heights) * wide * 4,
        *(pltpu.with_memory_space_constraint(w, pltpu.HBM) for w in (w_query, w_key)),
        in_specs=[pl.BlockSpec(memory_space=pl.ANY)] * 2,
        out_specs=[pl.BlockSpec(memory_space=pltpu.VMEM)] * len(plan),
        scratch_shapes=[pltpu.SemaphoreType.DMA((len(plan), 2))],
    )


def join_kernel(groups, nargs, *refs):
    for group, out_ref in zip(groups, refs[-len(groups) :]):
        at = 0
        for i, start, size in group:
            out_ref[at : at + size, :] = refs[i][start : start + size, :]
            at += size


def join(*groups, tokens=()):
    args, spec = [], []
    for group in groups:
        spec.append(tuple((place_in(args, x), start, size) for x, start, size in group))
    return call(
        functools.partial(join_kernel, tuple(spec), len(args)),
        [jax.ShapeDtypeStruct((sum(size for _, _, size in group), args[0].shape[1]), BF16) for group in spec],
        0, 0, *args, *tokens,
        in_specs=[pl.BlockSpec(memory_space=pltpu.VMEM)] * len(args)
        + [pl.BlockSpec(memory_space=pl.ANY)] * len(tokens),
        out_specs=[pl.BlockSpec(memory_space=pltpu.VMEM)] * len(groups),
    )


def place_in(args, x):
    for i, y in enumerate(args):
        if y is x:
            return i
    args.append(x)
    return len(args) - 1


def rows_of(refs, low, high):
    parts, at = [], 0
    for ref in refs:
        first, last = max(low, at), min(high, at + ref.shape[0])
        if first < last:
            parts.append(ref[first - at : last - at, :])
        at += ref.shape[0]
    return parts[0] if len(parts) == 1 else jnp.concatenate(parts)


def row_block(weights, grads):
    share = weights.shape[0] // 2
    return contract(jnp.concatenate([weights[:share], weights[share:]], axis=1), grads, 1, 0)


def own_kernel(wq_ref, wk_ref, grads_ref, out_ref, near_q, near_k, sems):
    chunk, wide = near_q.shape
    rows = pl.ds(pl.multiple_of(lax.axis_index("head") * chunk, 16), chunk)
    copies = [
        pltpu.make_async_copy(src.at[rows, :], dst, sems.at[i])
        for i, (src, dst) in enumerate(((wq_ref, near_q), (wk_ref, near_k)))
    ]
    for copy in copies:
        copy.start()
    for copy in copies:
        copy.wait()
    out_ref[...] = contract(near_q[...], grads_ref[:wide, :], 1, 0) + contract(
        near_k[...], grads_ref[wide:, :], 1, 0
    )


def own_product(w_query, w_key, grads, chunk):
    wide = w_query.shape[1]
    return call(
        own_kernel, jax.ShapeDtypeStruct((chunk, grads.shape[1]), F32),
        4 * chunk * grads.shape[1] * wide, chunk * wide * 4,
        *(pltpu.with_memory_space_constraint(w, pltpu.HBM) for w in (w_query, w_key)), grads,
        in_specs=[pl.BlockSpec(memory_space=pl.ANY)] * 2 + [pl.BlockSpec(memory_space=pltpu.VMEM)],
        out_specs=pl.BlockSpec(memory_space=pltpu.VMEM),
        scratch_shapes=[pltpu.VMEM((chunk, wide), BF16)] * 2 + [pltpu.SemaphoreType.DMA((2,))],
    )


def relay_kernel(own_ref, handed_ref, kept_ref, relay_ref):
    mine, odd = lax.axis_index("head"), lax.rem(lax.axis_index("seq"), 2)
    inner = (mine == 1) | (mine == 2)

    @pl.when(inner & (mine + odd == 2))
    def _():
        relay_ref[...] = kept_ref[...]

    @pl.when(inner & (mine + odd != 2))
    def _():
        relay_ref[...] = handed_ref[...]

    @pl.when(jnp.logical_not(inner))
    def _():
        relay_ref[...] = own_ref[...]


def split_kernel(both_ref, token_ref, theirs_ref):
    odd = lax.rem(lax.axis_index("seq"), 2)
    share = theirs_ref.shape[0] // 2
    for parity in range(2):

        @pl.when(odd == parity)
        def _():
            for j in range(2):
                at = (2 * j + 1 - parity) * share
                theirs_ref[j * share : (j + 1) * share, :] = both_ref[at : at + share, :]


def pick_kernel(both_ref, got_ref, out_ref):
    odd = lax.rem(lax.axis_index("seq"), 2)
    upper = lax.axis_index("head") // 2
    share = out_ref.shape[0] // 2

    @pl.when(odd != upper)
    def _():
        out_ref[...] = got_ref[...]

    for parity in range(2):

        @pl.when((odd == parity) & (upper == parity))
        def _():
            for j in range(2):
                at = (2 * j + parity) * share
                out_ref[j * share : (j + 1) * share, :] = both_ref[at : at + share, :]


def pair_kernel(count, table_ref, total_ref, *refs):
    weights, (kept_ref, got_ref), (out_ref, head_ref, tail_ref) = refs[:count], refs[count : count + 2], refs[count + 2 :]
    nblocks = table_ref.shape[0]
    size = out_ref.shape[0] // nblocks
    split = head_ref.shape[0] // size
    span = out_ref.shape[1]
    grads = jnp.concatenate([kept_ref[...], got_ref[...]], axis=1)
    for j in range(nblocks):
        both = row_block(rows_of(weights, 2 * size * j, 2 * size * (j + 1)), grads)
        place = table_ref[j]
        rows = pl.ds(pl.multiple_of(place * size, 16), size)
        out_ref[rows, :] = total_ref[rows, :] + both[:, :span]
        sent = both[:, span:].astype(BF16)

        @pl.when(place < split)
        def _(sent=sent, place=place):
            head_ref[pl.ds(pl.multiple_of(place * size, 16), size), :] = sent

        @pl.when(place >= split)
        def _(sent=sent, place=place):
            tail_ref[pl.ds(pl.multiple_of((place - split) * size, 16), size), :] = sent


def pair_product(table, total, weights, kept, got, split):
    chunk, span = total.shape
    return call(
        functools.partial(pair_kernel, len(weights)),
        (
            jax.ShapeDtypeStruct((chunk, span), F32),
            jax.ShapeDtypeStruct((split, span), BF16),
            jax.ShapeDtypeStruct((chunk - split, span), BF16),
        ),
        0, 0,
        table, total, *weights, kept, got,
        in_specs=[pl.BlockSpec(memory_space=pltpu.SMEM)]
        + [pl.BlockSpec(memory_space=pltpu.VMEM)] * (3 + len(weights)),
        out_specs=[pl.BlockSpec(memory_space=pltpu.VMEM)] * 3,
        vmem=14 * 1024 * 1024,
    )


def add_kernel(blocks, base, low, high, plus, table_ref, total_ref, grads_ref, *refs):
    args, out_ref = refs[:-1], refs[-1]
    nshares = table_ref.shape[0]
    share = out_ref.shape[0] // nshares
    for j in range(nshares):
        rows = pl.ds(pl.multiple_of(table_ref[j] * share, 8), share)
        total = total_ref[rows, :]
        if plus:
            head, tail = (args[i] for i in plus)
            split, place = head.shape[0] // share, table_ref[j]
            from_head = head[pl.ds(pl.multiple_of(jnp.minimum(place, split - 1) * share, 16), share), :]
            from_tail = tail[pl.ds(pl.multiple_of(jnp.maximum(place - split, 0) * share, 16), share), :]
            total = total + jnp.where(place < split, from_head, from_tail).astype(F32)
        if low <= j < high:
            weights = rows_of([args[i] for i in blocks], 2 * share * (j - base), 2 * share * (j + 1 - base))
            total = total + row_block(weights, grads_ref[...])
        out_ref[rows, :] = total.astype(out_ref.dtype)


def add_product(table, total, blocks, grads, last, plus=(), base=0, low=0, high=None):
    chunk, span = total.shape
    args = []
    blocks = tuple(place_in(args, x) for x in blocks)
    plus = tuple(place_in(args, x) for x in plus)
    high = table.shape[0] if high is None else high
    return call(
        functools.partial(add_kernel, blocks, base, low, high, plus),
        jax.ShapeDtypeStruct((chunk, span), BF16 if last else F32),
        2 * chunk * span * grads.shape[0], chunk * span * 8,
        table, total, grads, *args,
        in_specs=[pl.BlockSpec(memory_space=pltpu.SMEM)]
        + [pl.BlockSpec(memory_space=pltpu.VMEM)] * (2 + len(args)),
        out_specs=pl.BlockSpec(memory_space=pltpu.VMEM),
        vmem=14 * 1024 * 1024,
    )


def shards(query_act, key_act, value_act, grad_output, log_decay, w_query, w_key):
    span = query_act.shape[0]
    nheads = log_decay.shape[1]
    width = query_act.shape[1] // nheads
    nseq, nhead = lax.axis_size("seq"), lax.axis_size("head")
    my_seq, my_head = lax.axis_index("seq"), lax.axis_index("head")
    chunk = w_query.shape[0] // nhead
    share = chunk // nseq
    rows = nheads * width

    shifts = [1, nhead - 1] + list(range(2, nhead - 1))
    ring = {k: [(i, (i + k) % nhead) for i in range(nhead)] for k in shifts}
    fast = nhead == 4 and nseq == 8
    if fast:
        packed = pack_weights(w_query, w_key, [(1, 3, 2), (2, 2, 2)], share)

        def moves(even, odd):
            return [
                (i * nhead + j, i * nhead + k) for i in range(nseq) for j, k in (odd if i % 2 else even)
            ]

        axes = ("seq", "head")
        first = lax.ppermute(packed[0], axes, moves(ring[1], ring[3]))
        passing = lax.ppermute(packed[1], axes, moves([(3, 2), (2, 1)], [(0, 1), (1, 2)]))
    else:
        packed = pack_weights(w_query, w_key, [(k, k, 1) for k in shifts], share)
        pieces = [lax.ppermute(p, "head", ring[k]) for p, k in zip(packed, shifts)]

    decay = log_decay.T
    sent, held, logs = call(
        functools.partial(states_kernel, nheads, width),
        (
            jax.ShapeDtypeStruct((2 * rows + 16, width), BF16),
            jax.ShapeDtypeStruct((2 * rows, width), F32),
            jax.ShapeDtypeStruct((24, width), F32),
        ),
        4 * span * rows * width, 8 * span * rows,
        decay, query_act, key_act, value_act, grad_output, packed[0],
        in_specs=[pl.BlockSpec(memory_space=pltpu.VMEM)] * 5 + [pl.BlockSpec(memory_space=pl.ANY)],
    )
    local = call(
        functools.partial(local_kernel, nheads, width),
        jax.ShapeDtypeStruct((2 * rows, span), F32),
        6 * span * span * rows, 16 * span * rows,
        decay, query_act, key_act, value_act, grad_output,
    )
    hop, enter = 1, None
    while True:
        got = lax.ppermute(sent, "seq", [(i, i ^ hop) for i in range(nseq)])
        if 2 * hop >= nseq:
            break
        final_next = 4 * hop >= nseq
        out_shape = (
            jax.ShapeDtypeStruct((rows if final_next else 2 * rows + 16, width), BF16),
            jax.ShapeDtypeStruct((2 * rows, width), F32),
            jax.ShapeDtypeStruct((24, width), F32),
            jax.ShapeDtypeStruct((2 * rows, width), F32),
        )
        args = [got, held, logs] + ([] if enter is None else [enter])
        sent, held, logs, enter = call(
            functools.partial(step_kernel, nheads, width, hop, enter is None, final_next),
            out_shape, 10 * rows * width, 16 * rows * width, *args,
        )
        hop *= 2
    both = call(
        functools.partial(carry_kernel, nheads, width, hop),
        jax.ShapeDtypeStruct((2 * rows, span), BF16),
        4 * span * rows * width, 16 * span * rows,
        decay, value_act, grad_output, got, logs, enter, local,
    )

    even, odd = share_deltas(nseq)
    deltas = jnp.where(my_seq % 2 == 1, jnp.array(odd, jnp.int32), jnp.array(even, jnp.int32))
    table = deltas ^ my_seq
    total = own_product(w_query, w_key, both, chunk)

    if fast:
        one, two = 2 * share, 4 * share
        (first,) = gate([first], [both])
        second = share_hop(first, 0)
        (near,) = join(((first, 0, two), (second, 0, two)))
        blocks = [near, share_hop(near, 1)]
        (ready,) = gate([both], [total])
        handed = lax.ppermute(ready, axes, moves(ring[3], ring[1]))
        kept = lax.ppermute(ready, axes, moves(ring[1], ring[3]))
        (passing,) = gate([passing], [first])
        passing = lax.ppermute(passing, axes, moves([(2, 1), (1, 0)], [(1, 2), (2, 3)]))
        theirs = call(
            split_kernel, jax.ShapeDtypeStruct((one, passing.shape[1]), BF16), 0, 0, passing, total,
            in_specs=[pl.BlockSpec(memory_space=pltpu.VMEM), pl.BlockSpec(memory_space=pl.ANY)],
            out_specs=pl.BlockSpec(memory_space=pltpu.VMEM),
        )
        theirs = lax.ppermute(
            theirs, axes,
            [(i * nhead + j, (i ^ 1) * nhead + j) for i in range(nseq) for j in range(nhead) if (j >= 2) == (i % 2)],
        )
        third = call(
            pick_kernel, jax.ShapeDtypeStruct(theirs.shape, BF16), 0, 0, passing, theirs,
            in_specs=[pl.BlockSpec(memory_space=pltpu.VMEM)] * 2,
            out_specs=pl.BlockSpec(memory_space=pltpu.VMEM),
        )
        fourth, fifth = share_hop(third, 0), share_hop(third, 1)
        fourth, fifth = gate([fourth, fifth])
        sixth = share_hop(fourth, 1)
        (early,) = join(((third, 0, one), (fourth, 0, one), (fifth, 0, CUT)))
        handed, kept = gate([handed, kept], [total])
        relay = call(
            relay_kernel, jax.ShapeDtypeStruct(both.shape, BF16), 0, 0, ready, handed, kept,
            in_specs=[pl.BlockSpec(memory_space=pltpu.VMEM)] * 3,
            out_specs=pl.BlockSpec(memory_space=pltpu.VMEM),
        )
        p2 = lax.ppermute(relay, "head", [(0, 2), (1, 0), (2, 3), (3, 1)])
        got = share_hop(handed, 2)
        total, *handed = pair_product(table[: nseq // 2] // 2, total, blocks, kept, got, SPLIT)
        got = [share_hop(x, 2) for x in handed]
        (late,) = join(((fifth, CUT, one - CUT), (sixth, 0, one)), tokens=[p2])
        early, late = share_hop(early, 2), share_hop(late, 2)
        total = add_product(table, total, (third, fourth, fifth, sixth, early), p2, False, high=6)
        return add_product(table, total, (early, late), p2, True, plus=got, base=4, low=6)

    gathered = lax.all_gather(both, "head")
    for i, k in enumerate(shifts):
        held = [pieces[i]]
        for number in range(len(share_order(nseq)[0]) + 1):
            whole = held[0] if number == 0 else jnp.concatenate(held)
            held = [whole, share_hop(whole, number)]
        grads = gathered[(my_head + nhead - k) % nhead]
        total = add_product(table, total, held, grads, i == nhead - 2)
    return total


def solution(mesh):
    placed = (
        P("seq", "head"),
        P("seq", "head"),
        P("seq", "head"),
        P("seq", "head"),
        P("seq", "head"),
        P(None, "head"),
        P(None, "head"),
    )
    return jax.shard_map(
        shards, mesh=mesh, in_specs=placed, out_specs=P("head", "seq"), check_vma=False
    )
```

```python
import functools

import jax
import jax.numpy as jnp
from jax import lax
from jax.experimental import pallas as pl
from jax.experimental.pallas import tpu as pltpu
from jax.sharding import PartitionSpec as P

F32 = jnp.float32
BF16 = jnp.bfloat16
VMEM_BYTES = 10 * 1024 * 1024
CUT = 160
SPLIT = 1152


def contract(a, b, left, right):
    return lax.dot_general(a, b, (((left,), (right,)), ((), ())), preferred_element_type=F32)


def call(kernel, out_shape, flops, nbytes, *args, aliases=None, vmem=VMEM_BYTES, **spec):
    return pl.pallas_call(
        kernel,
        out_shape=out_shape,
        cost_estimate=pl.CostEstimate(flops=flops, bytes_accessed=nbytes, transcendentals=0),
        compiler_params=pltpu.CompilerParams(vmem_limit_bytes=vmem),
        input_output_aliases=aliases or {},
        **spec,
    )(*args)


def gate_kernel(count, *refs):
    del count, refs


def gate(passed, tokens=(), flops=0):
    return call(
        functools.partial(gate_kernel, len(passed)),
        [jax.ShapeDtypeStruct(x.shape, x.dtype) for x in passed],
        flops, 0, *passed, *tokens,
        aliases={i: i for i in range(len(passed))},
        in_specs=[pl.BlockSpec(memory_space=pl.ANY)] * (len(passed) + len(tokens)),
        out_specs=[pl.BlockSpec(memory_space=pl.ANY)] * len(passed),
    )


def thirds(x):
    high = x.astype(BF16)
    rest = x - high.astype(F32)
    middle = rest.astype(BF16)
    return high, middle, (rest - middle.astype(F32)).astype(BF16)


def triangle(span):
    rows = lax.broadcasted_iota(jnp.int32, (span, span), 0)
    cols = lax.broadcasted_iota(jnp.int32, (span, span), 1)
    return rows >= cols


def upper_half(hop):
    return ((lax.axis_index("seq") // hop) % 2).astype(F32)


def states_kernel(nheads, width, decay_ref, q_ref, k_ref, v_ref, g_ref, token_ref, sent_ref, held_ref, logs_ref):
    span = q_ref.shape[0]
    tri = triangle(span).astype(F32).astype(BF16)
    cum = sum(contract(tri, part, 1, 1) for part in thirds(decay_ref[...]))
    rows = nheads * width
    row = lax.broadcasted_iota(jnp.int32, (8, width), 0)
    totals = jnp.zeros((8, width), F32)
    for h in range(nheads):
        cols = slice(h * width, (h + 1) * width)
        cum_h = cum[:, h : h + 1]
        last = cum[span - 1 : span, h : h + 1]
        key_w = (k_ref[:, cols].astype(F32) * jnp.exp(last - cum_h)).astype(BF16)
        query_w = (q_ref[:, cols].astype(F32) * jnp.exp(cum_h)).astype(BF16)
        state = contract(key_w, v_ref[:, cols], 0, 0)
        grad = contract(query_w, g_ref[:, cols], 0, 0)
        held_ref[h * width : (h + 1) * width, :] = state
        held_ref[rows + h * width : rows + (h + 1) * width, :] = grad
        sent_ref[h * width : (h + 1) * width, :] = state.astype(BF16)
        sent_ref[rows + h * width : rows + (h + 1) * width, :] = grad.astype(BF16)
        totals = jnp.where(row == h, jnp.broadcast_to(last, (8, width)), totals)
    high = totals.astype(BF16).astype(F32)
    sent_ref[2 * rows :, :] = jnp.concatenate([high, totals - high]).astype(BF16)
    logs_ref[0:8, :] = totals
    logs_ref[8:24, :] = jnp.zeros((16, width), F32)


def step_kernel(nheads, width, hop, first, final_next, got_ref, held_ref, logs_ref, *refs):
    if first:
        sent_ref, held_out, logs_out, enter_out = refs
    else:
        enter_ref, sent_ref, held_out, logs_out, enter_out = refs
    rows = nheads * width
    up = upper_half(hop)
    low = 1.0 - up
    tail = got_ref[2 * rows :, :].astype(F32)
    got_total = tail[0:8] + tail[8:16]
    total, before, after = logs_ref[0:8, :], logs_ref[8:16, :], logs_ref[16:24, :]
    own_decay, got_decay = jnp.exp(total), jnp.exp(got_total)
    from_before, from_after = up * jnp.exp(before), low * jnp.exp(after)
    total = total + got_total
    logs_out[0:8, :] = total
    logs_out[8:16, :] = before + up * got_total
    logs_out[16:24, :] = after + low * got_total
    if final_next:
        next_up = upper_half(2 * hop) > 0.5
    else:
        high = total.astype(BF16).astype(F32)
        sent_ref[2 * rows :, :] = jnp.concatenate([high, total - high]).astype(BF16)
    for h in range(nheads):
        one = slice(h * width, (h + 1) * width)
        two = slice(rows + h * width, rows + (h + 1) * width)
        got_state, got_grad = got_ref[one, :].astype(F32), got_ref[two, :].astype(F32)
        own, got = own_decay[h : h + 1, :], got_decay[h : h + 1, :]
        state = (up + low * got) * held_ref[one, :] + (up * own + low) * got_state
        grad = (low + up * got) * held_ref[two, :] + (low * own + up) * got_grad
        state_in = from_before[h : h + 1, :] * got_state
        grad_in = from_after[h : h + 1, :] * got_grad
        if not first:
            state_in = enter_ref[one, :] + state_in
            grad_in = enter_ref[two, :] + grad_in
        enter_out[one, :] = state_in
        enter_out[two, :] = grad_in
        held_out[one, :] = state
        held_out[two, :] = grad
        if final_next:
            sent_ref[one, :] = jnp.where(next_up, grad, state).astype(BF16)
        else:
            sent_ref[one, :] = state.astype(BF16)
            sent_ref[two, :] = grad.astype(BF16)


def local_kernel(nheads, width, decay_ref, q_ref, k_ref, v_ref, g_ref, out_ref):
    span = q_ref.shape[0]
    rows = nheads * width
    causal = triangle(span)
    tri = causal.astype(F32).astype(BF16)
    parts = thirds(decay_ref[...])
    cum = sum(contract(tri, part, 1, 1) for part in parts)
    cum_rows = sum(contract(part, tri, 1, 1) for part in parts)
    for h in range(nheads):
        cols = slice(h * width, (h + 1) * width)
        gap = cum[:, h : h + 1] - cum_rows[h : h + 1, :]
        decay = jnp.where(causal, jnp.exp(jnp.minimum(gap, 0.0)), 0.0)
        weighted = (contract(g_ref[:, cols], v_ref[:, cols], 1, 1) * decay).astype(BF16)
        out_ref[h * width : (h + 1) * width, :] = contract(k_ref[:, cols], weighted, 0, 1)
        out_ref[rows + h * width : rows + (h + 1) * width, :] = contract(
            q_ref[:, cols], weighted, 0, 0
        )


def carry_kernel(nheads, width, hop, decay_ref, v_ref, g_ref, got_ref, logs_ref, enter_ref, local_ref, out_ref):
    span = v_ref.shape[0]
    rows = nheads * width
    tri = triangle(span).astype(F32).astype(BF16)
    cum_rows = sum(contract(part, tri, 1, 1) for part in thirds(decay_ref[...]))
    up = upper_half(hop)
    low = 1.0 - up
    from_before = up * jnp.exp(logs_ref[8:16, :])
    from_after = low * jnp.exp(logs_ref[16:24, :])
    for h in range(nheads):
        cols = slice(h * width, (h + 1) * width)
        two = slice(rows + h * width, rows + (h + 1) * width)
        got = got_ref[cols, :].astype(F32)
        state_in = (enter_ref[cols, :] + from_before[h : h + 1, :] * got).astype(BF16)
        grad_in = (enter_ref[two, :] + from_after[h : h + 1, :] * got).astype(BF16)
        cum_h = cum_rows[h : h + 1, :]
        last = cum_h[:, span - 1 : span]
        dq = local_ref[cols, :] + contract(state_in, g_ref[:, cols], 1, 1) * jnp.exp(cum_h)
        dk = local_ref[two, :] + contract(grad_in, v_ref[:, cols], 1, 1) * jnp.exp(last - cum_h)
        out_ref[cols, :] = dq.astype(BF16)
        out_ref[two, :] = dk.astype(BF16)


def share_order(count):
    bits = []
    hop = 2
    while hop < count:
        bits.append(hop)
        hop *= 2
    return bits, bits[::-1]


def share_hop(held, number):
    count = lax.axis_size("seq")
    even, odd = share_order(count)
    even, odd = even + [1], odd + [1]
    pairs = [(i, i ^ (odd[number] if i % 2 else even[number])) for i in range(count)]
    return lax.ppermute(held, "seq", pairs)


def share_deltas(count):
    even, odd = share_order(count)

    def spread(order):
        out = [0]
        for hop in order:
            out = out + [d ^ hop for d in out]
        return out

    return tuple(
        spread(first) + [d ^ 1 for d in spread(second)] for first, second in ((even, odd), (odd, even))
    )


def pack_kernel(share, plan, wq_ref, wk_ref, *refs):
    count, nseq = lax.axis_size("head"), lax.axis_size("seq")
    mine, my_seq = lax.axis_index("head"), lax.axis_index("seq")
    odd = lax.rem(my_seq, 2)
    outs, sems = refs[: len(plan)], refs[len(plan)]
    copies = []
    for i, (even_shift, odd_shift, many) in enumerate(plan):
        shift = even_shift + odd * (odd_shift - even_shift)
        block = lax.rem(mine + shift, count) * nseq + my_seq // many * many
        rows = pl.ds(pl.multiple_of(block * share, 16), many * share)
        for j, src in enumerate((wq_ref, wk_ref)):
            copies.append(
                pltpu.make_async_copy(
                    src.at[rows, :], outs[i].at[pl.ds(j * many * share, many * share), :], sems.at[i, j]
                )
            )
    for copy in copies:
        copy.start()
    for copy in copies:
        copy.wait()


def pack_weights(w_query, w_key, plan, share, pad=0):
    wide = w_query.shape[1]
    if share % 16:
        count, nseq = lax.axis_size("head"), lax.axis_size("seq")
        mine, my_seq = lax.axis_index("head"), lax.axis_index("seq")
        out = []
        for even_shift, odd_shift, many in plan:
            shift = jnp.where(my_seq % 2 == 1, odd_shift, even_shift)
            start = ((mine + shift) % count * nseq + my_seq // many * many) * share
            out.append(
                jnp.concatenate(
                    [lax.dynamic_slice_in_dim(w, start, many * share, 0) for w in (w_query, w_key)]
                )
            )
        return out
    heights = [2 * many * share for _, _, many in plan]
    heights[-1] += pad
    return call(
        functools.partial(pack_kernel, share, tuple(plan)),
        [jax.ShapeDtypeStruct((height, wide), BF16) for height in heights],
        0, sum(heights) * wide * 4,
        *(pltpu.with_memory_space_constraint(w, pltpu.HBM) for w in (w_query, w_key)),
        in_specs=[pl.BlockSpec(memory_space=pl.ANY)] * 2,
        out_specs=[pl.BlockSpec(memory_space=pltpu.VMEM)] * len(plan),
        scratch_shapes=[pltpu.SemaphoreType.DMA((len(plan), 2))],
    )


def join_kernel(groups, nargs, *refs):
    for group, out_ref in zip(groups, refs[-len(groups) :]):
        at = 0
        for i, start, size in group:
            out_ref[at : at + size, :] = refs[i][start : start + size, :]
            at += size


def join(*groups, tokens=()):
    args, spec = [], []
    for group in groups:
        spec.append(tuple((place_in(args, x), start, size) for x, start, size in group))
    return call(
        functools.partial(join_kernel, tuple(spec), len(args)),
        [jax.ShapeDtypeStruct((sum(size for _, _, size in group), args[0].shape[1]), BF16) for group in spec],
        0, 0, *args, *tokens,
        in_specs=[pl.BlockSpec(memory_space=pltpu.VMEM)] * len(args)
        + [pl.BlockSpec(memory_space=pl.ANY)] * len(tokens),
        out_specs=[pl.BlockSpec(memory_space=pltpu.VMEM)] * len(groups),
    )


def place_in(args, x):
    for i, y in enumerate(args):
        if y is x:
            return i
    args.append(x)
    return len(args) - 1


def rows_of(refs, low, high):
    parts, at = [], 0
    for ref in refs:
        first, last = max(low, at), min(high, at + ref.shape[0])
        if first < last:
            parts.append(ref[first - at : last - at, :])
        at += ref.shape[0]
    return parts[0] if len(parts) == 1 else jnp.concatenate(parts)


def row_block(weights, grads):
    share = weights.shape[0] // 2
    return contract(jnp.concatenate([weights[:share], weights[share:]], axis=1), grads, 1, 0)


def own_kernel(wq_ref, wk_ref, grads_ref, out_ref, near_q, near_k, sems):
    chunk, wide = near_q.shape
    rows = pl.ds(pl.multiple_of(lax.axis_index("head") * chunk, 16), chunk)
    copies = [
        pltpu.make_async_copy(src.at[rows, :], dst, sems.at[i])
        for i, (src, dst) in enumerate(((wq_ref, near_q), (wk_ref, near_k)))
    ]
    for copy in copies:
        copy.start()
    for copy in copies:
        copy.wait()
    out_ref[...] = contract(near_q[...], grads_ref[:wide, :], 1, 0) + contract(
        near_k[...], grads_ref[wide:, :], 1, 0
    )


def own_product(w_query, w_key, grads, chunk):
    wide = w_query.shape[1]
    return call(
        own_kernel, jax.ShapeDtypeStruct((chunk, grads.shape[1]), F32),
        4 * chunk * grads.shape[1] * wide, chunk * wide * 4,
        *(pltpu.with_memory_space_constraint(w, pltpu.HBM) for w in (w_query, w_key)), grads,
        in_specs=[pl.BlockSpec(memory_space=pl.ANY)] * 2 + [pl.BlockSpec(memory_space=pltpu.VMEM)],
        out_specs=pl.BlockSpec(memory_space=pltpu.VMEM),
        scratch_shapes=[pltpu.VMEM((chunk, wide), BF16)] * 2 + [pltpu.SemaphoreType.DMA((2,))],
    )


def relay_kernel(own_ref, handed_ref, kept_ref, relay_ref):
    mine, odd = lax.axis_index("head"), lax.rem(lax.axis_index("seq"), 2)
    inner = (mine == 1) | (mine == 2)

    @pl.when(inner & (mine + odd == 2))
    def _():
        relay_ref[...] = kept_ref[...]

    @pl.when(inner & (mine + odd != 2))
    def _():
        relay_ref[...] = handed_ref[...]

    @pl.when(jnp.logical_not(inner))
    def _():
        relay_ref[...] = own_ref[...]


def split_kernel(both_ref, token_ref, theirs_ref):
    odd = lax.rem(lax.axis_index("seq"), 2)
    share = theirs_ref.shape[0] // 2
    for parity in range(2):

        @pl.when(odd == parity)
        def _():
            for j in range(2):
                at = (2 * j + 1 - parity) * share
                theirs_ref[j * share : (j + 1) * share, :] = both_ref[at : at + share, :]


def pick_kernel(both_ref, got_ref, out_ref):
    odd = lax.rem(lax.axis_index("seq"), 2)
    upper = lax.axis_index("head") // 2
    share = out_ref.shape[0] // 2

    @pl.when(odd != upper)
    def _():
        out_ref[...] = got_ref[...]

    for parity in range(2):

        @pl.when((odd == parity) & (upper == parity))
        def _():
            for j in range(2):
                at = (2 * j + parity) * share
                out_ref[j * share : (j + 1) * share, :] = both_ref[at : at + share, :]


def pair_kernel(count, table_ref, total_ref, *refs):
    weights, (kept_ref, got_ref), (out_ref, head_ref, tail_ref) = refs[:count], refs[count : count + 2], refs[count + 2 :]
    nblocks = table_ref.shape[0]
    size = out_ref.shape[0] // nblocks
    split = head_ref.shape[0] // size
    span = out_ref.shape[1]
    grads = jnp.concatenate([kept_ref[...], got_ref[...]], axis=1)
    for j in range(nblocks):
        both = row_block(rows_of(weights, 2 * size * j, 2 * size * (j + 1)), grads)
        place = table_ref[j]
        rows = pl.ds(pl.multiple_of(place * size, 16), size)
        out_ref[rows, :] = total_ref[rows, :] + both[:, :span]
        sent = both[:, span:].astype(BF16)

        @pl.when(place < split)
        def _(sent=sent, place=place):
            head_ref[pl.ds(pl.multiple_of(place * size, 16), size), :] = sent

        @pl.when(place >= split)
        def _(sent=sent, place=place):
            tail_ref[pl.ds(pl.multiple_of((place - split) * size, 16), size), :] = sent


def pair_product(table, total, weights, kept, got, split):
    chunk, span = total.shape
    return call(
        functools.partial(pair_kernel, len(weights)),
        (
            jax.ShapeDtypeStruct((chunk, span), F32),
            jax.ShapeDtypeStruct((split, span), BF16),
            jax.ShapeDtypeStruct((chunk - split, span), BF16),
        ),
        0, 0,
        table, total, *weights, kept, got,
        in_specs=[pl.BlockSpec(memory_space=pltpu.SMEM)]
        + [pl.BlockSpec(memory_space=pltpu.VMEM)] * (3 + len(weights)),
        out_specs=[pl.BlockSpec(memory_space=pltpu.VMEM)] * 3,
        vmem=14 * 1024 * 1024,
    )


def add_kernel(blocks, base, low, high, plus, table_ref, total_ref, grads_ref, *refs):
    args, out_ref = refs[:-1], refs[-1]
    nshares = table_ref.shape[0]
    share = out_ref.shape[0] // nshares
    for j in range(nshares):
        rows = pl.ds(pl.multiple_of(table_ref[j] * share, 8), share)
        total = total_ref[rows, :]
        if plus:
            head, tail = (args[i] for i in plus)
            split, place = head.shape[0] // share, table_ref[j]
            from_head = head[pl.ds(pl.multiple_of(jnp.minimum(place, split - 1) * share, 16), share), :]
            from_tail = tail[pl.ds(pl.multiple_of(jnp.maximum(place - split, 0) * share, 16), share), :]
            total = total + jnp.where(place < split, from_head, from_tail).astype(F32)
        if low <= j < high:
            weights = rows_of([args[i] for i in blocks], 2 * share * (j - base), 2 * share * (j + 1 - base))
            total = total + row_block(weights, grads_ref[...])
        out_ref[rows, :] = total.astype(out_ref.dtype)


def add_product(table, total, blocks, grads, last, plus=(), base=0, low=0, high=None):
    chunk, span = total.shape
    args = []
    blocks = tuple(place_in(args, x) for x in blocks)
    plus = tuple(place_in(args, x) for x in plus)
    high = table.shape[0] if high is None else high
    return call(
        functools.partial(add_kernel, blocks, base, low, high, plus),
        jax.ShapeDtypeStruct((chunk, span), BF16 if last else F32),
        2 * chunk * span * grads.shape[0], chunk * span * 8,
        table, total, grads, *args,
        in_specs=[pl.BlockSpec(memory_space=pltpu.SMEM)]
        + [pl.BlockSpec(memory_space=pltpu.VMEM)] * (2 + len(args)),
        out_specs=pl.BlockSpec(memory_space=pltpu.VMEM),
        vmem=14 * 1024 * 1024,
    )


def shards(query_act, key_act, value_act, grad_output, log_decay, w_query, w_key):
    span = query_act.shape[0]
    nheads = log_decay.shape[1]
    width = query_act.shape[1] // nheads
    nseq, nhead = lax.axis_size("seq"), lax.axis_size("head")
    my_seq, my_head = lax.axis_index("seq"), lax.axis_index("head")
    chunk = w_query.shape[0] // nhead
    share = chunk // nseq
    rows = nheads * width

    shifts = [1, nhead - 1] + list(range(2, nhead - 1))
    ring = {k: [(i, (i + k) % nhead) for i in range(nhead)] for k in shifts}
    fast = nhead == 4 and nseq == 8
    if fast:
        packed = pack_weights(w_query, w_key, [(1, 3, 2), (2, 2, 2)], share)

        def moves(even, odd):
            return [
                (i * nhead + j, i * nhead + k) for i in range(nseq) for j, k in (odd if i % 2 else even)
            ]

        axes = ("seq", "head")
        first = lax.ppermute(packed[0], axes, moves(ring[1], ring[3]))
        passing = lax.ppermute(packed[1], axes, moves([(3, 2), (2, 1)], [(0, 1), (1, 2)]))
    else:
        packed = pack_weights(w_query, w_key, [(k, k, 1) for k in shifts], share)
        pieces = [lax.ppermute(p, "head", ring[k]) for p, k in zip(packed, shifts)]

    decay = log_decay.T
    sent, held, logs = call(
        functools.partial(states_kernel, nheads, width),
        (
            jax.ShapeDtypeStruct((2 * rows + 16, width), BF16),
            jax.ShapeDtypeStruct((2 * rows, width), F32),
            jax.ShapeDtypeStruct((24, width), F32),
        ),
        4 * span * rows * width, 8 * span * rows,
        decay, query_act, key_act, value_act, grad_output, packed[0],
        in_specs=[pl.BlockSpec(memory_space=pltpu.VMEM)] * 5 + [pl.BlockSpec(memory_space=pl.ANY)],
    )
    local = call(
        functools.partial(local_kernel, nheads, width),
        jax.ShapeDtypeStruct((2 * rows, span), F32),
        6 * span * span * rows, 16 * span * rows,
        decay, query_act, key_act, value_act, grad_output,
    )
    hop, enter = 1, None
    while True:
        got = lax.ppermute(sent, "seq", [(i, i ^ hop) for i in range(nseq)])
        if 2 * hop >= nseq:
            break
        final_next = 4 * hop >= nseq
        out_shape = (
            jax.ShapeDtypeStruct((rows if final_next else 2 * rows + 16, width), BF16),
            jax.ShapeDtypeStruct((2 * rows, width), F32),
            jax.ShapeDtypeStruct((24, width), F32),
            jax.ShapeDtypeStruct((2 * rows, width), F32),
        )
        args = [got, held, logs] + ([] if enter is None else [enter])
        sent, held, logs, enter = call(
            functools.partial(step_kernel, nheads, width, hop, enter is None, final_next),
            out_shape, 10 * rows * width, 16 * rows * width, *args,
        )
        hop *= 2
    both = call(
        functools.partial(carry_kernel, nheads, width, hop),
        jax.ShapeDtypeStruct((2 * rows, span), BF16),
        4 * span * rows * width, 16 * span * rows,
        decay, value_act, grad_output, got, logs, enter, local,
    )

    even, odd = share_deltas(nseq)
    deltas = jnp.where(my_seq % 2 == 1, jnp.array(odd, jnp.int32), jnp.array(even, jnp.int32))
    table = deltas ^ my_seq
    total = own_product(w_query, w_key, both, chunk)

    if fast:
        one, two = 2 * share, 4 * share
        (first,) = gate([first], [both])
        second = share_hop(first, 0)
        (near,) = join(((first, 0, two), (second, 0, two)))
        blocks = [near, share_hop(near, 1)]
        (ready,) = gate([both], [total])
        handed = lax.ppermute(ready, axes, moves(ring[3], ring[1]))
        kept = lax.ppermute(ready, axes, moves(ring[1], ring[3]))
        (passing,) = gate([passing], [first])
        passing = lax.ppermute(passing, axes, moves([(2, 1), (1, 0)], [(1, 2), (2, 3)]))
        theirs = call(
            split_kernel, jax.ShapeDtypeStruct((one, passing.shape[1]), BF16), 0, 0, passing, total,
            in_specs=[pl.BlockSpec(memory_space=pltpu.VMEM), pl.BlockSpec(memory_space=pl.ANY)],
            out_specs=pl.BlockSpec(memory_space=pltpu.VMEM),
        )
        theirs = lax.ppermute(
            theirs, axes,
            [(i * nhead + j, (i ^ 1) * nhead + j) for i in range(nseq) for j in range(nhead) if (j >= 2) == (i % 2)],
        )
        third = call(
            pick_kernel, jax.ShapeDtypeStruct(theirs.shape, BF16), 0, 0, passing, theirs,
            in_specs=[pl.BlockSpec(memory_space=pltpu.VMEM)] * 2,
            out_specs=pl.BlockSpec(memory_space=pltpu.VMEM),
        )
        fourth, fifth = share_hop(third, 0), share_hop(third, 1)
        fourth, fifth = gate([fourth, fifth])
        sixth = share_hop(fourth, 1)
        (early,) = join(((third, 0, one), (fourth, 0, one), (fifth, 0, CUT)))
        handed, kept = gate([handed, kept], [total])
        relay = call(
            relay_kernel, jax.ShapeDtypeStruct(both.shape, BF16), 0, 0, ready, handed, kept,
            in_specs=[pl.BlockSpec(memory_space=pltpu.VMEM)] * 3,
            out_specs=pl.BlockSpec(memory_space=pltpu.VMEM),
        )
        p2 = lax.ppermute(relay, "head", [(0, 2), (1, 0), (2, 3), (3, 1)])
        got = share_hop(handed, 2)
        total, *handed = pair_product(table[: nseq // 2] // 2, total, blocks, kept, got, SPLIT)
        got = [share_hop(x, 2) for x in handed]
        (late,) = join(((fifth, CUT, one - CUT), (sixth, 0, one)), tokens=[p2])
        early, late = share_hop(early, 2), share_hop(late, 2)
        total = add_product(table, total, (third, fourth, fifth, sixth, early), p2, False, high=6)
        return add_product(table, total, (early, late), p2, True, plus=got, base=4, low=6)

    gathered = lax.all_gather(both, "head")
    for i, k in enumerate(shifts):
        held = [pieces[i]]
        for number in range(len(share_order(nseq)[0]) + 1):
            whole = held[0] if number == 0 else jnp.concatenate(held)
            held = [whole, share_hop(whole, number)]
        grads = gathered[(my_head + nhead - k) % nhead]
        total = add_product(table, total, held, grads, i == nhead - 2)
    return total


def solution(mesh):
    placed = (
        P("seq", "head"),
        P("seq", "head"),
        P("seq", "head"),
        P("seq", "head"),
        P("seq", "head"),
        P(None, "head"),
        P(None, "head"),
    )
    return jax.shard_map(
        shards, mesh=mesh, in_specs=placed, out_specs=P("head", "seq"), check_vma=False
    )
```
